128 devices in a mesh: row: 8 (over z, core), col: 16 (over x, y).
Axes of the slice: x: 4, y: 4, z: 4, core: 2. Of those that a mesh axis runs over, the one named last changes fastest.
Arguments:
- scans: float32 [16384, 4, 8, 128], P(('row', 'col')), may hold values from -6 to 6
- dest: int32 [16384, 1], P(('row', 'col')), may hold values from 0 to 127; in each aligned block of 128 rows (0 to 127, 128 to 255, ...) at most 2 rows name the same one
- offsets: int32 [16384], P(('row', 'col')), may hold values from 0 to 252
- profile_index: int32 [16384], P(('row', 'col')), may hold values from 0 to 15
- profiles: float32 [16, 4, 128], replicated, may hold values from 0.1 to 1.5
- embed_weight: bfloat16 [512, 1024], replicated, may hold values from -0.25 to 0.25
- attn_gain: float32 [2, 1024], replicated, may hold values from 0.1 to 1.9
- qkv_weight: bfloat16 [2, 1024, 3072], replicated, may hold values from -3 to 3
- out_weight: bfloat16 [2, 1024, 1024], replicated, may hold values from -0.1875 to 0.1875
Outputs:
- tokens: bfloat16 [256, 256, 1024], P('row', 'col')
The draws below stay inside these ranges and needn't reach their ends.
Inputs may be any that keep to these rules, and one draw needn't show every extreme that they name: dest[b, 0] is the tile of block b, numbered 16 * tile row + tile column; of the 128 blocks of one device at most 2 go to any one tile.
All inputs are finite; a program needn't handle non-finite values.
Results may differ from the reference program's by a relative error of at most 0.012.
Values may be sent and summed in bfloat16 or wider, within the bound.
No kernel may reach another device: no remote copies, remote signals or barrier semaphores. Data moves between devices by JAX's collectives and lax.ppermute only.
A program may use at most 128 MiB of HBM per device.

```python
import math
import jax
import jax.numpy as jnp
import numpy as np
from jax import lax

C = 8
D = 1024
HEADS = 16
RADIUS = 4
LAYERS = 2
BR = 4
NWT = 16
TOK_H = 32
TOK_W = 16
SCANS = 128
CAP = 2
NBLK = 16384
N_ROW = 8
N_COL = 16
DEVICES = 128


def draw_qkv_weight(key, part):
    drawn = jnp.clip(jax.random.normal(key, (LAYERS, D, 3 * D), jnp.float32), -4.0, 4.0) * D ** (-0.5)
    return drawn.astype(jnp.bfloat16)


def plant(entries, own_key, smallest, high):
    spot = [jax.random.randint(jax.random.fold_in(own_key, axis), (), 0, length) for axis, length in enumerate(entries.shape)]
    longest = entries.shape.index(max(entries.shape))
    neighbour = spot[:longest] + [(spot[longest] + 1) % entries.shape[longest]] + spot[longest + 1:]
    return entries.at[tuple(spot)].set(smallest).at[tuple(neighbour)].set(high)


def block_levels(stream_key, shape, cuts, smallest, top_value):
    loudness, own = 1.0, jax.random.fold_in(stream_key, 6)
    for dim, parts in cuts:
        steps = jnp.exp(jax.random.uniform(jax.random.fold_in(own, dim), (parts,), jnp.float32, smallest / len(cuts), top_value / len(cuts)))
        loudness = loudness * jnp.repeat(steps, shape[dim] // parts).reshape([-1 if axis == dim else 1 for axis in range(len(shape))])
    return loudness


def routed_block(own_key, own, number, rows, amount, top, bound, skew):
    ranking = jax.random.permutation(own_key, amount)
    heavy_load, common = portions_of(amount, rows * top, bound, skew, True), portions_of(amount, rows * top, bound, skew, False)
    places = jnp.arange(amount)

    def named(lengths, rotation):
        used = int((lengths > 0).sum())
        fixed = max(1, used // 4)
        moved = fixed + (places - fixed + rotation * (used - fixed)) % max(1, amount - fixed)
        return jnp.zeros((amount,), jnp.int32).at[ranking[jnp.where(places < fixed, places, moved)]].set(jnp.asarray(lengths, jnp.int32))

    lengths = jnp.where(number % 4 == 0, named(heavy_load, number // 4), named(common, number - number // 4 - 1))
    mixed = jax.random.permutation(jax.random.fold_in(own, 3), amount)
    giver, taker = mixed[0:amount // 2 * 2:2], mixed[1:amount // 2 * 2:2]
    slack = jnp.minimum(lengths[giver] - 1, bound - lengths[taker]) // 2
    slack = jnp.where((giver == ranking[0]) | (taker == ranking[0]) | (lengths[taker] == 0), 0, jnp.maximum(slack, 0))
    moved = jax.random.randint(jax.random.fold_in(own, 4), (amount // 2,), 0, 1 << 20) % (slack + 1)
    lengths = lengths.at[giver].add(-moved).at[taker].add(moved)
    items = jnp.searchsorted(jnp.cumsum(lengths), jnp.arange(rows * top), side="right").astype(jnp.int32)
    table = items.reshape(top, rows).T
    table = table[jax.random.permutation(jax.random.fold_in(own, 1), rows)]
    rotation = jax.random.randint(jax.random.fold_in(own, 2), (rows, 1), 0, top)
    return jnp.take_along_axis(table, (jnp.arange(top)[None, :] + rotation) % top, axis=1)


def portions_of(number_of, total, limit, slope, full):
    weights = [(1 << 20) // math.isqrt(grade ** slope) + 1 for grade in range(1, number_of + 1)]
    largest = limit if full else min(limit, max(-(-total // number_of), total * weights[0] // sum(weights)))
    least = 1 if total - largest >= number_of - 1 else 0
    holding, surplus = [largest] + [least] * (number_of - 1), total - largest - least * (number_of - 1)
    while surplus > 0:
        movable = [i for i in range(1, number_of) if holding[i] < largest] or [i for i in range(1, number_of) if holding[i] < limit]
        pool, budget = sum([weights[i] for i in movable]), surplus
        for i in movable:
            extra = min(limit - holding[i], max(1, budget * weights[i] // pool), surplus)
            holding[i] = holding[i] + extra
            surplus = surplus - extra
    return np.array(holding)


def noise(stream_key, shape, deviation, most, pieces=(), kind=jnp.bfloat16):
    array = jax.random.normal(stream_key, shape, jnp.float32) * deviation
    if len(pieces) > 0:
        array = block_levels(stream_key, shape, pieces, -0.22, 0.18) * array
    return jnp.clip(array, min=-most, max=most).astype(kind)


def setup_inputs(seed: int = 0) -> dict:
    arg_keys = jax.random.split(jax.random.key(seed), 10)
    scans = noise(arg_keys[0], (NBLK, BR, C, 8 * TOK_W), 1.0, 6.0, ((0, 128),), jnp.float32)
    dest_keys = jax.random.split(jax.random.fold_in(arg_keys[1], 1), NBLK // SCANS)
    dest_turns = jax.random.permutation(jax.random.fold_in(arg_keys[1], 3), NBLK // SCANS)
    dest = jax.vmap(lambda own, number: routed_block(jax.random.fold_in(arg_keys[1], 2), own, number, SCANS, DEVICES, 1, CAP, 2))(dest_keys, dest_turns).reshape((NBLK, 1))
    offsets = plant(jax.random.randint(arg_keys[2], (NBLK,), 0, 8 * TOK_H - BR + 1), jax.random.fold_in(arg_keys[2], 1), 0, 8 * TOK_H - BR).astype(jnp.int32)
    profile_index = plant(jax.random.randint(arg_keys[3], (NBLK,), 0, NWT), jax.random.fold_in(arg_keys[3], 1), 0, NWT - 1).astype(jnp.int32)
    profiles = jnp.clip(jnp.exp(jax.random.uniform(arg_keys[4], (NWT, BR, 8 * TOK_W), jnp.float32, math.log(0.1), math.log(1.5))), 0.1, 1.5)
    embed_weight = noise(arg_keys[5], (64 * C, D), (64 * C) ** -0.5, 0.25)
    attn_gain = jnp.clip(1.0 + 0.18 * jax.random.normal(arg_keys[6], (LAYERS, D), jnp.float32), 0.1, 1.9)
    qkv_weight = draw_qkv_weight(jax.random.fold_in(arg_keys[9], 71), 0)
    out_weight = noise(arg_keys[8], (LAYERS, D, D), D ** -0.5, 0.1875)
    return dict(scans=scans, dest=dest, offsets=offsets, profile_index=profile_index, profiles=profiles, embed_weight=embed_weight, attn_gain=attn_gain, qkv_weight=qkv_weight, out_weight=out_weight)


def normed(stream, gain_row):
    centre = lax.optimization_barrier(jnp.mean(stream, -1, keepdims=True))
    spread = lax.optimization_barrier(jnp.mean(jnp.square(stream - centre), -1, keepdims=True))
    return ((stream - centre) * lax.rsqrt(spread + 1e-05) * gain_row).astype(jnp.bfloat16)

def reference(scans, dest, offsets, profile_index, profiles, embed_weight, attn_gain, qkv_weight, out_weight):
    tile_rows = TOK_H * 8
    tile_cols = TOK_W * 8
    grid_h = TOK_H * N_ROW
    grid_w = TOK_W * N_COL
    pixel_cols = grid_w * 8
    pixel_total = grid_h * 8 * pixel_cols
    targets = dest[:, 0]
    block_weight = profiles[profile_index]
    weighted = scans * block_weight[:, :, None, :]
    top_row = (targets // N_COL * tile_rows + offsets).astype(jnp.int32)
    left_col = (targets % N_COL * tile_cols).astype(jnp.int32)
    pix_rows = top_row[:, None] + jnp.arange(BR, dtype=jnp.int32)[None, :]
    pix_cols = left_col[:, None] + jnp.arange(tile_cols, dtype=jnp.int32)[None, :]
    flat_idx = (pix_rows[:, :, None] * pixel_cols + pix_cols[:, None, :]).reshape(-1).astype(jnp.int32)
    weighted_rows = weighted.transpose(0, 1, 3, 2).reshape(-1, C)
    numerator = jax.ops.segment_sum(weighted_rows, flat_idx, num_segments=pixel_total)
    numerator = numerator.reshape(grid_h * 8, pixel_cols, C).transpose(0, 2, 1)
    weight_sum = jax.ops.segment_sum(block_weight.reshape(-1), flat_idx, num_segments=pixel_total)
    weight_sum = weight_sum.reshape(grid_h * 8, pixel_cols)
    merged = (numerator / (1.0 + weight_sum[:, None, :])).astype(jnp.bfloat16)
    patches = merged.reshape(grid_h, 8, C, grid_w, 8).transpose(0, 3, 2, 1, 4).reshape(grid_h * grid_w, C * 64)
    stream = jnp.dot(patches, embed_weight, preferred_element_type=jnp.float32)
    head_dim = D // HEADS
    score_scale = head_dim ** (-0.5)
    window = 2 * RADIUS + 1
    inside_grid = jnp.pad(jnp.ones((grid_h, grid_w), jnp.float32), RADIUS)
    padding = ((RADIUS, RADIUS), (RADIUS, RADIUS), (0, 0), (0, 0))
    for layer_idx in range(LAYERS):
        inputs = normed(stream, attn_gain[layer_idx])
        projected = jnp.dot(inputs, qkv_weight[layer_idx], preferred_element_type=jnp.float32).astype(jnp.bfloat16)
        queries = projected[:, :D].reshape(grid_h, grid_w, HEADS, head_dim)
        key_heads = jnp.pad(projected[:, D:2 * D].reshape(grid_h, grid_w, HEADS, head_dim), padding)
        values = jnp.pad(projected[:, 2 * D:].reshape(grid_h, grid_w, HEADS, head_dim), padding)

        def one_row(row_idx):
            query_row = lax.dynamic_index_in_dim(queries, row_idx, 0, keepdims=False).astype(jnp.float32)
            key_slab = lax.dynamic_slice_in_dim(key_heads, row_idx, window, 0)
            value_slab = lax.dynamic_slice_in_dim(values, row_idx, window, 0)
            mask_slab = lax.dynamic_slice_in_dim(inside_grid, row_idx, window, 0)
            logit_list = []
            for row_step in range(window):
                for col_step in range(window):
                    shifted = key_slab[row_step, col_step:col_step + grid_w].astype(jnp.float32)
                    logits = lax.optimization_barrier(jnp.sum(query_row * shifted, -1)) * score_scale
                    inside = mask_slab[row_step, col_step:col_step + grid_w][:, None] > 0.5
                    logit_list.append(jnp.where(inside, logits, -1e+30))
            logits = jnp.stack(logit_list)
            row_max = lax.optimization_barrier(jnp.max(logits, 0))
            exponent = jnp.exp(logits - row_max)
            attention = (exponent / lax.optimization_barrier(jnp.sum(exponent, 0))).astype(jnp.bfloat16)
            accumulated = jnp.zeros((grid_w, HEADS, head_dim), jnp.float32)
            for row_step in range(window):
                for col_step in range(window):
                    shifted = value_slab[row_step, col_step:col_step + grid_w].astype(jnp.float32)
                    share = attention[row_step * window + col_step][:, :, None].astype(jnp.float32)
                    accumulated = accumulated + share * shifted
            return accumulated.astype(jnp.bfloat16)
        attended = lax.map(one_row, jnp.arange(grid_h, dtype=jnp.int32)).reshape(grid_h * grid_w, D)
        stream = stream + jnp.dot(attended, out_weight[layer_idx], preferred_element_type=jnp.float32)
    return stream.astype(jnp.bfloat16).reshape(grid_h, grid_w, D)
```

```python
import functools

import jax
import jax.numpy as jnp
from jax import lax
from jax.experimental import pallas as pl
from jax.experimental.pallas import tpu as pltpu
from jax.sharding import PartitionSpec as P

HEADS = 16
RADIUS = 4
TOK_H = 32
TOK_W = 16
BR = 4
CH = 8
MODEL = 1024
PATCH = 512
GRP = 128
FULL = 160
HALO = 16
EDGE = 4 * HALO
META = 128
VMEM_BYTES = 50 * 1024 * 1024

f32 = jnp.float32
bf16 = jnp.bfloat16
i32 = jnp.int32


def dot(a, b):
    return lax.dot_general(a, b, (((1,), (0,)), ((), ())), preferred_element_type=f32)


def dot_nt(a, b):
    return lax.dot_general(a, b, (((1,), (1,)), ((), ())), preferred_element_type=f32)


def iota(shape, dim):
    return lax.broadcasted_iota(i32, shape, dim)


def onehot(cond):
    return jnp.where(cond, 1.0, 0.0).astype(bf16)


def halves(x):
    high = x.astype(bf16)
    return high, (x - high.astype(f32)).astype(bf16)


def pack_kernel(dest_ref, offs_ref, pidx_ref, prof_ref, scans_ref, out_ref, w_ref):
    count = dest_ref.shape[0]
    eye = iota((count, count), 0) == iota((count, count), 1)
    dest_col = dest_ref[...].astype(f32)
    dest_row = jnp.sum(jnp.where(eye, dest_col, 0.0), axis=0, keepdims=True)
    before = iota((count, count), 0) < iota((count, count), 1)
    same = (dest_col == dest_row) & before
    rank = jnp.sum(jnp.where(same, 1.0, 0.0), axis=0, keepdims=True)
    slot = dest_row * (2.0 * BR) + rank * float(BR)
    offs_col = jnp.sum(jnp.where(eye, offs_ref[...].astype(f32), 0.0), axis=1, keepdims=True)
    pidx_col = jnp.sum(jnp.where(eye, pidx_ref[...].astype(f32), 0.0), axis=1, keepdims=True)
    chosen = onehot(pidx_col == iota((count, prof_ref.shape[0]), 1).astype(f32))
    lane = iota((count, META), 1)
    meta = jnp.where(lane == 0, offs_col, jnp.where(lane == 1, pidx_col, 1.0)).astype(bf16)
    for k in range(BR):
        high, low = halves(prof_ref[:, k, :])
        weight = dot(chosen, high) + dot(chosen, low)
        for c in range(CH):
            block = scans_ref[pl.ds(k * CH + c, count, stride=BR * CH), :]
            w_ref[k * count : (k + 1) * count, c * 128 : (c + 1) * 128] = (block * weight).astype(
                bf16
            )
        w_ref[k * count : (k + 1) * count, CH * 128 :] = meta
    rows = out_ref.shape[0]
    slots = jnp.concatenate([slot + float(k) for k in range(BR)], axis=1)
    step = 256
    for r in range(0, rows, step):
        here = (iota((step, BR * count), 0) + r).astype(f32)
        placing = onehot(here == slots)
        out_ref[r : r + step, :] = dot(placing, w_ref[...]).astype(bf16)


def pack(dest, offsets, profile_index, profiles, scans):
    count = scans.shape[0]
    rows = count * 2 * BR
    return pl.pallas_call(
        pack_kernel,
        out_shape=jax.ShapeDtypeStruct((rows, CH * 128 + META), bf16),
        scratch_shapes=[pltpu.VMEM((BR * count, CH * 128 + META), bf16)],
        compiler_params=pltpu.CompilerParams(vmem_limit_bytes=VMEM_BYTES),
        name="pack",
    )(
        dest,
        offsets.reshape(1, count),
        profile_index.reshape(1, count),
        profiles,
        scans.reshape(count * BR * CH, 128),
    )


def merge_kernel(pay_ref, prof_ref, x_ref, top_ref, bot_ref, mg_ref, y_ref, xg_ref):
    rows = pay_ref.shape[0]
    pick = onehot(iota((8, META), 0) == iota((8, META), 1))
    fields = dot_nt(pick, pay_ref[:, CH * 128 :])
    offs = fields[0:1, :]
    pidx = fields[1:2, :]
    valid = fields[2:3, :]
    strip = (iota((1, rows), 1) % BR).astype(f32)
    land = jnp.where(valid > 0.5, offs + strip, 4096.0)
    kind = pidx + 16.0 * strip
    r = iota((TOK_H * 8, rows), 0)
    pixel = (r % TOK_H) * 8 + r // TOK_H
    placing = onehot(pixel.astype(f32) == land)
    kinds = onehot(iota((16 * BR, rows), 0).astype(f32) == kind)
    counts = dot_nt(placing, kinds).astype(bf16)
    table = jnp.concatenate([prof_ref[:, k, :] for k in range(BR)], axis=0)
    high, low = halves(table)
    scale = 1.0 / (1.0 + dot(counts, high) + dot(counts, low))
    for c in range(CH):
        part = dot(placing, pay_ref[:, c * 128 : (c + 1) * 128])
        mg_ref[:, c * 128 : (c + 1) * 128] = (part * scale).astype(bf16)
    width = CH * 128
    step = 256
    for n in range(0, width, step):
        source = iota((width, step), 0)
        to = iota((width, step), 1) + n
        wanted = (to // 8 % CH) * 128 + (to // 64) * 8 + to % 8
        y_ref[:, n : n + step] = dot(mg_ref[...], onehot(source == wanted))
    low_half = iota((TOK_H, 128), 1) < 64
    order = iota((GRP, GRP), 1)
    want = iota((GRP, GRP), 0)
    reorder = onehot(order == (want % 4) * TOK_H + want // 4)
    for g in range(4):
        for jj in range(4):
            j = 4 * g + jj
            tile = (j // 2) * 128
            for pp in range(4):
                a = y_ref[2 * pp * TOK_H : (2 * pp + 1) * TOK_H, tile : tile + 128]
                b = y_ref[(2 * pp + 1) * TOK_H : (2 * pp + 2) * TOK_H, tile : tile + 128]
                if j % 2 == 0:
                    piece = jnp.where(low_half, a, pltpu.roll(b, 64, 1))
                else:
                    piece = jnp.where(low_half, pltpu.roll(a, 64, 1), b)
                xg_ref[jj * TOK_H : (jj + 1) * TOK_H, pp * 128 : (pp + 1) * 128] = piece.astype(
                    bf16
                )
        tokens = dot(reorder, xg_ref[...]).astype(bf16)
        x_ref[g * GRP : (g + 1) * GRP, :] = tokens
        top_ref[g * HALO : (g + 1) * HALO, :] = tokens[:HALO, :]
        bot_ref[g * HALO : (g + 1) * HALO, :] = tokens[GRP - HALO :, :]


def merge(payload, profiles):
    return pl.pallas_call(
        merge_kernel,
        out_shape=[
            jax.ShapeDtypeStruct((4 * GRP, PATCH), bf16),
            jax.ShapeDtypeStruct((EDGE, PATCH), bf16),
            jax.ShapeDtypeStruct((EDGE, PATCH), bf16),
        ],
        scratch_shapes=[
            pltpu.VMEM((TOK_H * 8, CH * 128), bf16),
            pltpu.VMEM((TOK_H * 8, CH * 128), f32),
            pltpu.VMEM((GRP, PATCH), bf16),
        ],
        compiler_params=pltpu.CompilerParams(vmem_limit_bytes=VMEM_BYTES),
        name="merge",
    )(payload, profiles)


def normed(stream, gain):
    centre = jnp.mean(stream, -1, keepdims=True)
    moved = stream - centre
    spread = jnp.mean(jnp.square(moved), -1, keepdims=True)
    return (moved * lax.rsqrt(spread + 1e-05) * gain).astype(bf16)


def own_kernel(layer, *refs):
    if layer == 0:
        x_ref, embed_ref, gain_ref, w_ref, stream_ref, qkv_ref, w_vmem, sem, inp_ref = refs
    else:
        x_ref, w_ref, qkv_ref, w_vmem, sem = refs
        inp_ref = x_ref
    copies = [
        pltpu.make_async_copy(
            w_ref.at[layer, :, pl.ds(n * MODEL, MODEL)], w_vmem.at[n], sem.at[n]
        )
        for n in range(3)
    ]
    for copy in copies:
        copy.start()
    if layer == 0:
        for r in range(0, 4 * GRP, GRP):
            stream = dot(x_ref[r : r + GRP, :], embed_ref[...])
            stream_ref[r : r + GRP, :] = stream
            inp_ref[r : r + GRP, :] = normed(stream, gain_ref[0:1, :])
    step = 256
    for n in range(3):
        copies[n].wait()
        for m in range(0, MODEL, step):
            part = dot(inp_ref[...], w_vmem[n, :, m : m + step]).astype(bf16)
            if n == 0:
                part = part * jnp.asarray(0.125, bf16)
            qkv_ref[:, n * MODEL + m : n * MODEL + m + step] = part


def own_part(layer, x, embed, gain, qkv_weight):
    any_spec = pl.BlockSpec(memory_space=pl.ANY)
    vmem = pl.BlockSpec(memory_space=pltpu.VMEM)
    qkv = jax.ShapeDtypeStruct((4 * GRP, 3 * MODEL), bf16)
    scratch = [pltpu.VMEM((3, MODEL, MODEL), bf16), pltpu.SemaphoreType.DMA((3,))]
    params = pltpu.CompilerParams(vmem_limit_bytes=VMEM_BYTES)
    cost = pl.CostEstimate(
        flops=2 * 4 * GRP * MODEL * 3 * MODEL, bytes_accessed=12 << 20, transcendentals=0
    )
    if layer == 0:
        return pl.pallas_call(
            functools.partial(own_kernel, layer),
            out_shape=[jax.ShapeDtypeStruct((4 * GRP, MODEL), f32), qkv],
            in_specs=[vmem, vmem, vmem, any_spec],
            scratch_shapes=scratch + [pltpu.VMEM((4 * GRP, MODEL), bf16)],
            compiler_params=params,
            cost_estimate=cost,
            name="own0",
        )(x, embed, gain, qkv_weight)
    return pl.pallas_call(
        functools.partial(own_kernel, layer),
        out_shape=qkv,
        in_specs=[vmem, any_spec],
        scratch_shapes=scratch,
        compiler_params=params,
        cost_estimate=cost,
        name="own1",
    )(x, qkv_weight)


def attend_kernel(layer, *refs):
    if layer == 0:
        (place_ref, top_ref, bot_ref, left_ref, right_ref, stream_ref, qkv_ref, gain_ref, embed_ref,
         w_ref, o_ref, out_ref, x_ref, xt_ref, xb_ref,
         w_vmem, o_vmem, sem, halo_ref, kv_ref, att_ref) = refs
    else:
        (place_ref, top_ref, bot_ref, left_ref, right_ref, stream_ref, qkv_ref,
         w_ref, o_ref, out_ref,
         w_vmem, o_vmem, sem, halo_ref, kv_ref, att_ref) = refs
    copies = [
        pltpu.make_async_copy(
            w_ref.at[layer, :, pl.ds((n + 1) * MODEL, MODEL)], w_vmem.at[n], sem.at[n]
        )
        for n in range(2)
    ]
    copies.append(pltpu.make_async_copy(o_ref.at[layer], o_vmem, sem.at[2]))
    for copy in copies:
        copy.start()
    row = 0
    for ref in (top_ref, bot_ref, left_ref, right_ref):
        part = ref[...]
        if layer == 0:
            part = normed(dot(part, embed_ref[...]), gain_ref[0:1, :])
        halo_ref[row : row + ref.shape[0], :] = part
        row += ref.shape[0]
    for g in range(4):
        at = (g + 1) * FULL + HALO
        kv_ref[at : at + GRP, :] = qkv_ref[g * GRP : (g + 1) * GRP, MODEL:]
    step = 256
    for n in range(2):
        copies[n].wait()
        for m in range(0, MODEL, step):
            part = dot(halo_ref[...], w_vmem[n, :, m : m + step]).astype(bf16)
            lanes = slice(n * MODEL + m, n * MODEL + m + step)
            for g in range(4):
                at = (g + 1) * FULL
                kv_ref[at : at + HALO, lanes] = part[g * HALO : (g + 1) * HALO, :]
                kv_ref[at + HALO + GRP : at + FULL, lanes] = part[
                    EDGE + g * HALO : EDGE + (g + 1) * HALO, :
                ]
            kv_ref[0:FULL, lanes] = part[2 * EDGE : 2 * EDGE + FULL, :]
            kv_ref[5 * FULL : 6 * FULL, lanes] = part[2 * EDGE + FULL :, :]

    query = iota((64, 256), 0)
    key = iota((64, 256), 1)
    row_gap = (key % 64) // 4 - 4 - (query % 32) // 4
    col_gap = (key // 64 - 1) * 4 + key % 4 - (query // 32) * 4 - query % 4
    near = (jnp.abs(row_gap) <= RADIUS) & (jnp.abs(col_gap) <= RADIUS)
    near_bias = jnp.where(near, 0.0, -1e30)
    lane_key = iota((1, 256), 1)
    key_row = (lane_key % 64) // 4 - 4
    key_col = (lane_key // 64 - 1) * 4 + lane_key % 4
    low_half = iota((64, 128), 1) < 64
    zero = jnp.zeros((64, 128), bf16)
    ones = jnp.ones((256, 128), bf16)
    height, width = place_ref[2], place_ref[3]

    def block(b, carry):
        bi, bj = b // 2, b % 2
        at_row = key_row + bi * 8 + place_ref[0]
        at_col = key_col + bj * 8 + place_ref[1]
        inside = (at_row >= 0) & (at_row < height) & (at_col >= 0) & (at_col < width)
        bias = near_bias + jnp.where(inside, 0.0, -1e30)
        bias = jnp.concatenate([bias, bias], axis=0)
        q_rows = [pl.multiple_of((2 * bj + g) * GRP + bi * 32, 32) for g in range(2)]
        k_rows = [pl.multiple_of((2 * bj + g) * FULL + bi * 32, 32) for g in range(4)]
        for h in range(HEADS // 2):
            lanes = slice(h * 128, (h + 1) * 128)
            q = jnp.concatenate([qkv_ref[pl.ds(r, 32), lanes] for r in q_rows], axis=0)
            q = jnp.concatenate([jnp.where(low_half, q, zero), jnp.where(low_half, zero, q)], axis=0)
            k = jnp.concatenate([kv_ref[pl.ds(r, 64), lanes] for r in k_rows], axis=0)
            v_lanes = slice(MODEL + h * 128, MODEL + (h + 1) * 128)
            v = jnp.concatenate([kv_ref[pl.ds(r, 64), v_lanes] for r in k_rows], axis=0)
            logits = dot_nt(q, k) + bias
            top = jnp.max(logits, axis=-1, keepdims=True)
            share = jnp.exp(logits - top).astype(bf16)
            both = dot(share, jnp.concatenate([v, ones], axis=1))
            mixed = both[:, :128] / both[:, 128:]
            picked = jnp.where(low_half, mixed[:64, :], mixed[64:, :]).astype(bf16)
            for g in range(2):
                att_ref[pl.ds(q_rows[g], 32), lanes] = picked[g * 32 : (g + 1) * 32, :]
        return carry

    lax.fori_loop(0, 8, block, 0)

    copies[2].wait()
    if layer == 0:
        for g in range(4):
            rows = slice(g * GRP, (g + 1) * GRP)
            stream = stream_ref[rows, :] + dot(att_ref[rows, :], o_vmem[...])
            out_ref[rows, :] = stream
            inputs = normed(stream, gain_ref[1:2, :])
            x_ref[rows, :] = inputs
            xt_ref[g * HALO : (g + 1) * HALO, :] = inputs[:HALO, :]
            xb_ref[g * HALO : (g + 1) * HALO, :] = inputs[GRP - HALO :, :]
    else:
        for g in range(4):
            rows = slice(g * GRP, (g + 1) * GRP)
            stream = stream_ref[rows, :] + dot(att_ref[rows, :], o_vmem[...])
            att_ref[rows, :] = stream.astype(bf16)
        for r in range(0, 4 * GRP, GRP):
            to = iota((GRP, 4 * GRP), 0) + r
            source = iota((GRP, 4 * GRP), 1)
            wanted = (to // 4 % 4) * GRP + (to // 16) * 4 + to % 4
            out_ref[r : r + GRP, :] = dot(onehot(source == wanted), att_ref[...]).astype(bf16)


def attend(layer, place, halos, stream, qkv, gain, embed, qkv_weight, out_weight):
    any_spec = pl.BlockSpec(memory_space=pl.ANY)
    vmem = pl.BlockSpec(memory_space=pltpu.VMEM)
    smem = pl.BlockSpec(memory_space=pltpu.SMEM)
    operands = [place, *halos, stream, qkv]
    specs = [smem] + [vmem] * 6
    if layer == 0:
        operands += [gain, embed]
        specs += [vmem, vmem]
        out_shape = [
            jax.ShapeDtypeStruct((4 * GRP, MODEL), f32),
            jax.ShapeDtypeStruct((4 * GRP, MODEL), bf16),
            jax.ShapeDtypeStruct((EDGE, MODEL), bf16),
            jax.ShapeDtypeStruct((EDGE, MODEL), bf16),
        ]
    else:
        out_shape = jax.ShapeDtypeStruct((4 * GRP, MODEL), bf16)
    operands += [qkv_weight, out_weight]
    specs += [any_spec, any_spec]
    return pl.pallas_call(
        functools.partial(attend_kernel, layer),
        out_shape=out_shape,
        in_specs=specs,
        scratch_shapes=[
            pltpu.VMEM((2, MODEL, MODEL), bf16),
            pltpu.VMEM((MODEL, MODEL), bf16),
            pltpu.SemaphoreType.DMA((3,)),
            pltpu.VMEM((2 * EDGE + 2 * FULL, MODEL), bf16),
            pltpu.VMEM((6 * FULL, 2 * MODEL), bf16),
            pltpu.VMEM((4 * GRP, MODEL), bf16),
        ],
        compiler_params=pltpu.CompilerParams(vmem_limit_bytes=VMEM_BYTES),
        name="attend%d" % layer,
    )(*operands)


def shifted(cells, axis, by):
    count = lax.axis_size(axis)
    return lax.ppermute(cells, axis, [(i, (i + by) % count) for i in range(count)])


def around(x, first, last):
    top = shifted(last, "row", 1)
    bottom = shifted(first, "row", -1)
    right_edge = jnp.concatenate([top[3 * HALO :], x[3 * GRP :], bottom[3 * HALO :]], axis=0)
    left_edge = jnp.concatenate([top[:HALO], x[:GRP], bottom[:HALO]], axis=0)
    left = shifted(right_edge, "col", 1)
    right = shifted(left_edge, "col", -1)
    return top, bottom, left, right


def per_device(
    scans, dest, offsets, profile_index, profiles, embed_weight, attn_gain, qkv_weight, out_weight
):
    place = jnp.stack(
        [
            lax.axis_index("row") * TOK_H,
            lax.axis_index("col") * TOK_W,
            jnp.asarray(lax.axis_size("row") * TOK_H, i32),
            jnp.asarray(lax.axis_size("col") * TOK_W, i32),
        ]
    ).astype(i32)
    embed = embed_weight.reshape(CH, 8, 8, MODEL).transpose(1, 0, 2, 3).reshape(PATCH, MODEL)
    payload = pack(dest, offsets, profile_index, profiles, scans)
    payload = lax.all_to_all(payload, ("row", "col"), split_axis=0, concat_axis=0, tiled=True)
    x, first, last = merge(payload, profiles)
    halos = around(x, first, last)
    stream, qkv = own_part(0, x, embed, attn_gain, qkv_weight)
    stream, x, first, last = attend(
        0, place, halos, stream, qkv, attn_gain, embed, qkv_weight, out_weight
    )
    halos = around(x, first, last)
    qkv = own_part(1, x, None, None, qkv_weight)
    tokens = attend(1, place, halos, stream, qkv, None, None, qkv_weight, out_weight)
    return tokens.reshape(TOK_H, TOK_W, MODEL)


def solution(mesh):
    placed = (
        P(("row", "col"), None, None, None),
        P(("row", "col"), None),
        P(("row", "col")),
        P(("row", "col")),
        P(),
        P(),
        P(),
        P(),
        P(),
    )
    return jax.shard_map(
        per_device, mesh=mesh, in_specs=placed, out_specs=P("row", "col", None), check_vma=False
    )
```

```python
import functools

import jax
import jax.numpy as jnp
from jax import lax
from jax.experimental import pallas as pl
from jax.experimental.pallas import tpu as pltpu
from jax.sharding import PartitionSpec as P

HEADS = 16
RADIUS = 4
TOK_H = 32
TOK_W = 16
BR = 4
CH = 8
MODEL = 1024
PATCH = 512
GRP = 128
FULL = 160
HALO = 16
EDGE = 4 * HALO
META = 128
CHUNKS = 4
VMEM_BYTES = 20 * 1024 * 1024

f32 = jnp.float32
bf16 = jnp.bfloat16
i32 = jnp.int32


def dot(a, b):
    return lax.dot_general(a, b, (((1,), (0,)), ((), ())), preferred_element_type=f32)


def dot_nt(a, b):
    return lax.dot_general(a, b, (((1,), (1,)), ((), ())), preferred_element_type=f32)


def iota(shape, dim):
    return lax.broadcasted_iota(i32, shape, dim)


def onehot(cond):
    return jnp.where(cond, 1.0, 0.0).astype(bf16)


def halves(x):
    high = x.astype(bf16)
    return high, (x - high.astype(f32)).astype(bf16)


def pack_kernel(
    dest_hbm, offs_hbm, pidx_hbm, prof_hbm, scans_hbm, out_ref,
    dest_ref, offs_ref, pidx_ref, prof_ref, scans_ref, w_ref, sem,
):
    count = dest_ref.shape[1]
    chunk = scans_ref.shape[0] // CHUNKS
    small = [
        pltpu.make_async_copy(a, b, sem.at[n])
        for n, (a, b) in enumerate(
            [(dest_hbm, dest_ref), (offs_hbm, offs_ref), (pidx_hbm, pidx_ref), (prof_hbm, prof_ref)]
        )
    ]
    large = [
        pltpu.make_async_copy(
            scans_hbm.at[pl.ds(n * chunk, chunk)], scans_ref.at[pl.ds(n * chunk, chunk)], sem.at[4 + n]
        )
        for n in range(CHUNKS)
    ]
    for copy in small + large:
        copy.start()
    for copy in small:
        copy.wait()
    eye = iota((count, count), 0) == iota((count, count), 1)
    dest_row = dest_ref[...].astype(f32)
    dest_col = jnp.sum(jnp.where(eye, dest_row, 0.0), axis=1, keepdims=True)
    before = iota((count, count), 0) < iota((count, count), 1)
    same = (dest_col == dest_row) & before
    rank = jnp.sum(jnp.where(same, 1.0, 0.0), axis=0, keepdims=True)
    slot = dest_row * (2.0 * BR) + rank * float(BR)
    offs_col = jnp.sum(jnp.where(eye, offs_ref[...].astype(f32), 0.0), axis=1, keepdims=True)
    pidx_col = jnp.sum(jnp.where(eye, pidx_ref[...].astype(f32), 0.0), axis=1, keepdims=True)
    chosen = onehot(pidx_col == iota((count, prof_ref.shape[0]), 1).astype(f32))
    lane = iota((count, META), 1)
    meta = jnp.where(lane == 0, offs_col, jnp.where(lane == 1, pidx_col, 1.0)).astype(bf16)
    weights = []
    for k in range(BR):
        high, low = halves(prof_ref[:, k, :])
        weights.append(dot(chosen, high) + dot(chosen, low))
        w_ref[k * count : (k + 1) * count, CH * 128 :] = meta
    some = count // CHUNKS
    for n in range(CHUNKS):
        large[n].wait()
        for k in range(BR):
            for c in range(CH):
                block = scans_ref[pl.ds(n * chunk + k * CH + c, some, stride=BR * CH), :]
                at = k * count + n * some
                w_ref[at : at + some, c * 128 : (c + 1) * 128] = (
                    block * weights[k][n * some : (n + 1) * some, :]
                ).astype(bf16)
    rows = out_ref.shape[0]
    slots = jnp.concatenate([slot + float(k) for k in range(BR)], axis=1)
    step = 256
    for r in range(0, rows, step):
        here = (iota((step, BR * count), 0) + r).astype(f32)
        placing = onehot(here == slots)
        out_ref[r : r + step, :] = dot(placing, w_ref[...]).astype(bf16)


def pack(dest, offsets, profile_index, profiles, scans):
    count = scans.shape[0]
    rows = count * 2 * BR
    return pl.pallas_call(
        pack_kernel,
        out_shape=jax.ShapeDtypeStruct((rows, CH * 128 + META), bf16),
        in_specs=[pl.BlockSpec(memory_space=pltpu.HBM)] * 5,
        scratch_shapes=[
            pltpu.VMEM((1, count), i32),
            pltpu.VMEM((1, count), i32),
            pltpu.VMEM((1, count), i32),
            pltpu.VMEM(profiles.shape, f32),
            pltpu.VMEM((count * BR * CH, 128), f32),
            pltpu.VMEM((BR * count, CH * 128 + META), bf16),
            pltpu.SemaphoreType.DMA((4 + CHUNKS,)),
        ],
        compiler_params=pltpu.CompilerParams(vmem_limit_bytes=VMEM_BYTES),
        name="pack",
    )(
        in_hbm(dest.reshape(1, count)),
        in_hbm(offsets.reshape(1, count)),
        in_hbm(profile_index.reshape(1, count)),
        in_hbm(profiles),
        in_hbm(scans.reshape(count * BR * CH, 128)),
    )


def in_hbm(x):
    return pltpu.with_memory_space_constraint(x, pltpu.HBM)


def in_vmem(x):
    return pltpu.with_memory_space_constraint(x, pltpu.VMEM)


def merge_kernel(
    pay_ref, prof_ref, embed_hbm, w_hbm, x_ref, top_ref, bot_ref, embed_ref, w_ref,
    mg_ref, y_ref, xg_ref, sem,
):
    rows = pay_ref.shape[0]
    copies = [
        pltpu.make_async_copy(embed_hbm, embed_ref, sem.at[0]),
        pltpu.make_async_copy(w_hbm.at[0], w_ref, sem.at[1]),
    ]
    for copy in copies:
        copy.start()
    pick = onehot(iota((8, META), 0) == iota((8, META), 1))
    fields = dot_nt(pick, pay_ref[:, CH * 128 :])
    offs = fields[0:1, :]
    pidx = fields[1:2, :]
    valid = fields[2:3, :]
    strip = (iota((1, rows), 1) % BR).astype(f32)
    land = jnp.where(valid > 0.5, offs + strip, 4096.0)
    kind = pidx + 16.0 * strip
    r = iota((TOK_H * 8, rows), 0)
    pixel = (r % TOK_H) * 8 + r // TOK_H
    placing = onehot(pixel.astype(f32) == land)
    kinds = onehot(iota((16 * BR, rows), 0).astype(f32) == kind)
    counts = dot_nt(placing, kinds).astype(bf16)
    table = jnp.concatenate([prof_ref[:, k, :] for k in range(BR)], axis=0)
    high, low = halves(table)
    scale = 1.0 / (1.0 + dot(counts, high) + dot(counts, low))
    for c in range(CH):
        part = dot(placing, pay_ref[:, c * 128 : (c + 1) * 128])
        mg_ref[:, c * 128 : (c + 1) * 128] = (part * scale).astype(bf16)
    width = CH * 128
    step = 256
    for n in range(0, width, step):
        source = iota((width, step), 0)
        to = iota((width, step), 1) + n
        wanted = (to // 8 % CH) * 128 + (to // 64) * 8 + to % 8
        y_ref[:, n : n + step] = dot(mg_ref[...], onehot(source == wanted))
    low_half = iota((TOK_H, 128), 1) < 64
    order = iota((GRP, GRP), 1)
    want = iota((GRP, GRP), 0)
    reorder = onehot(order == (want % 4) * TOK_H + want // 4)
    for g in range(4):
        for jj in range(4):
            j = 4 * g + jj
            tile = (j // 2) * 128
            for pp in range(4):
                a = y_ref[2 * pp * TOK_H : (2 * pp + 1) * TOK_H, tile : tile + 128]
                b = y_ref[(2 * pp + 1) * TOK_H : (2 * pp + 2) * TOK_H, tile : tile + 128]
                if j % 2 == 0:
                    piece = jnp.where(low_half, a, pltpu.roll(b, 64, 1))
                else:
                    piece = jnp.where(low_half, pltpu.roll(a, 64, 1), b)
                xg_ref[jj * TOK_H : (jj + 1) * TOK_H, pp * 128 : (pp + 1) * 128] = piece.astype(
                    bf16
                )
        tokens = dot(reorder, xg_ref[...]).astype(bf16)
        x_ref[g * GRP : (g + 1) * GRP, :] = tokens
        top_ref[g * HALO : (g + 1) * HALO, :] = tokens[:HALO, :]
        bot_ref[g * HALO : (g + 1) * HALO, :] = tokens[GRP - HALO :, :]
    for copy in copies:
        copy.wait()


def merge(payload, profiles, embed, qkv_weight):
    vmem = pl.BlockSpec(memory_space=pltpu.VMEM)
    hbm = pl.BlockSpec(memory_space=pltpu.HBM)
    return pl.pallas_call(
        merge_kernel,
        out_shape=[
            jax.ShapeDtypeStruct((4 * GRP, PATCH), bf16),
            jax.ShapeDtypeStruct((EDGE, PATCH), bf16),
            jax.ShapeDtypeStruct((EDGE, PATCH), bf16),
            pltpu.VMEM((PATCH, MODEL), bf16),
            pltpu.VMEM((MODEL, 3 * MODEL), bf16),
        ],
        in_specs=[vmem, vmem, hbm, hbm],
        scratch_shapes=[
            pltpu.VMEM((TOK_H * 8, CH * 128), bf16),
            pltpu.VMEM((TOK_H * 8, CH * 128), f32),
            pltpu.VMEM((GRP, PATCH), bf16),
            pltpu.SemaphoreType.DMA((2,)),
        ],
        compiler_params=pltpu.CompilerParams(vmem_limit_bytes=VMEM_BYTES),
        name="merge",
    )(payload, profiles, in_hbm(embed), in_hbm(qkv_weight))


def normed(stream, gain):
    centre = jnp.mean(stream, -1, keepdims=True)
    moved = stream - centre
    spread = jnp.mean(jnp.square(moved), -1, keepdims=True)
    return (moved * lax.rsqrt(spread + 1e-05) * gain).astype(bf16)


def own_kernel(layer, *refs):
    if layer == 0:
        x_ref, embed_ref, gain_ref, w_ref, stream_ref, qkv_ref, inp_ref = refs
        for r in range(0, 4 * GRP, GRP):
            stream = dot(x_ref[r : r + GRP, :], embed_ref[...])
            stream_ref[r : r + GRP, :] = stream
            inp_ref[r : r + GRP, :] = normed(stream, gain_ref[0:1, :])
    else:
        inp_ref, w_ref, qkv_ref = refs
    step = 256
    for m in range(0, 3 * MODEL, step):
        part = dot(inp_ref[...], w_ref[:, m : m + step]).astype(bf16)
        if m < MODEL:
            part = part * jnp.asarray(0.125, bf16)
        qkv_ref[:, m : m + step] = part


def own_part(layer, x, embed, gain, w):
    vmem = pl.BlockSpec(memory_space=pltpu.VMEM)
    qkv = jax.ShapeDtypeStruct((4 * GRP, 3 * MODEL), bf16)
    params = pltpu.CompilerParams(vmem_limit_bytes=VMEM_BYTES)
    cost = pl.CostEstimate(
        flops=2 * 4 * GRP * MODEL * 3 * MODEL, bytes_accessed=12 << 20, transcendentals=0
    )
    if layer == 0:
        return pl.pallas_call(
            functools.partial(own_kernel, layer),
            out_shape=[jax.ShapeDtypeStruct((4 * GRP, MODEL), f32), qkv],
            in_specs=[vmem] * 4,
            scratch_shapes=[pltpu.VMEM((4 * GRP, MODEL), bf16)],
            compiler_params=params,
            cost_estimate=cost,
            name="own0",
        )(x, in_vmem(embed), gain, in_vmem(w))
    return pl.pallas_call(
        functools.partial(own_kernel, layer),
        out_shape=qkv,
        in_specs=[vmem] * 2,
        compiler_params=params,
        cost_estimate=cost,
        name="own1",
    )(x, in_vmem(w))


def attend_kernel(layer, *refs):
    if layer == 0:
        (place_ref, top_ref, bot_ref, left_ref, right_ref, stream_ref, qkv_ref, gain_ref, embed_ref,
         w_ref, o_hbm, next_hbm, out_ref, x_ref, xt_ref, xb_ref, next_ref,
         halo_ref, kv_ref, att_ref, o_ref, sem) = refs
    else:
        (place_ref, top_ref, bot_ref, left_ref, right_ref, stream_ref, qkv_ref,
         w_ref, o_hbm, out_ref,
         halo_ref, kv_ref, att_ref, o_ref, sem) = refs
    copies = [pltpu.make_async_copy(o_hbm.at[layer], o_ref, sem.at[0])]
    if layer == 0:
        copies.append(pltpu.make_async_copy(next_hbm.at[1], next_ref, sem.at[1]))
    for copy in copies:
        copy.start()
    row = 0
    for ref in (top_ref, bot_ref, left_ref, right_ref):
        part = ref[...]
        if layer == 0:
            part = normed(dot(part, embed_ref[...]), gain_ref[0:1, :])
        halo_ref[row : row + ref.shape[0], :] = part
        row += ref.shape[0]
    for g in range(4):
        at = (g + 1) * FULL + HALO
        kv_ref[at : at + GRP, :] = qkv_ref[g * GRP : (g + 1) * GRP, MODEL:]
    step = 256
    for n in range(2):
        for m in range(0, MODEL, step):
            lanes = slice(n * MODEL + m, n * MODEL + m + step)
            part = dot(
                halo_ref[...], w_ref[:, MODEL + lanes.start : MODEL + lanes.stop]
            ).astype(bf16)
            for g in range(4):
                at = (g + 1) * FULL
                kv_ref[at : at + HALO, lanes] = part[g * HALO : (g + 1) * HALO, :]
                kv_ref[at + HALO + GRP : at + FULL, lanes] = part[
                    EDGE + g * HALO : EDGE + (g + 1) * HALO, :
                ]
            kv_ref[0:FULL, lanes] = part[2 * EDGE : 2 * EDGE + FULL, :]
            kv_ref[5 * FULL : 6 * FULL, lanes] = part[2 * EDGE + FULL :, :]

    query = iota((64, 256), 0)
    key = iota((64, 256), 1)
    row_gap = (key % 64) // 4 - 4 - (query % 32) // 4
    col_gap = (key // 64 - 1) * 4 + key % 4 - (query // 32) * 4 - query % 4
    near = (jnp.abs(row_gap) <= RADIUS) & (jnp.abs(col_gap) <= RADIUS)
    near_bias = jnp.where(near, 0.0, -1e30)
    lane_key = iota((1, 256), 1)
    key_row = (lane_key % 64) // 4 - 4
    key_col = (lane_key // 64 - 1) * 4 + lane_key % 4
    low_half = iota((64, 128), 1) < 64
    zero = jnp.zeros((64, 128), bf16)
    ones = jnp.ones((256, 128), bf16)
    height, width = place_ref[2], place_ref[3]

    def block(b, carry):
        bi, bj = b // 2, b % 2
        at_row = key_row + bi * 8 + place_ref[0]
        at_col = key_col + bj * 8 + place_ref[1]
        inside = (at_row >= 0) & (at_row < height) & (at_col >= 0) & (at_col < width)
        bias = near_bias + jnp.where(inside, 0.0, -1e30)
        bias = jnp.concatenate([bias, bias], axis=0)
        q_rows = [pl.multiple_of((2 * bj + g) * GRP + bi * 32, 32) for g in range(2)]
        k_rows = [pl.multiple_of((2 * bj + g) * FULL + bi * 32, 32) for g in range(4)]
        for h in range(HEADS // 2):
            lanes = slice(h * 128, (h + 1) * 128)
            q = jnp.concatenate([qkv_ref[pl.ds(r, 32), lanes] for r in q_rows], axis=0)
            q = jnp.concatenate([jnp.where(low_half, q, zero), jnp.where(low_half, zero, q)], axis=0)
            k = jnp.concatenate([kv_ref[pl.ds(r, 64), lanes] for r in k_rows], axis=0)
            v_lanes = slice(MODEL + h * 128, MODEL + (h + 1) * 128)
            v = jnp.concatenate([kv_ref[pl.ds(r, 64), v_lanes] for r in k_rows], axis=0)
            logits = dot_nt(q, k) + bias
            top = jnp.max(logits, axis=-1, keepdims=True)
            share = jnp.exp(logits - top).astype(bf16)
            both = dot(share, jnp.concatenate([v, ones], axis=1))
            mixed = both[:, :128] / both[:, 128:]
            picked = jnp.where(low_half, mixed[:64, :], mixed[64:, :]).astype(bf16)
            for g in range(2):
                att_ref[pl.ds(q_rows[g], 32), lanes] = picked[g * 32 : (g + 1) * 32, :]
        return carry

    lax.fori_loop(0, 8, block, 0)
    for copy in copies:
        copy.wait()

    if layer == 0:
        for g in range(4):
            rows = slice(g * GRP, (g + 1) * GRP)
            stream = stream_ref[rows, :] + dot(att_ref[rows, :], o_ref[...])
            out_ref[rows, :] = stream
            inputs = normed(stream, gain_ref[1:2, :])
            x_ref[rows, :] = inputs
            xt_ref[g * HALO : (g + 1) * HALO, :] = inputs[:HALO, :]
            xb_ref[g * HALO : (g + 1) * HALO, :] = inputs[GRP - HALO :, :]
    else:
        for g in range(4):
            rows = slice(g * GRP, (g + 1) * GRP)
            stream = stream_ref[rows, :] + dot(att_ref[rows, :], o_ref[...])
            att_ref[rows, :] = stream.astype(bf16)
        for r in range(0, 4 * GRP, GRP):
            to = iota((GRP, 4 * GRP), 0) + r
            source = iota((GRP, 4 * GRP), 1)
            wanted = (to // 4 % 4) * GRP + (to // 16) * 4 + to % 4
            out_ref[r : r + GRP, :] = dot(onehot(source == wanted), att_ref[...]).astype(bf16)


def attend(layer, place, halos, stream, qkv, gain, embed, w, out_weight, qkv_weight):
    hbm = pl.BlockSpec(memory_space=pltpu.HBM)
    vmem = pl.BlockSpec(memory_space=pltpu.VMEM)
    smem = pl.BlockSpec(memory_space=pltpu.SMEM)
    operands = [place, *halos, stream, qkv]
    specs = [smem] + [vmem] * 6
    if layer == 0:
        operands += [gain, in_vmem(embed)]
        specs += [vmem, vmem]
        out_shape = [
            jax.ShapeDtypeStruct((4 * GRP, MODEL), f32),
            jax.ShapeDtypeStruct((4 * GRP, MODEL), bf16),
            jax.ShapeDtypeStruct((EDGE, MODEL), bf16),
            jax.ShapeDtypeStruct((EDGE, MODEL), bf16),
        ]
    else:
        out_shape = jax.ShapeDtypeStruct((4 * GRP, MODEL), bf16)
    operands += [in_vmem(w), in_hbm(out_weight)]
    specs += [vmem, hbm]
    if layer == 0:
        operands.append(in_hbm(qkv_weight))
        specs.append(hbm)
        out_shape.append(pltpu.VMEM((MODEL, 3 * MODEL), bf16))
    return pl.pallas_call(
        functools.partial(attend_kernel, layer),
        out_shape=out_shape,
        in_specs=specs,
        scratch_shapes=[
            pltpu.VMEM((2 * EDGE + 2 * FULL, MODEL), bf16),
            pltpu.VMEM((6 * FULL, 2 * MODEL), bf16),
            pltpu.VMEM((4 * GRP, MODEL), bf16),
            pltpu.VMEM((MODEL, MODEL), bf16),
            pltpu.SemaphoreType.DMA((2,)),
        ],
        compiler_params=pltpu.CompilerParams(vmem_limit_bytes=VMEM_BYTES),
        name="attend%d" % layer,
    )(*operands)


def shifted(cells, axis, by):
    count = lax.axis_size(axis)
    return lax.ppermute(cells, axis, [(i, (i + by) % count) for i in range(count)])


def around(x, first, last):
    top = shifted(last, "row", 1)
    bottom = shifted(first, "row", -1)
    right_edge = jnp.concatenate([top[3 * HALO :], x[3 * GRP :], bottom[3 * HALO :]], axis=0)
    left_edge = jnp.concatenate([top[:HALO], x[:GRP], bottom[:HALO]], axis=0)
    left = shifted(right_edge, "col", 1)
    right = shifted(left_edge, "col", -1)
    return top, bottom, left, right


def per_device(
    scans, dest, offsets, profile_index, profiles, embed_weight, attn_gain, qkv_weight, out_weight
):
    place = jnp.stack(
        [
            lax.axis_index("row") * TOK_H,
            lax.axis_index("col") * TOK_W,
            jnp.asarray(lax.axis_size("row") * TOK_H, i32),
            jnp.asarray(lax.axis_size("col") * TOK_W, i32),
        ]
    ).astype(i32)
    embed = embed_weight.reshape(CH, 8, 8, MODEL).transpose(1, 0, 2, 3).reshape(PATCH, MODEL)
    payload = pack(dest, offsets, profile_index, profiles, scans)
    payload = lax.all_to_all(payload, ("row", "col"), split_axis=0, concat_axis=0, tiled=True)
    x, first, last, embed, w = merge(payload, profiles, embed, qkv_weight)
    halos = around(x, first, last)
    stream, qkv = own_part(0, x, embed, attn_gain, w)
    stream, x, first, last, w = attend(
        0, place, halos, stream, qkv, attn_gain, embed, w, out_weight, qkv_weight
    )
    halos = around(x, first, last)
    qkv = own_part(1, x, None, None, w)
    tokens = attend(1, place, halos, stream, qkv, None, None, w, out_weight, None)
    return tokens.reshape(TOK_H, TOK_W, MODEL)


def solution(mesh):
    placed = (
        P(("row", "col"), None, None, None),
        P(("row", "col"), None),
        P(("row", "col")),
        P(("row", "col")),
        P(),
        P(),
        P(),
        P(),
        P(),
    )
    return jax.shard_map(
        per_device, mesh=mesh, in_specs=placed, out_specs=P("row", "col", None), check_vma=False
    )
```

```python
import functools

import jax
import jax.numpy as jnp
from jax import lax
from jax.experimental import pallas as pl
from jax.experimental.pallas import tpu as pltpu
from jax.sharding import PartitionSpec as P

HEADS = 16
RADIUS = 4
TOK_H = 32
TOK_W = 16
BR = 4
CH = 8
MODEL = 1024
PATCH = 512
GRP = 128
MID = 160
WIDE = 192
HALO = 32
EDGE = 4 * HALO
SIDE = 2 * WIDE
META = 128
CHUNKS = 4
VMEM_BYTES = 20 * 1024 * 1024
LARGE_BYTES = 40 * 1024 * 1024

f32 = jnp.float32
bf16 = jnp.bfloat16
i32 = jnp.int32


def dot(a, b):
    return lax.dot_general(a, b, (((1,), (0,)), ((), ())), preferred_element_type=f32)


def dot_nt(a, b):
    return lax.dot_general(a, b, (((1,), (1,)), ((), ())), preferred_element_type=f32)


def iota(shape, dim):
    return lax.broadcasted_iota(i32, shape, dim)


def onehot(cond):
    return jnp.where(cond, 1.0, 0.0).astype(bf16)


def halves(x):
    high = x.astype(bf16)
    return high, (x - high.astype(f32)).astype(bf16)


def pack_kernel(
    dest_hbm, offs_hbm, pidx_hbm, prof_hbm, scans_hbm, out_ref,
    dest_ref, offs_ref, pidx_ref, prof_ref, scans_ref, w_ref, sem,
):
    count = dest_ref.shape[1]
    chunk = scans_ref.shape[0] // CHUNKS
    small = [
        pltpu.make_async_copy(a, b, sem.at[n])
        for n, (a, b) in enumerate(
            [(dest_hbm, dest_ref), (offs_hbm, offs_ref), (pidx_hbm, pidx_ref), (prof_hbm, prof_ref)]
        )
    ]
    large = [
        pltpu.make_async_copy(
            scans_hbm.at[pl.ds(n * chunk, chunk)], scans_ref.at[pl.ds(n * chunk, chunk)], sem.at[4 + n]
        )
        for n in range(CHUNKS)
    ]
    for copy in small + large:
        copy.start()
    for copy in small:
        copy.wait()
    eye = iota((count, count), 0) == iota((count, count), 1)
    dest_row = dest_ref[...].astype(f32)
    dest_col = jnp.sum(jnp.where(eye, dest_row, 0.0), axis=1, keepdims=True)
    before = iota((count, count), 0) < iota((count, count), 1)
    same = (dest_col == dest_row) & before
    rank = jnp.sum(jnp.where(same, 1.0, 0.0), axis=0, keepdims=True)
    slot = dest_row * (2.0 * BR) + rank * float(BR)
    offs_col = jnp.sum(jnp.where(eye, offs_ref[...].astype(f32), 0.0), axis=1, keepdims=True)
    pidx_col = jnp.sum(jnp.where(eye, pidx_ref[...].astype(f32), 0.0), axis=1, keepdims=True)
    chosen = onehot(pidx_col == iota((count, prof_ref.shape[0]), 1).astype(f32))
    lane = iota((count, META), 1)
    meta = jnp.where(lane == 0, offs_col, jnp.where(lane == 1, pidx_col, 1.0)).astype(bf16)
    weights = []
    for k in range(BR):
        high, low = halves(prof_ref[:, k, :])
        weights.append(dot(chosen, high) + dot(chosen, low))
        w_ref[k * count : (k + 1) * count, CH * 128 :] = meta
    some = count // CHUNKS
    for n in range(CHUNKS):
        large[n].wait()
        for k in range(BR):
            for c in range(CH):
                block = scans_ref[pl.ds(n * chunk + k * CH + c, some, stride=BR * CH), :]
                at = k * count + n * some
                w_ref[at : at + some, c * 128 : (c + 1) * 128] = (
                    block * weights[k][n * some : (n + 1) * some, :]
                ).astype(bf16)
    rows = out_ref.shape[0]
    slots = jnp.concatenate([slot + float(k) for k in range(BR)], axis=1)
    step = 256
    for r in range(0, rows, step):
        here = (iota((step, BR * count), 0) + r).astype(f32)
        placing = onehot(here == slots)
        out_ref[r : r + step, :] = dot(placing, w_ref[...]).astype(bf16)


def pack(dest, offsets, profile_index, profiles, scans):
    count = scans.shape[0]
    rows = count * 2 * BR
    return pl.pallas_call(
        pack_kernel,
        out_shape=jax.ShapeDtypeStruct((rows, CH * 128 + META), bf16),
        in_specs=[pl.BlockSpec(memory_space=pltpu.HBM)] * 5,
        scratch_shapes=[
            pltpu.VMEM((1, count), i32),
            pltpu.VMEM((1, count), i32),
            pltpu.VMEM((1, count), i32),
            pltpu.VMEM(profiles.shape, f32),
            pltpu.VMEM((count * BR * CH, 128), f32),
            pltpu.VMEM((BR * count, CH * 128 + META), bf16),
            pltpu.SemaphoreType.DMA((4 + CHUNKS,)),
        ],
        compiler_params=pltpu.CompilerParams(vmem_limit_bytes=VMEM_BYTES),
        name="pack",
    )(
        in_hbm(dest.reshape(1, count)),
        in_hbm(offsets.reshape(1, count)),
        in_hbm(profile_index.reshape(1, count)),
        in_hbm(profiles),
        in_hbm(scans.reshape(count * BR * CH, 128)),
    )


def in_hbm(x):
    return pltpu.with_memory_space_constraint(x, pltpu.HBM)


def in_vmem(x):
    return pltpu.with_memory_space_constraint(x, pltpu.VMEM)


def merge_kernel(
    pay_ref, prof_ref, embed_hbm, w_hbm, x_ref, top_ref, bot_ref, embed_ref, w_ref,
    mg_ref, y_ref, xg_ref, sem,
):
    rows = pay_ref.shape[0]
    copies = [
        pltpu.make_async_copy(embed_hbm, embed_ref, sem.at[0]),
        pltpu.make_async_copy(w_hbm.at[0], w_ref, sem.at[1]),
    ]
    for copy in copies:
        copy.start()
    pick = onehot(iota((8, META), 0) == iota((8, META), 1))
    fields = dot_nt(pick, pay_ref[:, CH * 128 :])
    offs = fields[0:1, :]
    pidx = fields[1:2, :]
    valid = fields[2:3, :]
    strip = (iota((1, rows), 1) % BR).astype(f32)
    land = jnp.where(valid > 0.5, offs + strip, 4096.0)
    kind = pidx + 16.0 * strip
    r = iota((TOK_H * 8, rows), 0)
    pixel = (r % TOK_H) * 8 + r // TOK_H
    placing = onehot(pixel.astype(f32) == land)
    kinds = onehot(iota((16 * BR, rows), 0).astype(f32) == kind)
    counts = dot_nt(placing, kinds).astype(bf16)
    table = jnp.concatenate([prof_ref[:, k, :] for k in range(BR)], axis=0)
    high, low = halves(table)
    scale = 1.0 / (1.0 + dot(counts, high) + dot(counts, low))
    for c in range(CH):
        part = dot(placing, pay_ref[:, c * 128 : (c + 1) * 128])
        mg_ref[:, c * 128 : (c + 1) * 128] = (part * scale).astype(bf16)
    width = CH * 128
    step = 256
    for n in range(0, width, step):
        source = iota((width, step), 0)
        to = iota((width, step), 1) + n
        wanted = (to // 8 % CH) * 128 + (to // 64) * 8 + to % 8
        y_ref[:, n : n + step] = dot(mg_ref[...], onehot(source == wanted))
    low_half = iota((TOK_H, 128), 1) < 64
    order = iota((GRP, GRP), 1)
    want = iota((GRP, GRP), 0)
    reorder = onehot(order == (want % 4) * TOK_H + want // 4)
    for g in range(4):
        for jj in range(4):
            j = 4 * g + jj
            tile = (j // 2) * 128
            for pp in range(4):
                a = y_ref[2 * pp * TOK_H : (2 * pp + 1) * TOK_H, tile : tile + 128]
                b = y_ref[(2 * pp + 1) * TOK_H : (2 * pp + 2) * TOK_H, tile : tile + 128]
                if j % 2 == 0:
                    piece = jnp.where(low_half, a, pltpu.roll(b, 64, 1))
                else:
                    piece = jnp.where(low_half, pltpu.roll(a, 64, 1), b)
                xg_ref[jj * TOK_H : (jj + 1) * TOK_H, pp * 128 : (pp + 1) * 128] = piece.astype(
                    bf16
                )
        tokens = dot(reorder, xg_ref[...]).astype(bf16)
        x_ref[g * GRP : (g + 1) * GRP, :] = tokens
        top_ref[g * HALO : (g + 1) * HALO, :] = tokens[:HALO, :]
        bot_ref[g * HALO : (g + 1) * HALO, :] = tokens[GRP - HALO :, :]
    for copy in copies:
        copy.wait()


def merge(payload, profiles, embed, qkv_weight):
    vmem = pl.BlockSpec(memory_space=pltpu.VMEM)
    hbm = pl.BlockSpec(memory_space=pltpu.HBM)
    return pl.pallas_call(
        merge_kernel,
        out_shape=[
            jax.ShapeDtypeStruct((4 * GRP, PATCH), bf16),
            jax.ShapeDtypeStruct((EDGE, PATCH), bf16),
            jax.ShapeDtypeStruct((EDGE, PATCH), bf16),
            pltpu.VMEM((PATCH, MODEL), bf16),
            pltpu.VMEM((MODEL, 3 * MODEL), bf16),
        ],
        in_specs=[vmem, vmem, hbm, hbm],
        scratch_shapes=[
            pltpu.VMEM((TOK_H * 8, CH * 128), bf16),
            pltpu.VMEM((TOK_H * 8, CH * 128), f32),
            pltpu.VMEM((GRP, PATCH), bf16),
            pltpu.SemaphoreType.DMA((2,)),
        ],
        compiler_params=pltpu.CompilerParams(vmem_limit_bytes=VMEM_BYTES),
        name="merge",
    )(payload, profiles, in_hbm(embed), in_hbm(qkv_weight))


def normed(stream, gain):
    centre = jnp.mean(stream, -1, keepdims=True)
    moved = stream - centre
    spread = jnp.mean(jnp.square(moved), -1, keepdims=True)
    return (moved * lax.rsqrt(spread + 1e-05) * gain).astype(bf16)


def own_kernel(x_ref, embed_ref, gain_ref, w_ref, stream_ref, qkv_ref, inp_ref):
    for r in range(0, 4 * GRP, GRP):
        stream = dot(x_ref[r : r + GRP, :], embed_ref[...])
        stream_ref[r : r + GRP, :] = stream
        inp_ref[r : r + GRP, :] = normed(stream, gain_ref[0:1, :])
    step = 256
    for m in range(0, 3 * MODEL, step):
        part = dot(inp_ref[...], w_ref[:, m : m + step]).astype(bf16)
        if m < MODEL:
            part = part * jnp.asarray(0.125, bf16)
        qkv_ref[:, m : m + step] = part


def own_part(x, embed, gain, w):
    return pl.pallas_call(
        own_kernel,
        out_shape=[
            jax.ShapeDtypeStruct((4 * GRP, MODEL), f32),
            jax.ShapeDtypeStruct((4 * GRP, 3 * MODEL), bf16),
        ],
        scratch_shapes=[pltpu.VMEM((4 * GRP, MODEL), bf16)],
        compiler_params=pltpu.CompilerParams(vmem_limit_bytes=VMEM_BYTES),
        cost_estimate=pl.CostEstimate(
            flops=2 * 4 * GRP * MODEL * 3 * MODEL, bytes_accessed=12 << 20, transcendentals=0
        ),
        name="own",
    )(x, in_vmem(embed), gain, in_vmem(w))


def attention(q_ref, q_at, q_pitch, kv_ref, k_pitch, a_ref, a_pitch, tall, broad, row, col, ends):
    query = iota((64, 256), 0)
    key = iota((64, 256), 1)
    row_gap = (key % 64) // 4 - 4 - (query % 32) // 4
    col_gap = (key // 64 - 1) * 4 + key % 4 - (query // 32) * 4 - query % 4
    near = (jnp.abs(row_gap) <= RADIUS) & (jnp.abs(col_gap) <= RADIUS)
    near_bias = jnp.where(near, 0.0, -1e30)
    lane_key = iota((1, 256), 1)
    key_row = (lane_key % 64) // 4 + row
    key_col = (lane_key // 64) * 4 + lane_key % 4 + col
    low_half = iota((64, 128), 1) < 64
    zero = jnp.zeros((64, 128), bf16)
    ones = jnp.ones((256, 128), bf16)

    def strip(bi, carry):
        at_row = key_row + bi * 8
        row_inside = (at_row >= 0) & (at_row < ends[0])
        for bj in range(broad):
            at_col = key_col + bj * 8
            inside = row_inside & (at_col >= 0) & (at_col < ends[1])
            bias = near_bias + jnp.where(inside, 0.0, -1e30)
            bias = jnp.concatenate([bias, bias], axis=0)
            q_rows = [
                pl.ds(pl.multiple_of((2 * bj + g) * q_pitch + q_at + bi * 32, 16), 32)
                for g in range(2)
            ]
            a_rows = [
                pl.ds(pl.multiple_of((2 * bj + g) * a_pitch + bi * 32, 32), 32) for g in range(2)
            ]
            k_rows = [
                pl.ds(pl.multiple_of((2 * bj + g) * k_pitch + bi * 32, 32), 64) for g in range(4)
            ]
            for h in range(HEADS // 2):
                lanes = slice(h * 128, (h + 1) * 128)
                q = jnp.concatenate([q_ref[r, lanes] for r in q_rows], axis=0)
                q = jnp.concatenate(
                    [jnp.where(low_half, q, zero), jnp.where(low_half, zero, q)], axis=0
                )
                k = jnp.concatenate([kv_ref[r, lanes] for r in k_rows], axis=0)
                v_lanes = slice(MODEL + h * 128, MODEL + (h + 1) * 128)
                v = jnp.concatenate([kv_ref[r, v_lanes] for r in k_rows], axis=0)
                logits = dot_nt(q, k) + bias
                top = jnp.max(logits, axis=-1, keepdims=True)
                share = jnp.exp(logits - top).astype(bf16)
                both = dot(share, jnp.concatenate([v, ones], axis=1))
                mixed = jnp.where(low_half, both[:64, :128], both[64:, :128])
                total = jnp.where(low_half, both[:64, 128:], both[64:, 128:])
                picked = (mixed / total).astype(bf16)
                for g in range(2):
                    a_ref[a_rows[g], lanes] = picked[g * 32 : (g + 1) * 32, :]
        return carry

    lax.fori_loop(0, tall, strip, 0, unroll=True)


def rest_kernel(
    place_ref, top_ref, bot_ref, left_ref, right_ref, stream_ref, qkv_ref, gain_ref, embed_ref,
    w_ref, w_hbm, o_hbm, out_ref,
    next_ref, o_ref, halo_ref, kv_ref, q_ref, mid_ref, att_ref, inp_ref, sem,
):
    copies = [
        pltpu.make_async_copy(o_hbm.at[0], o_ref.at[0], sem.at[0]),
        pltpu.make_async_copy(w_hbm.at[1], next_ref, sem.at[1]),
        pltpu.make_async_copy(o_hbm.at[1], o_ref.at[1], sem.at[2]),
    ]
    for copy in copies:
        copy.start()
    step = 256
    scale = jnp.asarray(0.125, bf16)

    for g in range(4):
        own = slice(g * GRP, (g + 1) * GRP)
        at = (g + 1) * MID + 16
        mid_ref[at : at + GRP, :] = stream_ref[own, :]
        q_ref[at : at + GRP, :] = qkv_ref[own, :MODEL]
        at = (g + 2) * WIDE + HALO
        kv_ref[at : at + GRP, :] = qkv_ref[own, MODEL:]

    def enter(piece, row):
        stream = dot(piece, embed_ref[...])
        halo_ref[row : row + piece.shape[0], :] = normed(stream, gain_ref[0:1, :])
        return stream

    def side(ref, g):
        return jnp.concatenate(
            [
                ref[g * HALO : (g + 1) * HALO, :],
                ref[2 * HALO + g * GRP : 2 * HALO + (g + 1) * GRP, :],
                ref[2 * HALO + 2 * GRP + g * HALO : 2 * HALO + 2 * GRP + (g + 1) * HALO, :],
            ],
            axis=0,
        )

    first_q = WIDE
    left_q = WIDE + 2 * EDGE
    right_q = left_q + WIDE
    last = right_q + WIDE
    enter(side(left_ref, 0), 0)
    top = enter(top_ref[...], first_q)
    bottom = enter(bot_ref[...], first_q + EDGE)
    for g in range(4):
        at = (g + 1) * MID
        mid_ref[at : at + 16, :] = top[g * HALO + 16 : (g + 1) * HALO, :]
        mid_ref[at + 16 + GRP : at + MID, :] = bottom[g * HALO : g * HALO + 16, :]
    mid_ref[:MID, :] = enter(side(left_ref, 1), left_q)[16 : 16 + MID, :]
    mid_ref[5 * MID :, :] = enter(side(right_ref, 0), right_q)[16 : 16 + MID, :]
    enter(side(right_ref, 1), last)
    for m in range(0, 3 * MODEL, step):
        if m < MODEL:
            lanes = slice(m, m + step)
            part = dot(halo_ref[first_q:last, :], w_ref[:, lanes]).astype(bf16) * scale
            for g in range(4):
                at = (g + 1) * MID
                q_ref[at : at + 16, lanes] = part[g * HALO + 16 : (g + 1) * HALO, :]
                q_ref[at + 16 + GRP : at + MID, lanes] = part[
                    EDGE + g * HALO : EDGE + g * HALO + 16, :
                ]
            at = left_q - first_q + 16
            q_ref[:MID, lanes] = part[at : at + MID, :]
            at = right_q - first_q + 16
            q_ref[5 * MID :, lanes] = part[at : at + MID, :]
        else:
            lanes = slice(m - MODEL, m - MODEL + step)
            part = dot(halo_ref[...], w_ref[:, m : m + step]).astype(bf16)
            kv_ref[:WIDE, lanes] = part[:WIDE, :]
            kv_ref[WIDE : 2 * WIDE, lanes] = part[left_q:right_q, :]
            kv_ref[6 * WIDE :, lanes] = part[right_q:, :]
            for g in range(4):
                at = (g + 2) * WIDE
                kv_ref[at : at + HALO, lanes] = part[first_q + g * HALO : first_q + (g + 1) * HALO, :]
                kv_ref[at + HALO + GRP : at + WIDE, lanes] = part[
                    first_q + EDGE + g * HALO : first_q + EDGE + (g + 1) * HALO, :
                ]

    ends = (place_ref[2], place_ref[3])
    attention(
        q_ref, 0, MID, kv_ref, WIDE, att_ref, MID, 5, 3, place_ref[0] - 8, place_ref[1] - 8, ends
    )
    copies[0].wait()
    for g in range(6):
        rows = slice(g * MID, (g + 1) * MID)
        stream = mid_ref[rows, :] + dot(att_ref[rows, :], o_ref[0])
        mid_ref[rows, :] = stream
        inp_ref[rows, :] = normed(stream, gain_ref[1:2, :])

    copies[1].wait()
    for m in range(0, 3 * MODEL, step):
        if m < MODEL:
            part = dot(inp_ref[MID : 5 * MID, :], next_ref[:, m : m + step]).astype(bf16) * scale
            q_ref[: 4 * MID, m : m + step] = part
        else:
            part = dot(inp_ref[...], next_ref[:, m : m + step]).astype(bf16)
            kv_ref[: 6 * MID, m - MODEL : m - MODEL + step] = part
    attention(
        q_ref, 16, MID, kv_ref, MID, att_ref, GRP, 4, 2, place_ref[0] - 4, place_ref[1] - 4, ends
    )
    copies[2].wait()
    for g in range(4):
        rows = slice(g * GRP, (g + 1) * GRP)
        at = (g + 1) * MID + 16
        stream = mid_ref[at : at + GRP, :] + dot(att_ref[rows, :], o_ref[1])
        inp_ref[rows, :] = stream.astype(bf16)
    for r in range(0, 4 * GRP, GRP):
        to = iota((GRP, 4 * GRP), 0) + r
        source = iota((GRP, 4 * GRP), 1)
        wanted = (to // 4 % 4) * GRP + (to // 16) * 4 + to % 4
        out_ref[r : r + GRP, :] = dot(onehot(source == wanted), inp_ref[: 4 * GRP, :]).astype(bf16)


def rest(place, halos, stream, qkv, gain, embed, w, qkv_weight, out_weight):
    hbm = pl.BlockSpec(memory_space=pltpu.HBM)
    vmem = pl.BlockSpec(memory_space=pltpu.VMEM)
    smem = pl.BlockSpec(memory_space=pltpu.SMEM)
    return pl.pallas_call(
        rest_kernel,
        out_shape=jax.ShapeDtypeStruct((4 * GRP, MODEL), bf16),
        in_specs=[smem] + [vmem] * 9 + [hbm] * 2,
        scratch_shapes=[
            pltpu.VMEM((MODEL, 3 * MODEL), bf16),
            pltpu.VMEM((2, MODEL, MODEL), bf16),
            pltpu.VMEM((2 * EDGE + 2 * SIDE, MODEL), bf16),
            pltpu.VMEM((8 * WIDE, 2 * MODEL), bf16),
            pltpu.VMEM((6 * MID, MODEL), bf16),
            pltpu.VMEM((6 * MID, MODEL), f32),
            pltpu.VMEM((6 * MID, MODEL), bf16),
            pltpu.VMEM((6 * MID, MODEL), bf16),
            pltpu.SemaphoreType.DMA((3,)),
        ],
        compiler_params=pltpu.CompilerParams(vmem_limit_bytes=LARGE_BYTES),
        name="rest",
    )(
        place, *halos, stream, qkv, gain, in_vmem(embed), in_vmem(w),
        in_hbm(qkv_weight), in_hbm(out_weight),
    )


def shifted(cells, axis, by):
    count = lax.axis_size(axis)
    return lax.ppermute(cells, axis, [(i, (i + by) % count) for i in range(count)])


def around(x, first, last):
    top = shifted(last, "row", 1)
    bottom = shifted(first, "row", -1)
    two = 2 * HALO
    right_edge = jnp.concatenate([top[two:], x[2 * GRP :], bottom[two:]], axis=0)
    left_edge = jnp.concatenate([top[:two], x[: 2 * GRP], bottom[:two]], axis=0)
    left = shifted(right_edge, "col", 1)
    right = shifted(left_edge, "col", -1)
    return top, bottom, left, right


def per_device(
    scans, dest, offsets, profile_index, profiles, embed_weight, attn_gain, qkv_weight, out_weight
):
    place = jnp.stack(
        [
            lax.axis_index("row") * TOK_H,
            lax.axis_index("col") * TOK_W,
            jnp.asarray(lax.axis_size("row") * TOK_H, i32),
            jnp.asarray(lax.axis_size("col") * TOK_W, i32),
        ]
    ).astype(i32)
    embed = embed_weight.reshape(CH, 8, 8, MODEL).transpose(1, 0, 2, 3).reshape(PATCH, MODEL)
    payload = pack(dest, offsets, profile_index, profiles, scans)
    payload = lax.all_to_all(payload, ("row", "col"), split_axis=0, concat_axis=0, tiled=True)
    payload, place = lax.optimization_barrier((payload, place))
    x, first, last, embed, w = merge(payload, profiles, embed, qkv_weight)
    halos = around(x, first, last)
    stream, qkv = own_part(x, embed, attn_gain, w)
    tokens = rest(place, halos, stream, qkv, attn_gain, embed, w, qkv_weight, out_weight)
    return tokens.reshape(TOK_H, TOK_W, MODEL)


def solution(mesh):
    placed = (
        P(("row", "col"), None, None, None),
        P(("row", "col"), None),
        P(("row", "col")),
        P(("row", "col")),
        P(),
        P(),
        P(),
        P(),
        P(),
    )
    return jax.shard_map(
        per_device, mesh=mesh, in_specs=placed, out_specs=P("row", "col", None), check_vma=False
    )
```

```python
import functools

import jax
import jax.numpy as jnp
from jax import lax
from jax.experimental import pallas as pl
from jax.experimental.pallas import tpu as pltpu
from jax.sharding import PartitionSpec as P

HEADS = 16
RADIUS = 4
TOK_H = 32
TOK_W = 16
BR = 4
CH = 8
MODEL = 1024
PATCH = 512
GRP = 128
MID = 160
WIDE = 192
HALO = 32
EDGE = 4 * HALO
META = 128
CHUNKS = 4
VMEM_BYTES = 20 * 1024 * 1024
LARGE_BYTES = 30 * 1024 * 1024

f32 = jnp.float32
bf16 = jnp.bfloat16
i32 = jnp.int32


def dot(a, b):
    return lax.dot_general(a, b, (((1,), (0,)), ((), ())), preferred_element_type=f32)


def dot_nt(a, b):
    return lax.dot_general(a, b, (((1,), (1,)), ((), ())), preferred_element_type=f32)


def iota(shape, dim):
    return lax.broadcasted_iota(i32, shape, dim)


def onehot(cond):
    return jnp.where(cond, 1.0, 0.0).astype(bf16)


def halves(x):
    high = x.astype(bf16)
    return high, (x - high.astype(f32)).astype(bf16)


def pack_kernel(
    dest_hbm, offs_hbm, pidx_hbm, prof_hbm, scans_hbm, out_ref,
    dest_ref, offs_ref, pidx_ref, prof_ref, scans_ref, w_ref, sem,
):
    count = dest_ref.shape[1]
    chunk = scans_ref.shape[0] // CHUNKS
    small = [
        pltpu.make_async_copy(a, b, sem.at[n])
        for n, (a, b) in enumerate(
            [(dest_hbm, dest_ref), (offs_hbm, offs_ref), (pidx_hbm, pidx_ref), (prof_hbm, prof_ref)]
        )
    ]
    large = [
        pltpu.make_async_copy(
            scans_hbm.at[pl.ds(n * chunk, chunk)], scans_ref.at[pl.ds(n * chunk, chunk)], sem.at[4 + n]
        )
        for n in range(CHUNKS)
    ]
    for copy in small + large:
        copy.start()
    for copy in small:
        copy.wait()
    eye = iota((count, count), 0) == iota((count, count), 1)
    dest_row = dest_ref[...].astype(f32)
    dest_col = jnp.sum(jnp.where(eye, dest_row, 0.0), axis=1, keepdims=True)
    before = iota((count, count), 0) < iota((count, count), 1)
    same = (dest_col == dest_row) & before
    rank = jnp.sum(jnp.where(same, 1.0, 0.0), axis=0, keepdims=True)
    slot = dest_row * (2.0 * BR) + rank * float(BR)
    offs_col = jnp.sum(jnp.where(eye, offs_ref[...].astype(f32), 0.0), axis=1, keepdims=True)
    pidx_col = jnp.sum(jnp.where(eye, pidx_ref[...].astype(f32), 0.0), axis=1, keepdims=True)
    chosen = onehot(pidx_col == iota((count, prof_ref.shape[0]), 1).astype(f32))
    lane = iota((count, META), 1)
    meta = jnp.where(lane == 0, offs_col, jnp.where(lane == 1, pidx_col, 1.0)).astype(bf16)
    weights = []
    for k in range(BR):
        high, low = halves(prof_ref[:, k, :])
        weights.append(dot(chosen, high) + dot(chosen, low))
        w_ref[k * count : (k + 1) * count, CH * 128 :] = meta
    some = count // CHUNKS
    for n in range(CHUNKS):
        large[n].wait()
        for k in range(BR):
            for c in range(CH):
                block = scans_ref[pl.ds(n * chunk + k * CH + c, some, stride=BR * CH), :]
                at = k * count + n * some
                w_ref[at : at + some, c * 128 : (c + 1) * 128] = (
                    block * weights[k][n * some : (n + 1) * some, :]
                ).astype(bf16)
    rows = out_ref.shape[0]
    slots = jnp.concatenate([slot + float(k) for k in range(BR)], axis=1)
    step = 256
    for r in range(0, rows, step):
        here = (iota((step, BR * count), 0) + r).astype(f32)
        placing = onehot(here == slots)
        out_ref[r : r + step, :] = dot(placing, w_ref[...]).astype(bf16)


def pack(dest, offsets, profile_index, profiles, scans):
    count = scans.shape[0]
    rows = count * 2 * BR
    return pl.pallas_call(
        pack_kernel,
        out_shape=jax.ShapeDtypeStruct((rows, CH * 128 + META), bf16),
        in_specs=[pl.BlockSpec(memory_space=pltpu.HBM)] * 5,
        scratch_shapes=[
            pltpu.VMEM((1, count), i32),
            pltpu.VMEM((1, count), i32),
            pltpu.VMEM((1, count), i32),
            pltpu.VMEM(profiles.shape, f32),
            pltpu.VMEM((count * BR * CH, 128), f32),
            pltpu.VMEM((BR * count, CH * 128 + META), bf16),
            pltpu.SemaphoreType.DMA((4 + CHUNKS,)),
        ],
        compiler_params=pltpu.CompilerParams(vmem_limit_bytes=VMEM_BYTES),
        name="pack",
    )(
        in_hbm(dest.reshape(1, count)),
        in_hbm(offsets.reshape(1, count)),
        in_hbm(profile_index.reshape(1, count)),
        in_hbm(profiles),
        in_hbm(scans.reshape(count * BR * CH, 128)),
    )


def in_hbm(x):
    return pltpu.with_memory_space_constraint(x, pltpu.HBM)


def in_vmem(x):
    return pltpu.with_memory_space_constraint(x, pltpu.VMEM)


def merge_kernel(
    pay_ref, prof_ref, embed_hbm, w_hbm, x_ref, top_ref, bot_ref, embed_ref, w_ref,
    mg_ref, y_ref, xg_ref, sem,
):
    rows = pay_ref.shape[0]
    copies = [
        pltpu.make_async_copy(embed_hbm, embed_ref, sem.at[0]),
        pltpu.make_async_copy(w_hbm.at[0], w_ref, sem.at[1]),
    ]
    for copy in copies:
        copy.start()
    pick = onehot(iota((8, META), 0) == iota((8, META), 1))
    fields = dot_nt(pick, pay_ref[:, CH * 128 :])
    offs = fields[0:1, :]
    pidx = fields[1:2, :]
    valid = fields[2:3, :]
    strip = (iota((1, rows), 1) % BR).astype(f32)
    land = jnp.where(valid > 0.5, offs + strip, 4096.0)
    kind = pidx + 16.0 * strip
    r = iota((TOK_H * 8, rows), 0)
    pixel = (r % TOK_H) * 8 + r // TOK_H
    placing = onehot(pixel.astype(f32) == land)
    kinds = onehot(iota((16 * BR, rows), 0).astype(f32) == kind)
    counts = dot_nt(placing, kinds).astype(bf16)
    table = jnp.concatenate([prof_ref[:, k, :] for k in range(BR)], axis=0)
    high, low = halves(table)
    scale = 1.0 / (1.0 + dot(counts, high) + dot(counts, low))
    for c in range(CH):
        part = dot(placing, pay_ref[:, c * 128 : (c + 1) * 128])
        mg_ref[:, c * 128 : (c + 1) * 128] = (part * scale).astype(bf16)
    width = CH * 128
    step = 256
    for n in range(0, width, step):
        source = iota((width, step), 0)
        to = iota((width, step), 1) + n
        wanted = (to // 8 % CH) * 128 + (to // 64) * 8 + to % 8
        y_ref[:, n : n + step] = dot(mg_ref[...], onehot(source == wanted))
    low_half = iota((TOK_H, 128), 1) < 64
    order = iota((GRP, GRP), 1)
    want = iota((GRP, GRP), 0)
    reorder = onehot(order == (want % 4) * TOK_H + want // 4)
    for g in range(4):
        for jj in range(4):
            j = 4 * g + jj
            tile = (j // 2) * 128
            for pp in range(4):
                a = y_ref[2 * pp * TOK_H : (2 * pp + 1) * TOK_H, tile : tile + 128]
                b = y_ref[(2 * pp + 1) * TOK_H : (2 * pp + 2) * TOK_H, tile : tile + 128]
                if j % 2 == 0:
                    piece = jnp.where(low_half, a, pltpu.roll(b, 64, 1))
                else:
                    piece = jnp.where(low_half, pltpu.roll(a, 64, 1), b)
                xg_ref[jj * TOK_H : (jj + 1) * TOK_H, pp * 128 : (pp + 1) * 128] = piece.astype(
                    bf16
                )
        tokens = dot(reorder, xg_ref[...]).astype(bf16)
        x_ref[g * GRP : (g + 1) * GRP, :] = tokens
        top_ref[g * HALO : (g + 1) * HALO, :] = tokens[:HALO, :]
        bot_ref[g * HALO : (g + 1) * HALO, :] = tokens[GRP - HALO :, :]
    for copy in copies:
        copy.wait()


def merge(payload, profiles, embed, qkv_weight):
    vmem = pl.BlockSpec(memory_space=pltpu.VMEM)
    hbm = pl.BlockSpec(memory_space=pltpu.HBM)
    return pl.pallas_call(
        merge_kernel,
        out_shape=[
            jax.ShapeDtypeStruct((4 * GRP, PATCH), bf16),
            jax.ShapeDtypeStruct((EDGE, PATCH), bf16),
            jax.ShapeDtypeStruct((EDGE, PATCH), bf16),
            pltpu.VMEM((PATCH, MODEL), bf16),
            pltpu.VMEM((MODEL, 3 * MODEL), bf16),
        ],
        in_specs=[vmem, vmem, hbm, hbm],
        scratch_shapes=[
            pltpu.VMEM((TOK_H * 8, CH * 128), bf16),
            pltpu.VMEM((TOK_H * 8, CH * 128), f32),
            pltpu.VMEM((GRP, PATCH), bf16),
            pltpu.SemaphoreType.DMA((2,)),
        ],
        compiler_params=pltpu.CompilerParams(vmem_limit_bytes=VMEM_BYTES),
        name="merge",
    )(payload, profiles, in_hbm(embed), in_hbm(qkv_weight))


def normed(stream, gain):
    centre = jnp.mean(stream, -1, keepdims=True)
    moved = stream - centre
    spread = jnp.mean(jnp.square(moved), -1, keepdims=True)
    return (moved * lax.rsqrt(spread + 1e-05) * gain).astype(bf16)


def own_kernel(
    place_ref, x_ref, top_ref, bot_ref, embed_ref, gain_ref, w_ref,
    stream_ref, q_ref, kv_ref, att_ref, inp_ref,
):
    for g in range(4):
        edge = slice(g * HALO, (g + 1) * HALO)
        tokens = jnp.concatenate(
            [top_ref[edge, :], x_ref[g * GRP : (g + 1) * GRP, :], bot_ref[edge, :]], axis=0
        )
        stream = dot(tokens, embed_ref[...])
        rows = slice(g * WIDE, (g + 1) * WIDE)
        stream_ref[rows, :] = stream
        inp_ref[rows, :] = normed(stream, gain_ref[0:1, :])
    project(inp_ref[...], inp_ref[...], w_ref, q_ref, kv_ref)
    attention(
        [1],
        5,
        lambda g: (q_ref, (g - 1) * WIDE + 16),
        lambda g: (kv_ref, (g - 2) * WIDE),
        lambda g: (att_ref, (g - 2) * MID),
        place_ref[0] - 8,
        place_ref[1] - 8,
        (place_ref[2], place_ref[3]),
    )


def project(query_inputs, inputs, w_ref, q_ref, kv_ref):
    step = 256
    for m in range(0, MODEL, step):
        part = dot(query_inputs, w_ref[:, m : m + step]).astype(bf16)
        q_ref[: part.shape[0], m : m + step] = part * jnp.asarray(0.125, bf16)
    for m in range(0, 2 * MODEL, step):
        part = dot(inputs, w_ref[:, MODEL + m : MODEL + m + step]).astype(bf16)
        kv_ref[: part.shape[0], m : m + step] = part


def own_part(place, x, top, bottom, embed, gain, w):
    vmem = pl.BlockSpec(memory_space=pltpu.VMEM)
    smem = pl.BlockSpec(memory_space=pltpu.SMEM)
    return pl.pallas_call(
        own_kernel,
        out_shape=[
            jax.ShapeDtypeStruct((4 * WIDE, MODEL), f32),
            jax.ShapeDtypeStruct((4 * WIDE, MODEL), bf16),
            jax.ShapeDtypeStruct((4 * WIDE, 2 * MODEL), bf16),
            jax.ShapeDtypeStruct((2 * MID, MODEL), bf16),
        ],
        in_specs=[smem] + [vmem] * 6,
        scratch_shapes=[pltpu.VMEM((4 * WIDE, MODEL), bf16)],
        compiler_params=pltpu.CompilerParams(vmem_limit_bytes=VMEM_BYTES),
        cost_estimate=pl.CostEstimate(
            flops=2 * 4 * WIDE * MODEL * 3 * MODEL, bytes_accessed=12 << 20, transcendentals=0
        ),
        name="own",
    )(place, x, top, bottom, in_vmem(embed), gain, in_vmem(w))


def attention(broad, tall, q_of, kv_of, a_of, row, col, ends):
    query = iota((64, 256), 0)
    key = iota((64, 256), 1)
    row_gap = (key % 64) // 4 - 4 - (query % 32) // 4
    col_gap = (key // 64 - 1) * 4 + key % 4 - (query // 32) * 4 - query % 4
    near = (jnp.abs(row_gap) <= RADIUS) & (jnp.abs(col_gap) <= RADIUS)
    near_bias = jnp.where(near, 0.0, -1e30)
    lane_key = iota((1, 256), 1)
    key_row = (lane_key % 64) // 4 + row
    key_col = (lane_key // 64) * 4 + lane_key % 4 + col
    low_half = iota((64, 128), 1) < 64
    zero = jnp.zeros((64, 128), bf16)
    ones = jnp.ones((256, 128), bf16)

    for bi in range(tall):
        at_row = key_row + bi * 8
        row_inside = (at_row >= 0) & (at_row < ends[0])
        for bj in broad:
            at_col = key_col + bj * 8
            inside = row_inside & (at_col >= 0) & (at_col < ends[1])
            bias = near_bias + jnp.where(inside, 0.0, -1e30)
            bias = jnp.concatenate([bias, bias], axis=0)
            q_from = [q_of(2 * bj + g) for g in range(2)]
            k_from = [kv_of(2 * bj + g) for g in range(4)]
            a_to = [a_of(2 * bj + g) for g in range(2)]
            at = bi * 32
            for h in range(HEADS // 2):
                lanes = slice(h * 128, (h + 1) * 128)
                q = jnp.concatenate([r[b + at : b + at + 32, lanes] for r, b in q_from], axis=0)
                q = jnp.concatenate(
                    [jnp.where(low_half, q, zero), jnp.where(low_half, zero, q)], axis=0
                )
                k = jnp.concatenate([r[b + at : b + at + 64, lanes] for r, b in k_from], axis=0)
                v_lanes = slice(MODEL + h * 128, MODEL + (h + 1) * 128)
                v = jnp.concatenate([r[b + at : b + at + 64, v_lanes] for r, b in k_from], axis=0)
                logits = dot_nt(q, k) + bias
                top = jnp.max(logits, axis=-1, keepdims=True)
                share = jnp.exp(logits - top).astype(bf16)
                both = dot(share, jnp.concatenate([v, ones], axis=1))
                mixed = jnp.where(low_half, both[:64, :128], both[64:, :128])
                total = jnp.where(low_half, both[:64, 128:], both[64:, 128:])
                picked = (mixed / total).astype(bf16)
                for g, (r, b) in enumerate(a_to):
                    r[b + at : b + at + 32, lanes] = picked[g * 32 : (g + 1) * 32, :]


def rest_kernel(
    place_ref, left_ref, right_ref, stream_ref, oq_ref, okv_ref, oatt_ref, gain_ref, embed_ref,
    w_ref, w_hbm, o_hbm, out_ref,
    next_ref, o_ref, side_ref, sq_ref, skv_ref, q_ref, kv_ref, mid_ref, att_ref, inp_ref, sem,
):
    copies = [
        pltpu.make_async_copy(o_hbm.at[0], o_ref.at[0], sem.at[0]),
        pltpu.make_async_copy(w_hbm.at[1], next_ref, sem.at[1]),
        pltpu.make_async_copy(o_hbm.at[1], o_ref.at[1], sem.at[2]),
    ]
    for copy in copies:
        copy.start()

    for n in range(4):
        ref, g = (left_ref, right_ref)[n // 2], n % 2
        below = 2 * HALO + 2 * GRP
        tokens = jnp.concatenate(
            [
                ref[g * HALO : (g + 1) * HALO, :],
                ref[2 * HALO + g * GRP : 2 * HALO + (g + 1) * GRP, :],
                ref[below + g * HALO : below + (g + 1) * HALO, :],
            ],
            axis=0,
        )
        stream = dot(tokens, embed_ref[...])
        inp_ref[n * WIDE : (n + 1) * WIDE, :] = normed(stream, gain_ref[0:1, :])
        if n in (1, 2):
            side_ref[(n - 1) * WIDE : n * WIDE, :] = stream
    project(inp_ref[WIDE : 3 * WIDE, :], inp_ref[: 4 * WIDE, :], w_ref, sq_ref, skv_ref)

    def q_of(g):
        if g in (0, 5):
            return sq_ref, (g // 5) * WIDE + 16
        return oq_ref, (g - 1) * WIDE + 16

    def kv_of(g):
        if g in (0, 1, 6, 7):
            return skv_ref, (g if g < 2 else g - 4) * WIDE
        return okv_ref, (g - 2) * WIDE

    ends = (place_ref[2], place_ref[3])
    attention(
        [0, 2], 5, q_of, kv_of, lambda g: (att_ref, g * MID), place_ref[0] - 8, place_ref[1] - 8, ends
    )
    copies[0].wait()
    for g in range(6):
        rows = slice(g * MID, (g + 1) * MID)
        if g in (0, 5):
            before = side_ref[(g // 5) * WIDE + 16 : (g // 5) * WIDE + 16 + MID, :]
        else:
            before = stream_ref[(g - 1) * WIDE + 16 : (g - 1) * WIDE + 16 + MID, :]
        mixed = oatt_ref[(g - 2) * MID : (g - 1) * MID, :] if g in (2, 3) else att_ref[rows, :]
        stream = before + dot(mixed, o_ref[0])
        if g not in (0, 5):
            mid_ref[(g - 1) * GRP : g * GRP, :] = stream[16 : 16 + GRP, :]
        inp_ref[rows, :] = normed(stream, gain_ref[1:2, :])

    copies[1].wait()
    project(inp_ref[MID : 5 * MID, :], inp_ref[...], next_ref, q_ref, kv_ref)
    attention(
        [0, 1],
        4,
        lambda g: (q_ref, g * MID + 16),
        lambda g: (kv_ref, g * MID),
        lambda g: (att_ref, g * GRP),
        place_ref[0] - 4,
        place_ref[1] - 4,
        ends,
    )
    copies[2].wait()
    for g in range(4):
        rows = slice(g * GRP, (g + 1) * GRP)
        stream = mid_ref[rows, :] + dot(att_ref[rows, :], o_ref[1])
        inp_ref[rows, :] = stream.astype(bf16)
    for r in range(0, 4 * GRP, GRP):
        to = iota((GRP, 4 * GRP), 0) + r
        source = iota((GRP, 4 * GRP), 1)
        wanted = (to // 4 % 4) * GRP + (to // 16) * 4 + to % 4
        out_ref[r : r + GRP, :] = dot(onehot(source == wanted), inp_ref[: 4 * GRP, :]).astype(bf16)


def rest(place, left, right, own, gain, embed, w, qkv_weight, out_weight):
    hbm = pl.BlockSpec(memory_space=pltpu.HBM)
    vmem = pl.BlockSpec(memory_space=pltpu.VMEM)
    smem = pl.BlockSpec(memory_space=pltpu.SMEM)
    return pl.pallas_call(
        rest_kernel,
        out_shape=jax.ShapeDtypeStruct((4 * GRP, MODEL), bf16),
        in_specs=[smem] + [vmem] * 9 + [hbm] * 2,
        scratch_shapes=[
            pltpu.VMEM((MODEL, 3 * MODEL), bf16),
            pltpu.VMEM((2, MODEL, MODEL), bf16),
            pltpu.VMEM((2 * WIDE, MODEL), f32),
            pltpu.VMEM((2 * WIDE, MODEL), bf16),
            pltpu.VMEM((4 * WIDE, 2 * MODEL), bf16),
            pltpu.VMEM((4 * MID, MODEL), bf16),
            pltpu.VMEM((6 * MID, 2 * MODEL), bf16),
            pltpu.VMEM((4 * GRP, MODEL), f32),
            pltpu.VMEM((6 * MID, MODEL), bf16),
            pltpu.VMEM((6 * MID, MODEL), bf16),
            pltpu.SemaphoreType.DMA((3,)),
        ],
        compiler_params=pltpu.CompilerParams(vmem_limit_bytes=LARGE_BYTES),
        name="rest",
    )(
        place, left, right, *own, gain, in_vmem(embed), in_vmem(w),
        in_hbm(qkv_weight), in_hbm(out_weight),
    )


def shifted(cells, axis, by):
    count = lax.axis_size(axis)
    return lax.ppermute(cells, axis, [(i, (i + by) % count) for i in range(count)])


def around(x, first, last):
    top = shifted(last, "row", 1)
    bottom = shifted(first, "row", -1)
    two = 2 * HALO
    right_edge = jnp.concatenate([top[two:], x[2 * GRP :], bottom[two:]], axis=0)
    left_edge = jnp.concatenate([top[:two], x[: 2 * GRP], bottom[:two]], axis=0)
    left = shifted(right_edge, "col", 1)
    right = shifted(left_edge, "col", -1)
    return top, bottom, left, right


def per_device(
    scans, dest, offsets, profile_index, profiles, embed_weight, attn_gain, qkv_weight, out_weight
):
    place = jnp.stack(
        [
            lax.axis_index("row") * TOK_H,
            lax.axis_index("col") * TOK_W,
            jnp.asarray(lax.axis_size("row") * TOK_H, i32),
            jnp.asarray(lax.axis_size("col") * TOK_W, i32),
        ]
    ).astype(i32)
    embed = embed_weight.reshape(CH, 8, 8, MODEL).transpose(1, 0, 2, 3).reshape(PATCH, MODEL)
    payload = pack(dest, offsets, profile_index, profiles, scans)
    payload = lax.all_to_all(payload, ("row", "col"), split_axis=0, concat_axis=0, tiled=True)
    payload, place = lax.optimization_barrier((payload, place))
    x, first, last, embed, w = merge(payload, profiles, embed, qkv_weight)
    top, bottom, left, right = around(x, first, last)
    own = own_part(place, x, top, bottom, embed, attn_gain, w)
    tokens = rest(place, left, right, own, attn_gain, embed, w, qkv_weight, out_weight)
    return tokens.reshape(TOK_H, TOK_W, MODEL)


def solution(mesh):
    placed = (
        P(("row", "col"), None, None, None),
        P(("row", "col"), None),
        P(("row", "col")),
        P(("row", "col")),
        P(),
        P(),
        P(),
        P(),
        P(),
    )
    return jax.shard_map(
        per_device, mesh=mesh, in_specs=placed, out_specs=P("row", "col", None), check_vma=False
    )
```

```python
import functools

import jax
import jax.numpy as jnp
from jax import lax
from jax.experimental import pallas as pl
from jax.experimental.pallas import tpu as pltpu
from jax.sharding import PartitionSpec as P

HEADS = 16
RADIUS = 4
TOK_H = 32
TOK_W = 16
BR = 4
CH = 8
MODEL = 1024
PATCH = 512
GRP = 128
MID = 160
WIDE = 192
HALO = 32
EDGE = 4 * HALO
META = 128
CHUNKS = 4
VMEM_BYTES = 20 * 1024 * 1024
LARGE_BYTES = 30 * 1024 * 1024

f32 = jnp.float32
bf16 = jnp.bfloat16
i32 = jnp.int32


def dot(a, b):
    return lax.dot_general(a, b, (((1,), (0,)), ((), ())), preferred_element_type=f32)


def dot_nt(a, b):
    return lax.dot_general(a, b, (((1,), (1,)), ((), ())), preferred_element_type=f32)


def iota(shape, dim):
    return lax.broadcasted_iota(i32, shape, dim)


def onehot(cond):
    return jnp.where(cond, 1.0, 0.0).astype(bf16)


def halves(x):
    high = x.astype(bf16)
    return high, (x - high.astype(f32)).astype(bf16)


def pack_kernel(
    dest_hbm, offs_hbm, pidx_hbm, prof_hbm, scans_hbm, out_hbm,
    dest_ref, offs_ref, pidx_ref, prof_ref, scans_ref, w_ref, packed_ref, sem, out_sem,
):
    count = dest_ref.shape[1]
    chunk = scans_ref.shape[0] // CHUNKS
    small = [
        pltpu.make_async_copy(a, b, sem.at[n])
        for n, (a, b) in enumerate(
            [(dest_hbm, dest_ref), (offs_hbm, offs_ref), (pidx_hbm, pidx_ref), (prof_hbm, prof_ref)]
        )
    ]
    large = [
        pltpu.make_async_copy(
            scans_hbm.at[pl.ds(n * chunk, chunk)], scans_ref.at[pl.ds(n * chunk, chunk)], sem.at[4 + n]
        )
        for n in range(CHUNKS)
    ]
    for copy in small + large:
        copy.start()
    for copy in small:
        copy.wait()
    eye = iota((count, count), 0) == iota((count, count), 1)
    dest_row = dest_ref[...].astype(f32)
    dest_col = jnp.sum(jnp.where(eye, dest_row, 0.0), axis=1, keepdims=True)
    before = iota((count, count), 0) < iota((count, count), 1)
    same = (dest_col == dest_row) & before
    rank = jnp.sum(jnp.where(same, 1.0, 0.0), axis=0, keepdims=True)
    slot = dest_row * (2.0 * BR) + rank * float(BR)
    offs_col = jnp.sum(jnp.where(eye, offs_ref[...].astype(f32), 0.0), axis=1, keepdims=True)
    pidx_col = jnp.sum(jnp.where(eye, pidx_ref[...].astype(f32), 0.0), axis=1, keepdims=True)
    chosen = onehot(pidx_col == iota((count, prof_ref.shape[0]), 1).astype(f32))
    lane = iota((count, META), 1)
    meta = jnp.where(lane == 0, offs_col, jnp.where(lane == 1, pidx_col, 1.0)).astype(bf16)
    weights = []
    for k in range(BR):
        high, low = halves(prof_ref[:, k, :])
        weights.append(dot(chosen, high) + dot(chosen, low))
        w_ref[k * count : (k + 1) * count, CH * 128 :] = meta
    some = count // CHUNKS
    for n in range(CHUNKS):
        large[n].wait()
        for k in range(BR):
            for c in range(CH):
                block = scans_ref[pl.ds(n * chunk + k * CH + c, some, stride=BR * CH), :]
                at = k * count + n * some
                w_ref[at : at + some, c * 128 : (c + 1) * 128] = (
                    block * weights[k][n * some : (n + 1) * some, :]
                ).astype(bf16)
    slots = jnp.concatenate([slot + float(k) for k in range(BR)], axis=1)
    step = packed_ref.shape[0] // CHUNKS
    outs = []
    for n in range(CHUNKS):
        here = (iota((step, BR * count), 0) + n * step).astype(f32)
        rows = pl.ds(n * step, step)
        packed_ref[rows, :] = dot(onehot(here == slots), w_ref[...]).astype(bf16)
        outs.append(
            pltpu.make_async_copy(packed_ref.at[rows, :], out_hbm.at[rows, :], out_sem.at[n])
        )
        outs[-1].start()
    for copy in outs:
        copy.wait()


def pack(dest, offsets, profile_index, profiles, scans):
    count = scans.shape[0]
    rows = count * 2 * BR
    return pl.pallas_call(
        pack_kernel,
        out_shape=jax.ShapeDtypeStruct((rows, CH * 128 + META), bf16),
        in_specs=[pl.BlockSpec(memory_space=pltpu.HBM)] * 5,
        out_specs=pl.BlockSpec(memory_space=pltpu.HBM),
        scratch_shapes=[
            pltpu.VMEM((1, count), i32),
            pltpu.VMEM((1, count), i32),
            pltpu.VMEM((1, count), i32),
            pltpu.VMEM(profiles.shape, f32),
            pltpu.VMEM((count * BR * CH, 128), f32),
            pltpu.VMEM((BR * count, CH * 128 + META), bf16),
            pltpu.VMEM((rows, CH * 128 + META), bf16),
            pltpu.SemaphoreType.DMA((4 + CHUNKS,)),
            pltpu.SemaphoreType.DMA((CHUNKS,)),
        ],
        compiler_params=pltpu.CompilerParams(vmem_limit_bytes=VMEM_BYTES),
        name="pack",
    )(
        in_hbm(dest.reshape(1, count)),
        in_hbm(offsets.reshape(1, count)),
        in_hbm(profile_index.reshape(1, count)),
        in_hbm(profiles),
        in_hbm(scans.reshape(count * BR * CH, 128)),
    )


def in_hbm(x):
    return pltpu.with_memory_space_constraint(x, pltpu.HBM)


def in_vmem(x):
    return pltpu.with_memory_space_constraint(x, pltpu.VMEM)


def merge_kernel(
    pay_ref, prof_ref, embed_hbm, w_hbm, x_ref, top_ref, bot_ref, embed_ref, w_ref,
    mg_ref, y_ref, xg_ref, sem,
):
    rows = pay_ref.shape[0]
    copies = [
        pltpu.make_async_copy(embed_hbm, embed_ref, sem.at[0]),
        pltpu.make_async_copy(w_hbm.at[0], w_ref, sem.at[1]),
    ]
    for copy in copies:
        copy.start()
    pick = onehot(iota((8, META), 0) == iota((8, META), 1))
    fields = dot_nt(pick, pay_ref[:, CH * 128 :])
    offs = fields[0:1, :]
    pidx = fields[1:2, :]
    valid = fields[2:3, :]
    strip = (iota((1, rows), 1) % BR).astype(f32)
    land = jnp.where(valid > 0.5, offs + strip, 4096.0)
    kind = pidx + 16.0 * strip
    r = iota((TOK_H * 8, rows), 0)
    pixel = (r % TOK_H) * 8 + r // TOK_H
    placing = onehot(pixel.astype(f32) == land)
    kinds = onehot(iota((16 * BR, rows), 0).astype(f32) == kind)
    counts = dot_nt(placing, kinds).astype(bf16)
    table = jnp.concatenate([prof_ref[:, k, :] for k in range(BR)], axis=0)
    high, low = halves(table)
    scale = 1.0 / (1.0 + dot(counts, high) + dot(counts, low))
    for c in range(CH):
        part = dot(placing, pay_ref[:, c * 128 : (c + 1) * 128])
        mg_ref[:, c * 128 : (c + 1) * 128] = (part * scale).astype(bf16)
    width = CH * 128
    step = 256
    for n in range(0, width, step):
        source = iota((width, step), 0)
        to = iota((width, step), 1) + n
        wanted = (to // 8 % CH) * 128 + (to // 64) * 8 + to % 8
        y_ref[:, n : n + step] = dot(mg_ref[...], onehot(source == wanted))
    low_half = iota((TOK_H, 128), 1) < 64
    order = iota((GRP, GRP), 1)
    want = iota((GRP, GRP), 0)
    reorder = onehot(order == (want % 4) * TOK_H + want // 4)
    for g in range(4):
        for jj in range(4):
            j = 4 * g + jj
            tile = (j // 2) * 128
            for pp in range(4):
                a = y_ref[2 * pp * TOK_H : (2 * pp + 1) * TOK_H, tile : tile + 128]
                b = y_ref[(2 * pp + 1) * TOK_H : (2 * pp + 2) * TOK_H, tile : tile + 128]
                if j % 2 == 0:
                    piece = jnp.where(low_half, a, pltpu.roll(b, 64, 1))
                else:
                    piece = jnp.where(low_half, pltpu.roll(a, 64, 1), b)
                xg_ref[jj * TOK_H : (jj + 1) * TOK_H, pp * 128 : (pp + 1) * 128] = piece.astype(
                    bf16
                )
        tokens = dot(reorder, xg_ref[...]).astype(bf16)
        x_ref[g * GRP : (g + 1) * GRP, :] = tokens
        top_ref[g * HALO : (g + 1) * HALO, :] = tokens[:HALO, :]
        bot_ref[g * HALO : (g + 1) * HALO, :] = tokens[GRP - HALO :, :]
    for copy in copies:
        copy.wait()


def merge(payload, profiles, embed, qkv_weight):
    vmem = pl.BlockSpec(memory_space=pltpu.VMEM)
    hbm = pl.BlockSpec(memory_space=pltpu.HBM)
    return pl.pallas_call(
        merge_kernel,
        out_shape=[
            jax.ShapeDtypeStruct((4 * GRP, PATCH), bf16),
            jax.ShapeDtypeStruct((EDGE, PATCH), bf16),
            jax.ShapeDtypeStruct((EDGE, PATCH), bf16),
            pltpu.VMEM((PATCH, MODEL), bf16),
            pltpu.VMEM((MODEL, 3 * MODEL), bf16),
        ],
        in_specs=[vmem, vmem, hbm, hbm],
        scratch_shapes=[
            pltpu.VMEM((TOK_H * 8, CH * 128), bf16),
            pltpu.VMEM((TOK_H * 8, CH * 128), f32),
            pltpu.VMEM((GRP, PATCH), bf16),
            pltpu.SemaphoreType.DMA((2,)),
        ],
        compiler_params=pltpu.CompilerParams(vmem_limit_bytes=VMEM_BYTES),
        name="merge",
    )(payload, profiles, in_hbm(embed), in_hbm(qkv_weight))


def normed(stream, gain):
    centre = jnp.mean(stream, -1, keepdims=True)
    moved = stream - centre
    spread = jnp.mean(jnp.square(moved), -1, keepdims=True)
    return (moved * lax.rsqrt(spread + 1e-05) * gain).astype(bf16)


def own_kernel(
    place_ref, x_ref, top_ref, bot_ref, embed_ref, gain_ref, w_ref,
    stream_ref, q_ref, kv_ref, att_ref, inp_ref,
):
    for g in range(4):
        edge = slice(g * HALO, (g + 1) * HALO)
        tokens = jnp.concatenate(
            [top_ref[edge, :], x_ref[g * GRP : (g + 1) * GRP, :], bot_ref[edge, :]], axis=0
        )
        stream = dot(tokens, embed_ref[...])
        rows = slice(g * WIDE, (g + 1) * WIDE)
        stream_ref[rows, :] = stream
        inp_ref[rows, :] = normed(stream, gain_ref[0:1, :])
    project(inp_ref[...], inp_ref[...], w_ref, q_ref, kv_ref)
    attention(
        [1],
        5,
        lambda g: (q_ref, (g - 1) * WIDE + 16),
        lambda g: (kv_ref, (g - 2) * WIDE),
        lambda g: (att_ref, (g - 2) * MID),
        place_ref[0] - 8,
        place_ref[1] - 8,
        (place_ref[2], place_ref[3]),
    )


def project(query_inputs, inputs, w_ref, q_ref, kv_ref):
    step = 256
    for m in range(0, MODEL, step):
        part = dot(query_inputs, w_ref[:, m : m + step]).astype(bf16)
        q_ref[: part.shape[0], m : m + step] = part * jnp.asarray(0.125, bf16)
    for m in range(0, 2 * MODEL, step):
        part = dot(inputs, w_ref[:, MODEL + m : MODEL + m + step]).astype(bf16)
        kv_ref[: part.shape[0], m : m + step] = part


def own_part(place, x, top, bottom, embed, gain, w):
    vmem = pl.BlockSpec(memory_space=pltpu.VMEM)
    smem = pl.BlockSpec(memory_space=pltpu.SMEM)
    return pl.pallas_call(
        own_kernel,
        out_shape=[
            jax.ShapeDtypeStruct((4 * WIDE, MODEL), f32),
            jax.ShapeDtypeStruct((4 * WIDE, MODEL), bf16),
            jax.ShapeDtypeStruct((4 * WIDE, 2 * MODEL), bf16),
            jax.ShapeDtypeStruct((2 * MID, MODEL), bf16),
        ],
        in_specs=[smem] + [vmem] * 6,
        scratch_shapes=[pltpu.VMEM((4 * WIDE, MODEL), bf16)],
        compiler_params=pltpu.CompilerParams(vmem_limit_bytes=VMEM_BYTES),
        cost_estimate=pl.CostEstimate(
            flops=2 * 4 * WIDE * MODEL * 3 * MODEL, bytes_accessed=12 << 20, transcendentals=0
        ),
        name="own",
    )(place, x, top, bottom, in_vmem(embed), gain, in_vmem(w))


def attention(broad, tall, q_of, kv_of, a_of, row, col, ends):
    query = iota((64, 256), 0)
    key = iota((64, 256), 1)
    row_gap = (key % 64) // 4 - 4 - (query % 32) // 4
    col_gap = (key // 64 - 1) * 4 + key % 4 - (query // 32) * 4 - query % 4
    near = (jnp.abs(row_gap) <= RADIUS) & (jnp.abs(col_gap) <= RADIUS)
    near_bias = jnp.where(near, 0.0, -1e30)
    lane_key = iota((1, 256), 1)
    key_row = (lane_key % 64) // 4 + row
    key_col = (lane_key // 64) * 4 + lane_key % 4 + col
    low_half = iota((64, 128), 1) < 64
    zero = jnp.zeros((64, 128), bf16)
    ones = jnp.ones((256, 128), bf16)

    for bi in range(tall):
        at_row = key_row + bi * 8
        row_inside = (at_row >= 0) & (at_row < ends[0])
        for bj in broad:
            at_col = key_col + bj * 8
            inside = row_inside & (at_col >= 0) & (at_col < ends[1])
            bias = near_bias + jnp.where(inside, 0.0, -1e30)
            bias = jnp.concatenate([bias, bias], axis=0)
            q_from = [q_of(2 * bj + g) for g in range(2)]
            k_from = [kv_of(2 * bj + g) for g in range(4)]
            a_to = [a_of(2 * bj + g) for g in range(2)]
            at = bi * 32
            for h in range(HEADS // 2):
                lanes = slice(h * 128, (h + 1) * 128)
                q = jnp.concatenate([r[b + at : b + at + 32, lanes] for r, b in q_from], axis=0)
                q = jnp.concatenate(
                    [jnp.where(low_half, q, zero), jnp.where(low_half, zero, q)], axis=0
                )
                k = jnp.concatenate([r[b + at : b + at + 64, lanes] for r, b in k_from], axis=0)
                v_lanes = slice(MODEL + h * 128, MODEL + (h + 1) * 128)
                v = jnp.concatenate([r[b + at : b + at + 64, v_lanes] for r, b in k_from], axis=0)
                logits = dot_nt(q, k) + bias
                top = jnp.max(logits, axis=-1, keepdims=True)
                share = jnp.exp(logits - top).astype(bf16)
                both = dot(share, jnp.concatenate([v, ones], axis=1))
                mixed = jnp.where(low_half, both[:64, :128], both[64:, :128])
                total = jnp.where(low_half, both[:64, 128:], both[64:, 128:])
                picked = (mixed / total).astype(bf16)
                for g, (r, b) in enumerate(a_to):
                    r[b + at : b + at + 32, lanes] = picked[g * 32 : (g + 1) * 32, :]


def rest_kernel(
    place_ref, right_ref, left_ref, stream_ref, oq_ref, okv_ref, oatt_ref, gain_ref, embed_ref,
    w_ref, w_hbm, o_hbm, out_ref,
    next_ref, o_ref, side_ref, sq_ref, skv_ref, q_ref, kv_ref, mid_ref, att_ref, inp_ref, sem,
):
    copies = [
        pltpu.make_async_copy(o_hbm.at[0], o_ref.at[0], sem.at[0]),
        pltpu.make_async_copy(w_hbm.at[1], next_ref, sem.at[1]),
        pltpu.make_async_copy(o_hbm.at[1], o_ref.at[1], sem.at[2]),
    ]
    for copy in copies:
        copy.start()

    for n in range(4):
        ref, g = (left_ref, right_ref)[n // 2], n % 2
        below = 2 * HALO + 2 * GRP
        tokens = jnp.concatenate(
            [
                ref[g * HALO : (g + 1) * HALO, :],
                ref[2 * HALO + g * GRP : 2 * HALO + (g + 1) * GRP, :],
                ref[below + g * HALO : below + (g + 1) * HALO, :],
            ],
            axis=0,
        )
        stream = dot(tokens, embed_ref[...])
        inp_ref[n * WIDE : (n + 1) * WIDE, :] = normed(stream, gain_ref[0:1, :])
        if n in (1, 2):
            side_ref[(n - 1) * WIDE : n * WIDE, :] = stream
    project(inp_ref[WIDE : 3 * WIDE, :], inp_ref[: 4 * WIDE, :], w_ref, sq_ref, skv_ref)

    def q_of(g):
        if g in (0, 5):
            return sq_ref, (g // 5) * WIDE + 16
        return oq_ref, (g - 1) * WIDE + 16

    def kv_of(g):
        if g in (0, 1, 6, 7):
            return skv_ref, (g if g < 2 else g - 4) * WIDE
        return okv_ref, (g - 2) * WIDE

    ends = (place_ref[2], place_ref[3])
    attention(
        [0, 2], 5, q_of, kv_of, lambda g: (att_ref, g * MID), place_ref[0] - 8, place_ref[1] - 8, ends
    )
    copies[0].wait()
    for g in range(6):
        rows = slice(g * MID, (g + 1) * MID)
        if g in (0, 5):
            before = side_ref[(g // 5) * WIDE + 16 : (g // 5) * WIDE + 16 + MID, :]
        else:
            before = stream_ref[(g - 1) * WIDE + 16 : (g - 1) * WIDE + 16 + MID, :]
        mixed = oatt_ref[(g - 2) * MID : (g - 1) * MID, :] if g in (2, 3) else att_ref[rows, :]
        stream = before + dot(mixed, o_ref[0])
        if g not in (0, 5):
            mid_ref[(g - 1) * GRP : g * GRP, :] = stream[16 : 16 + GRP, :]
        inp_ref[rows, :] = normed(stream, gain_ref[1:2, :])

    copies[1].wait()
    project(inp_ref[MID : 5 * MID, :], inp_ref[...], next_ref, q_ref, kv_ref)
    attention(
        [0, 1],
        4,
        lambda g: (q_ref, g * MID + 16),
        lambda g: (kv_ref, g * MID),
        lambda g: (att_ref, g * GRP),
        place_ref[0] - 4,
        place_ref[1] - 4,
        ends,
    )
    copies[2].wait()
    for g in range(4):
        rows = slice(g * GRP, (g + 1) * GRP)
        stream = mid_ref[rows, :] + dot(att_ref[rows, :], o_ref[1])
        inp_ref[rows, :] = stream.astype(bf16)
    for r in range(0, 4 * GRP, GRP):
        to = iota((GRP, 4 * GRP), 0) + r
        source = iota((GRP, 4 * GRP), 1)
        wanted = (to // 4 % 4) * GRP + (to // 16) * 4 + to % 4
        out_ref[r : r + GRP, :] = dot(onehot(source == wanted), inp_ref[: 4 * GRP, :]).astype(bf16)


def rest(place, left, right, own, gain, embed, w, qkv_weight, out_weight):
    hbm = pl.BlockSpec(memory_space=pltpu.HBM)
    vmem = pl.BlockSpec(memory_space=pltpu.VMEM)
    smem = pl.BlockSpec(memory_space=pltpu.SMEM)
    return pl.pallas_call(
        rest_kernel,
        out_shape=jax.ShapeDtypeStruct((4 * GRP, MODEL), bf16),
        in_specs=[smem] + [vmem] * 9 + [hbm] * 2,
        scratch_shapes=[
            pltpu.VMEM((MODEL, 3 * MODEL), bf16),
            pltpu.VMEM((2, MODEL, MODEL), bf16),
            pltpu.VMEM((2 * WIDE, MODEL), f32),
            pltpu.VMEM((2 * WIDE, MODEL), bf16),
            pltpu.VMEM((4 * WIDE, 2 * MODEL), bf16),
            pltpu.VMEM((4 * MID, MODEL), bf16),
            pltpu.VMEM((6 * MID, 2 * MODEL), bf16),
            pltpu.VMEM((4 * GRP, MODEL), f32),
            pltpu.VMEM((6 * MID, MODEL), bf16),
            pltpu.VMEM((6 * MID, MODEL), bf16),
            pltpu.SemaphoreType.DMA((3,)),
        ],
        compiler_params=pltpu.CompilerParams(vmem_limit_bytes=LARGE_BYTES),
        name="rest",
    )(
        place, right, left, *own, gain, in_vmem(embed), in_vmem(w),
        in_hbm(qkv_weight), in_hbm(out_weight),
    )


def shifted(cells, axis, by):
    count = lax.axis_size(axis)
    return lax.ppermute(cells, axis, [(i, (i + by) % count) for i in range(count)])


def around(x, first, last):
    top = shifted(last, "row", 1)
    bottom = shifted(first, "row", -1)
    two = 2 * HALO
    right_edge = jnp.concatenate([top[two:], x[2 * GRP :], bottom[two:]], axis=0)
    left_edge = jnp.concatenate([top[:two], x[: 2 * GRP], bottom[:two]], axis=0)
    right = shifted(left_edge, "col", -1)
    left = shifted(right_edge, "col", 1)
    return top, bottom, left, right


def per_device(
    scans, dest, offsets, profile_index, profiles, embed_weight, attn_gain, qkv_weight, out_weight
):
    place = jnp.stack(
        [
            lax.axis_index("row") * TOK_H,
            lax.axis_index("col") * TOK_W,
            jnp.asarray(lax.axis_size("row") * TOK_H, i32),
            jnp.asarray(lax.axis_size("col") * TOK_W, i32),
        ]
    ).astype(i32)
    embed = embed_weight.reshape(CH, 8, 8, MODEL).transpose(1, 0, 2, 3).reshape(PATCH, MODEL)
    payload = pack(dest, offsets, profile_index, profiles, scans)
    payload = lax.all_to_all(payload, ("row", "col"), split_axis=0, concat_axis=0, tiled=True)
    payload, place = lax.optimization_barrier((payload, place))
    x, first, last, embed, w = merge(payload, profiles, embed, qkv_weight)
    top, bottom, left, right = around(x, first, last)
    own = own_part(place, x, top, bottom, embed, attn_gain, w)
    tokens = rest(place, left, right, own, attn_gain, embed, w, qkv_weight, out_weight)
    return tokens.reshape(TOK_H, TOK_W, MODEL)


def solution(mesh):
    placed = (
        P(("row", "col"), None, None, None),
        P(("row", "col"), None),
        P(("row", "col")),
        P(("row", "col")),
        P(),
        P(),
        P(),
        P(),
        P(),
    )
    return jax.shard_map(
        per_device, mesh=mesh, in_specs=placed, out_specs=P("row", "col", None), check_vma=False
    )
```

```python
import functools

import jax
import jax.numpy as jnp
from jax import lax
from jax.experimental import pallas as pl
from jax.experimental.pallas import tpu as pltpu
from jax.sharding import PartitionSpec as P

HEADS = 16
RADIUS = 4
TOK_H = 32
TOK_W = 16
BR = 4
CH = 8
MODEL = 1024
PATCH = 512
GRP = 128
MID = 160
WIDE = 192
HALO = 32
EDGE = 4 * HALO
META = 128
CHUNKS = 4
VMEM_BYTES = 16 * 1024 * 1024
LARGE_BYTES = 22 * 1024 * 1024

f32 = jnp.float32
bf16 = jnp.bfloat16
i32 = jnp.int32


def dot(a, b):
    return lax.dot_general(a, b, (((1,), (0,)), ((), ())), preferred_element_type=f32)


def dot_nt(a, b):
    return lax.dot_general(a, b, (((1,), (1,)), ((), ())), preferred_element_type=f32)


def iota(shape, dim):
    return lax.broadcasted_iota(i32, shape, dim)


def onehot(cond):
    return jnp.where(cond, 1.0, 0.0).astype(bf16)


def halves(x):
    high = x.astype(bf16)
    return high, (x - high.astype(f32)).astype(bf16)


def pack_kernel(
    dest_hbm, offs_hbm, pidx_hbm, prof_hbm, scans_hbm, out_hbm,
    dest_ref, offs_ref, pidx_ref, prof_ref, scans_ref, w_ref, packed_ref, sem, out_sem,
):
    count = dest_ref.shape[1]
    chunk = scans_ref.shape[0] // CHUNKS
    small = [
        pltpu.make_async_copy(a, b, sem.at[n])
        for n, (a, b) in enumerate(
            [(dest_hbm, dest_ref), (offs_hbm, offs_ref), (pidx_hbm, pidx_ref), (prof_hbm, prof_ref)]
        )
    ]
    large = [
        pltpu.make_async_copy(
            scans_hbm.at[pl.ds(n * chunk, chunk)], scans_ref.at[pl.ds(n * chunk, chunk)], sem.at[4 + n]
        )
        for n in range(CHUNKS)
    ]
    for copy in small + large:
        copy.start()
    for copy in small:
        copy.wait()
    eye = iota((count, count), 0) == iota((count, count), 1)
    dest_row = dest_ref[...].astype(f32)
    dest_col = jnp.sum(jnp.where(eye, dest_row, 0.0), axis=1, keepdims=True)
    before = iota((count, count), 0) < iota((count, count), 1)
    same = (dest_col == dest_row) & before
    rank = jnp.sum(jnp.where(same, 1.0, 0.0), axis=0, keepdims=True)
    slot = dest_row * (2.0 * BR) + rank * float(BR)
    offs_col = jnp.sum(jnp.where(eye, offs_ref[...].astype(f32), 0.0), axis=1, keepdims=True)
    pidx_col = jnp.sum(jnp.where(eye, pidx_ref[...].astype(f32), 0.0), axis=1, keepdims=True)
    chosen = onehot(pidx_col == iota((count, prof_ref.shape[0]), 1).astype(f32))
    lane = iota((count, META), 1)
    meta = jnp.where(lane == 0, offs_col, jnp.where(lane == 1, pidx_col, 1.0)).astype(bf16)
    weights = []
    for k in range(BR):
        high, low = halves(prof_ref[:, k, :])
        weights.append(dot(chosen, high) + dot(chosen, low))
        w_ref[k * count : (k + 1) * count, CH * 128 :] = meta
    some = count // CHUNKS
    for n in range(CHUNKS):
        large[n].wait()
        for k in range(BR):
            for c in range(CH):
                block = scans_ref[pl.ds(n * chunk + k * CH + c, some, stride=BR * CH), :]
                at = k * count + n * some
                w_ref[at : at + some, c * 128 : (c + 1) * 128] = (
                    block * weights[k][n * some : (n + 1) * some, :]
                ).astype(bf16)
    slots = jnp.concatenate([slot + float(k) for k in range(BR)], axis=1)
    step = packed_ref.shape[0] // CHUNKS
    outs = []
    for n in range(CHUNKS):
        here = (iota((step, BR * count), 0) + n * step).astype(f32)
        rows = pl.ds(n * step, step)
        packed_ref[rows, :] = dot(onehot(here == slots), w_ref[...]).astype(bf16)
        outs.append(
            pltpu.make_async_copy(packed_ref.at[rows, :], out_hbm.at[rows, :], out_sem.at[n])
        )
        outs[-1].start()
    for copy in outs:
        copy.wait()


def pack(dest, offsets, profile_index, profiles, scans):
    count = scans.shape[0]
    rows = count * 2 * BR
    return pl.pallas_call(
        pack_kernel,
        out_shape=jax.ShapeDtypeStruct((rows, CH * 128 + META), bf16),
        in_specs=[pl.BlockSpec(memory_space=pltpu.HBM)] * 5,
        out_specs=pl.BlockSpec(memory_space=pltpu.HBM),
        scratch_shapes=[
            pltpu.VMEM((1, count), i32),
            pltpu.VMEM((1, count), i32),
            pltpu.VMEM((1, count), i32),
            pltpu.VMEM(profiles.shape, f32),
            pltpu.VMEM((count * BR * CH, 128), f32),
            pltpu.VMEM((BR * count, CH * 128 + META), bf16),
            pltpu.VMEM((rows, CH * 128 + META), bf16),
            pltpu.SemaphoreType.DMA((4 + CHUNKS,)),
            pltpu.SemaphoreType.DMA((CHUNKS,)),
        ],
        compiler_params=pltpu.CompilerParams(vmem_limit_bytes=VMEM_BYTES),
        name="pack",
    )(
        in_hbm(dest.reshape(1, count)),
        in_hbm(offsets.reshape(1, count)),
        in_hbm(profile_index.reshape(1, count)),
        in_hbm(profiles),
        in_hbm(scans.reshape(count * BR * CH, 128)),
    )


def in_hbm(x):
    return pltpu.with_memory_space_constraint(x, pltpu.HBM)


def in_vmem(x):
    return pltpu.with_memory_space_constraint(x, pltpu.VMEM)


def merge_kernel(
    pay_ref, prof_ref, embed_hbm, w_hbm, x_ref, top_ref, bot_ref, embed_ref, w_ref,
    mg_ref, y_ref, xg_ref, sem,
):
    rows = pay_ref.shape[0]
    copies = [
        pltpu.make_async_copy(embed_hbm, embed_ref, sem.at[0]),
        pltpu.make_async_copy(w_hbm.at[0], w_ref, sem.at[1]),
    ]
    for copy in copies:
        copy.start()
    pick = onehot(iota((8, META), 0) == iota((8, META), 1))
    fields = dot_nt(pick, pay_ref[:, CH * 128 :])
    offs = fields[0:1, :]
    pidx = fields[1:2, :]
    valid = fields[2:3, :]
    strip = (iota((1, rows), 1) % BR).astype(f32)
    land = jnp.where(valid > 0.5, offs + strip, 4096.0)
    kind = pidx + 16.0 * strip
    r = iota((TOK_H * 8, rows), 0)
    pixel = (r % TOK_H) * 8 + r // TOK_H
    placing = onehot(pixel.astype(f32) == land)
    kinds = onehot(iota((16 * BR, rows), 0).astype(f32) == kind)
    counts = dot_nt(placing, kinds).astype(bf16)
    table = jnp.concatenate([prof_ref[:, k, :] for k in range(BR)], axis=0)
    high, low = halves(table)
    scale = 1.0 / (1.0 + dot(counts, high) + dot(counts, low))
    for c in range(CH):
        part = dot(placing, pay_ref[:, c * 128 : (c + 1) * 128])
        mg_ref[:, c * 128 : (c + 1) * 128] = (part * scale).astype(bf16)
    width = CH * 128
    step = 256
    for n in range(0, width, step):
        source = iota((width, step), 0)
        to = iota((width, step), 1) + n
        wanted = (to // 8 % CH) * 128 + (to // 64) * 8 + to % 8
        y_ref[:, n : n + step] = dot(mg_ref[...], onehot(source == wanted))
    low_half = iota((TOK_H, 128), 1) < 64
    order = iota((GRP, GRP), 1)
    want = iota((GRP, GRP), 0)
    reorder = onehot(order == (want % 4) * TOK_H + want // 4)
    for g in range(4):
        for jj in range(4):
            j = 4 * g + jj
            tile = (j // 2) * 128
            for pp in range(4):
                a = y_ref[2 * pp * TOK_H : (2 * pp + 1) * TOK_H, tile : tile + 128]
                b = y_ref[(2 * pp + 1) * TOK_H : (2 * pp + 2) * TOK_H, tile : tile + 128]
                if j % 2 == 0:
                    piece = jnp.where(low_half, a, pltpu.roll(b, 64, 1))
                else:
                    piece = jnp.where(low_half, pltpu.roll(a, 64, 1), b)
                xg_ref[jj * TOK_H : (jj + 1) * TOK_H, pp * 128 : (pp + 1) * 128] = piece.astype(
                    bf16
                )
        tokens = dot(reorder, xg_ref[...]).astype(bf16)
        x_ref[g * GRP : (g + 1) * GRP, :] = tokens
        top_ref[g * HALO : (g + 1) * HALO, :] = tokens[:HALO, :]
        bot_ref[g * HALO : (g + 1) * HALO, :] = tokens[GRP - HALO :, :]
    for copy in copies:
        copy.wait()


def merge(payload, profiles, embed, qkv_weight):
    vmem = pl.BlockSpec(memory_space=pltpu.VMEM)
    hbm = pl.BlockSpec(memory_space=pltpu.HBM)
    return pl.pallas_call(
        merge_kernel,
        out_shape=[
            jax.ShapeDtypeStruct((4 * GRP, PATCH), bf16),
            jax.ShapeDtypeStruct((EDGE, PATCH), bf16),
            jax.ShapeDtypeStruct((EDGE, PATCH), bf16),
            pltpu.VMEM((PATCH, MODEL), bf16),
            pltpu.VMEM((MODEL, 3 * MODEL), bf16),
        ],
        in_specs=[vmem, vmem, hbm, hbm],
        scratch_shapes=[
            pltpu.VMEM((TOK_H * 8, CH * 128), bf16),
            pltpu.VMEM((TOK_H * 8, CH * 128), f32),
            pltpu.VMEM((GRP, PATCH), bf16),
            pltpu.SemaphoreType.DMA((2,)),
        ],
        compiler_params=pltpu.CompilerParams(vmem_limit_bytes=VMEM_BYTES),
        name="merge",
    )(payload, profiles, in_hbm(embed), in_hbm(qkv_weight))


def normed(stream, gain):
    centre = jnp.mean(stream, -1, keepdims=True)
    moved = stream - centre
    spread = jnp.mean(jnp.square(moved), -1, keepdims=True)
    return (moved * lax.rsqrt(spread + 1e-05) * gain).astype(bf16)


def own_kernel(
    place_ref, x_ref, top_ref, bot_ref, embed_ref, gain_ref, w_ref, w_hbm, o_hbm,
    stream_ref, q_ref, kv_ref, mid_ref, later_q_ref, later_kv_ref, o_ref, next_ref,
    inp_ref, att_ref, sem,
):
    copies = [
        pltpu.make_async_copy(o_hbm.at[0], o_ref, sem.at[0]),
        pltpu.make_async_copy(w_hbm.at[1], next_ref, sem.at[1]),
    ]
    for copy in copies:
        copy.start()
    for g in range(4):
        edge = slice(g * HALO, (g + 1) * HALO)
        tokens = jnp.concatenate(
            [top_ref[edge, :], x_ref[g * GRP : (g + 1) * GRP, :], bot_ref[edge, :]], axis=0
        )
        stream = dot(tokens, embed_ref[...])
        rows = slice(g * WIDE, (g + 1) * WIDE)
        stream_ref[rows, :] = stream
        inp_ref[rows, :] = normed(stream, gain_ref[0:1, :])
    project(inp_ref[...], inp_ref[...], w_ref, q_ref, kv_ref)
    attention(
        [1],
        5,
        lambda g: (q_ref, (g - 1) * WIDE + 16),
        lambda g: (kv_ref, (g - 2) * WIDE),
        lambda g: (att_ref, (g - 2) * MID),
        place_ref[0] - 8,
        place_ref[1] - 8,
        (place_ref[2], place_ref[3]),
    )
    for copy in copies:
        copy.wait()
    for n in range(2):
        rows = slice(n * MID, (n + 1) * MID)
        before = stream_ref[(n + 1) * WIDE + 16 : (n + 1) * WIDE + 16 + MID, :]
        stream = before + dot(att_ref[rows, :], o_ref[...])
        mid_ref[n * GRP : (n + 1) * GRP, :] = stream[16 : 16 + GRP, :]
        inp_ref[rows, :] = normed(stream, gain_ref[1:2, :])
    inputs = inp_ref[: 2 * MID, :]
    project(inputs, inputs, next_ref, later_q_ref, later_kv_ref)


def project(query_inputs, inputs, w_ref, q_ref, kv_ref):
    step = 256
    for m in range(0, MODEL, step):
        part = dot(query_inputs, w_ref[:, m : m + step]).astype(bf16)
        q_ref[: part.shape[0], m : m + step] = part * jnp.asarray(0.125, bf16)
    for m in range(0, 2 * MODEL, step):
        part = dot(inputs, w_ref[:, MODEL + m : MODEL + m + step]).astype(bf16)
        kv_ref[: part.shape[0], m : m + step] = part


def own_part(place, x, top, bottom, embed, gain, w, qkv_weight, out_weight):
    hbm = pl.BlockSpec(memory_space=pltpu.HBM)
    vmem = pl.BlockSpec(memory_space=pltpu.VMEM)
    smem = pl.BlockSpec(memory_space=pltpu.SMEM)
    return pl.pallas_call(
        own_kernel,
        out_shape=[
            jax.ShapeDtypeStruct((4 * WIDE, MODEL), f32),
            jax.ShapeDtypeStruct((4 * WIDE, MODEL), bf16),
            jax.ShapeDtypeStruct((4 * WIDE, 2 * MODEL), bf16),
            jax.ShapeDtypeStruct((2 * GRP, MODEL), f32),
            jax.ShapeDtypeStruct((2 * MID, MODEL), bf16),
            jax.ShapeDtypeStruct((2 * MID, 2 * MODEL), bf16),
            pltpu.VMEM((MODEL, MODEL), bf16),
            pltpu.VMEM((MODEL, 3 * MODEL), bf16),
        ],
        in_specs=[smem] + [vmem] * 6 + [hbm] * 2,
        scratch_shapes=[
            pltpu.VMEM((4 * WIDE, MODEL), bf16),
            pltpu.VMEM((2 * MID, MODEL), bf16),
            pltpu.SemaphoreType.DMA((2,)),
        ],
        compiler_params=pltpu.CompilerParams(vmem_limit_bytes=VMEM_BYTES),
        cost_estimate=pl.CostEstimate(
            flops=2 * 4 * WIDE * MODEL * 3 * MODEL, bytes_accessed=12 << 20, transcendentals=0
        ),
        name="own",
    )(
        place, x, top, bottom, in_vmem(embed), gain, in_vmem(w),
        in_hbm(qkv_weight), in_hbm(out_weight),
    )


def attention(broad, tall, q_of, kv_of, a_of, row, col, ends):
    query = iota((64, 256), 0)
    key = iota((64, 256), 1)
    row_gap = (key % 64) // 4 - 4 - (query % 32) // 4
    col_gap = (key // 64 - 1) * 4 + key % 4 - (query // 32) * 4 - query % 4
    near = (jnp.abs(row_gap) <= RADIUS) & (jnp.abs(col_gap) <= RADIUS)
    near_bias = jnp.where(near, 0.0, -1e30)
    lane_key = iota((1, 256), 1)
    key_row = (lane_key % 64) // 4 + row
    key_col = (lane_key // 64) * 4 + lane_key % 4 + col
    low_half = iota((64, 128), 1) < 64
    zero = jnp.zeros((64, 128), bf16)
    ones = jnp.ones((256, 128), bf16)

    for bi in range(tall):
        at_row = key_row + bi * 8
        row_inside = (at_row >= 0) & (at_row < ends[0])
        for bj in broad:
            at_col = key_col + bj * 8
            inside = row_inside & (at_col >= 0) & (at_col < ends[1])
            bias = near_bias + jnp.where(inside, 0.0, -1e30)
            bias = jnp.concatenate([bias, bias], axis=0)
            q_from = [q_of(2 * bj + g) for g in range(2)]
            k_from = [kv_of(2 * bj + g) for g in range(4)]
            a_to = [a_of(2 * bj + g) for g in range(2)]
            at = bi * 32
            for h in range(HEADS // 2):
                lanes = slice(h * 128, (h + 1) * 128)
                q = jnp.concatenate([r[b + at : b + at + 32, lanes] for r, b in q_from], axis=0)
                q = jnp.concatenate(
                    [jnp.where(low_half, q, zero), jnp.where(low_half, zero, q)], axis=0
                )
                k = jnp.concatenate([r[b + at : b + at + 64, lanes] for r, b in k_from], axis=0)
                v_lanes = slice(MODEL + h * 128, MODEL + (h + 1) * 128)
                v = jnp.concatenate([r[b + at : b + at + 64, v_lanes] for r, b in k_from], axis=0)
                logits = dot_nt(q, k) + bias
                top = jnp.max(logits, axis=-1, keepdims=True)
                share = jnp.exp(logits - top).astype(bf16)
                both = dot(share, jnp.concatenate([v, ones], axis=1))
                mixed = jnp.where(low_half, both[:64, :128], both[64:, :128])
                total = jnp.where(low_half, both[:64, 128:], both[64:, 128:])
                picked = (mixed / total).astype(bf16)
                for g, (r, b) in enumerate(a_to):
                    r[b + at : b + at + 32, lanes] = picked[g * 32 : (g + 1) * 32, :]


def rest_kernel(
    place_ref, right_ref, left_ref, stream_ref, oq_ref, okv_ref, omid_ref, mq_ref, mkv_ref, o_ref,
    next_ref, gain_ref, embed_ref, w_ref, o_hbm, out_ref,
    last_ref, side_ref, sq_ref, skv_ref, q_ref, kv_ref, mid_ref, att_ref, inp_ref, sem,
):
    copy = pltpu.make_async_copy(o_hbm.at[1], last_ref, sem)
    copy.start()

    for n in range(4):
        ref, g = (left_ref, right_ref)[n // 2], n % 2
        below = 2 * HALO + 2 * GRP
        tokens = jnp.concatenate(
            [
                ref[g * HALO : (g + 1) * HALO, :],
                ref[2 * HALO + g * GRP : 2 * HALO + (g + 1) * GRP, :],
                ref[below + g * HALO : below + (g + 1) * HALO, :],
            ],
            axis=0,
        )
        stream = dot(tokens, embed_ref[...])
        inp_ref[n * WIDE : (n + 1) * WIDE, :] = normed(stream, gain_ref[0:1, :])
        if n in (1, 2):
            side_ref[(n - 1) * WIDE : n * WIDE, :] = stream
    project(inp_ref[WIDE : 3 * WIDE, :], inp_ref[: 4 * WIDE, :], w_ref, sq_ref, skv_ref)

    def q_of(g):
        if g in (0, 5):
            return sq_ref, (g // 5) * WIDE + 16
        return oq_ref, (g - 1) * WIDE + 16

    def kv_of(g):
        if g in (0, 1, 6, 7):
            return skv_ref, (g if g < 2 else g - 4) * WIDE
        return okv_ref, (g - 2) * WIDE

    ends = (place_ref[2], place_ref[3])
    attention(
        [0, 2], 5, q_of, kv_of, lambda g: (att_ref, g * MID), place_ref[0] - 8, place_ref[1] - 8, ends
    )
    for n, g in enumerate((0, 1, 4, 5)):
        rows = slice(n * MID, (n + 1) * MID)
        if g in (0, 5):
            before = side_ref[(g // 5) * WIDE + 16 : (g // 5) * WIDE + 16 + MID, :]
        else:
            before = stream_ref[(g - 1) * WIDE + 16 : (g - 1) * WIDE + 16 + MID, :]
        stream = before + dot(att_ref[g * MID : (g + 1) * MID, :], o_ref[...])
        if n in (1, 2):
            mid_ref[(n - 1) * GRP : n * GRP, :] = stream[16 : 16 + GRP, :]
        inp_ref[rows, :] = normed(stream, gain_ref[1:2, :])

    project(inp_ref[MID : 3 * MID, :], inp_ref[: 4 * MID, :], next_ref, q_ref, kv_ref)

    def later_q_of(g):
        if g in (0, 3):
            return q_ref, (g // 3) * MID + 16
        return mq_ref, (g - 1) * MID + 16

    def later_kv_of(g):
        if g in (2, 3):
            return mkv_ref, (g - 2) * MID
        return kv_ref, (g if g < 2 else g - 2) * MID

    attention(
        [0, 1],
        4,
        later_q_of,
        later_kv_of,
        lambda g: (att_ref, g * GRP),
        place_ref[0] - 4,
        place_ref[1] - 4,
        ends,
    )
    copy.wait()
    for g in range(4):
        rows = slice(g * GRP, (g + 1) * GRP)
        before = omid_ref[(g - 1) * GRP : g * GRP, :] if g in (1, 2) else mid_ref[
            (g // 3) * GRP : (g // 3 + 1) * GRP, :
        ]
        inp_ref[rows, :] = (before + dot(att_ref[rows, :], last_ref[...])).astype(bf16)
    for r in range(0, 4 * GRP, GRP):
        to = iota((GRP, 4 * GRP), 0) + r
        source = iota((GRP, 4 * GRP), 1)
        wanted = (to // 4 % 4) * GRP + (to // 16) * 4 + to % 4
        out_ref[r : r + GRP, :] = dot(onehot(source == wanted), inp_ref[: 4 * GRP, :]).astype(bf16)


def rest(place, left, right, own, gain, embed, w, out_weight):
    hbm = pl.BlockSpec(memory_space=pltpu.HBM)
    vmem = pl.BlockSpec(memory_space=pltpu.VMEM)
    smem = pl.BlockSpec(memory_space=pltpu.SMEM)
    *own, o, later = own
    return pl.pallas_call(
        rest_kernel,
        out_shape=jax.ShapeDtypeStruct((4 * GRP, MODEL), bf16),
        in_specs=[smem] + [vmem] * 13 + [hbm],
        scratch_shapes=[
            pltpu.VMEM((MODEL, MODEL), bf16),
            pltpu.VMEM((2 * WIDE, MODEL), f32),
            pltpu.VMEM((2 * WIDE, MODEL), bf16),
            pltpu.VMEM((4 * WIDE, 2 * MODEL), bf16),
            pltpu.VMEM((2 * MID, MODEL), bf16),
            pltpu.VMEM((4 * MID, 2 * MODEL), bf16),
            pltpu.VMEM((2 * GRP, MODEL), f32),
            pltpu.VMEM((6 * MID, MODEL), bf16),
            pltpu.VMEM((4 * WIDE, MODEL), bf16),
            pltpu.SemaphoreType.DMA,
        ],
        compiler_params=pltpu.CompilerParams(vmem_limit_bytes=LARGE_BYTES),
        name="rest",
    )(
        place, right, left, *own, in_vmem(o), in_vmem(later), gain, in_vmem(embed), in_vmem(w),
        in_hbm(out_weight),
    )


def shifted(cells, axis, by):
    count = lax.axis_size(axis)
    return lax.ppermute(cells, axis, [(i, (i + by) % count) for i in range(count)])


def around(x, first, last):
    top = shifted(last, "row", 1)
    bottom = shifted(first, "row", -1)
    two = 2 * HALO
    right_edge = jnp.concatenate([top[two:], x[2 * GRP :], bottom[two:]], axis=0)
    left_edge = jnp.concatenate([top[:two], x[: 2 * GRP], bottom[:two]], axis=0)
    right = shifted(left_edge, "col", -1)
    left = shifted(right_edge, "col", 1)
    return top, bottom, left, right


def per_device(
    scans, dest, offsets, profile_index, profiles, embed_weight, attn_gain, qkv_weight, out_weight
):
    place = jnp.stack(
        [
            lax.axis_index("row") * TOK_H,
            lax.axis_index("col") * TOK_W,
            jnp.asarray(lax.axis_size("row") * TOK_H, i32),
            jnp.asarray(lax.axis_size("col") * TOK_W, i32),
        ]
    ).astype(i32)
    embed = embed_weight.reshape(CH, 8, 8, MODEL).transpose(1, 0, 2, 3).reshape(PATCH, MODEL)
    payload = pack(dest, offsets, profile_index, profiles, scans)
    payload = lax.all_to_all(payload, ("row", "col"), split_axis=0, concat_axis=0, tiled=True)
    payload, place = lax.optimization_barrier((payload, place))
    x, first, last, embed, w = merge(payload, profiles, embed, qkv_weight)
    top, bottom, left, right = around(x, first, last)
    own = own_part(place, x, top, bottom, embed, attn_gain, w, qkv_weight, out_weight)
    tokens = rest(place, left, right, own, attn_gain, embed, w, out_weight)
    return tokens.reshape(TOK_H, TOK_W, MODEL)


def solution(mesh):
    placed = (
        P(("row", "col"), None, None, None),
        P(("row", "col"), None),
        P(("row", "col")),
        P(("row", "col")),
        P(),
        P(),
        P(),
        P(),
        P(),
    )
    return jax.shard_map(
        per_device, mesh=mesh, in_specs=placed, out_specs=P("row", "col", None), check_vma=False
    )
```

```python
import functools

import jax
import jax.numpy as jnp
from jax import lax
from jax.experimental import pallas as pl
from jax.experimental.pallas import tpu as pltpu
from jax.sharding import Mesh
from jax.sharding import PartitionSpec as P

HEADS = 16
RADIUS = 4
TOK_H = 32
TOK_W = 16
N_COL = 16
BR = 4
CH = 8
MODEL = 1024
PATCH = 512
GRP = 128
MID = 160
WIDE = 192
HALO = 32
EDGE = 4 * HALO
META = 128
CHUNKS = 4
VMEM_BYTES = 16 * 1024 * 1024
LARGE_BYTES = 22 * 1024 * 1024

ROW = ("z", "core")

f32 = jnp.float32
bf16 = jnp.bfloat16
i32 = jnp.int32


def dot(a, b):
    return lax.dot_general(a, b, (((1,), (0,)), ((), ())), preferred_element_type=f32)


def dot_nt(a, b):
    return lax.dot_general(a, b, (((1,), (1,)), ((), ())), preferred_element_type=f32)


def iota(shape, dim):
    return lax.broadcasted_iota(i32, shape, dim)


def onehot(cond):
    return jnp.where(cond, 1.0, 0.0).astype(bf16)


def halves(x):
    high = x.astype(bf16)
    return high, (x - high.astype(f32)).astype(bf16)


def pack_kernel(
    dest_hbm, offs_hbm, pidx_hbm, prof_hbm, scans_hbm, out_hbm,
    dest_ref, offs_ref, pidx_ref, prof_ref, scans_ref, w_ref, packed_ref, sem, out_sem,
):
    count = dest_ref.shape[1]
    chunk = scans_ref.shape[0] // CHUNKS
    small = [
        pltpu.make_async_copy(a, b, sem.at[n])
        for n, (a, b) in enumerate(
            [(dest_hbm, dest_ref), (offs_hbm, offs_ref), (pidx_hbm, pidx_ref), (prof_hbm, prof_ref)]
        )
    ]
    large = [
        pltpu.make_async_copy(
            scans_hbm.at[pl.ds(n * chunk, chunk)], scans_ref.at[pl.ds(n * chunk, chunk)], sem.at[4 + n]
        )
        for n in range(CHUNKS)
    ]
    for copy in small + large:
        copy.start()
    for copy in small:
        copy.wait()
    eye = iota((count, count), 0) == iota((count, count), 1)
    tile = dest_ref[...]
    depth = count // (2 * N_COL)
    place = (tile // N_COL % 2 * depth + tile // (2 * N_COL)) * N_COL + tile % N_COL
    dest_row = place.astype(f32)
    dest_col = jnp.sum(jnp.where(eye, dest_row, 0.0), axis=1, keepdims=True)
    before = iota((count, count), 0) < iota((count, count), 1)
    same = (dest_col == dest_row) & before
    rank = jnp.sum(jnp.where(same, 1.0, 0.0), axis=0, keepdims=True)
    slot = dest_row * (2.0 * BR) + rank * float(BR)
    offs_col = jnp.sum(jnp.where(eye, offs_ref[...].astype(f32), 0.0), axis=1, keepdims=True)
    pidx_col = jnp.sum(jnp.where(eye, pidx_ref[...].astype(f32), 0.0), axis=1, keepdims=True)
    chosen = onehot(pidx_col == iota((count, prof_ref.shape[0]), 1).astype(f32))
    lane = iota((count, META), 1)
    meta = jnp.where(lane == 0, offs_col, jnp.where(lane == 1, pidx_col, 1.0)).astype(bf16)
    weights = []
    for k in range(BR):
        high, low = halves(prof_ref[:, k, :])
        weights.append(dot(chosen, high) + dot(chosen, low))
        w_ref[k * count : (k + 1) * count, CH * 128 :] = meta
    some = count // CHUNKS
    for n in range(CHUNKS):
        large[n].wait()
        for k in range(BR):
            for c in range(CH):
                block = scans_ref[pl.ds(n * chunk + k * CH + c, some, stride=BR * CH), :]
                at = k * count + n * some
                w_ref[at : at + some, c * 128 : (c + 1) * 128] = (
                    block * weights[k][n * some : (n + 1) * some, :]
                ).astype(bf16)
    slots = jnp.concatenate([slot + float(k) for k in range(BR)], axis=1)
    step = packed_ref.shape[0] // CHUNKS
    outs = []
    for n in range(CHUNKS):
        here = (iota((step, BR * count), 0) + n * step).astype(f32)
        rows = pl.ds(n * step, step)
        packed_ref[rows, :] = dot(onehot(here == slots), w_ref[...]).astype(bf16)
        outs.append(
            pltpu.make_async_copy(packed_ref.at[rows, :], out_hbm.at[rows, :], out_sem.at[n])
        )
        outs[-1].start()
    for copy in outs:
        copy.wait()


def pack(dest, offsets, profile_index, profiles, scans):
    count = scans.shape[0]
    rows = count * 2 * BR
    return pl.pallas_call(
        pack_kernel,
        out_shape=jax.ShapeDtypeStruct((rows, CH * 128 + META), bf16),
        in_specs=[pl.BlockSpec(memory_space=pltpu.HBM)] * 5,
        out_specs=pl.BlockSpec(memory_space=pltpu.HBM),
        scratch_shapes=[
            pltpu.VMEM((1, count), i32),
            pltpu.VMEM((1, count), i32),
            pltpu.VMEM((1, count), i32),
            pltpu.VMEM(profiles.shape, f32),
            pltpu.VMEM((count * BR * CH, 128), f32),
            pltpu.VMEM((BR * count, CH * 128 + META), bf16),
            pltpu.VMEM((rows, CH * 128 + META), bf16),
            pltpu.SemaphoreType.DMA((4 + CHUNKS,)),
            pltpu.SemaphoreType.DMA((CHUNKS,)),
        ],
        compiler_params=pltpu.CompilerParams(vmem_limit_bytes=VMEM_BYTES),
        name="pack",
    )(
        in_hbm(dest.reshape(1, count)),
        in_hbm(offsets.reshape(1, count)),
        in_hbm(profile_index.reshape(1, count)),
        in_hbm(profiles),
        in_hbm(scans.reshape(count * BR * CH, 128)),
    )


def in_hbm(x):
    return pltpu.with_memory_space_constraint(x, pltpu.HBM)


def in_vmem(x):
    return pltpu.with_memory_space_constraint(x, pltpu.VMEM)


def merge_kernel(
    pay_ref, prof_ref, embed_hbm, w_hbm, x_ref, top_ref, bot_ref, embed_ref, wq_ref,
    mg_ref, y_ref, xg_ref, sem,
):
    rows = pay_ref.shape[0]
    copies = [
        pltpu.make_async_copy(embed_hbm, embed_ref, sem.at[0]),
        pltpu.make_async_copy(w_hbm.at[0, :, pl.ds(0, MODEL)], wq_ref, sem.at[1]),
    ]
    for copy in copies:
        copy.start()
    pick = onehot(iota((8, META), 0) == iota((8, META), 1))
    fields = dot_nt(pick, pay_ref[:, CH * 128 :])
    offs = fields[0:1, :]
    pidx = fields[1:2, :]
    valid = fields[2:3, :]
    strip = (iota((1, rows), 1) % BR).astype(f32)
    land = jnp.where(valid > 0.5, offs + strip, 4096.0)
    kind = pidx + 16.0 * strip
    r = iota((TOK_H * 8, rows), 0)
    pixel = (r % TOK_H) * 8 + r // TOK_H
    placing = onehot(pixel.astype(f32) == land)
    kinds = onehot(iota((16 * BR, rows), 0).astype(f32) == kind)
    counts = dot_nt(placing, kinds).astype(bf16)
    table = jnp.concatenate([prof_ref[:, k, :] for k in range(BR)], axis=0)
    high, low = halves(table)
    scale = 1.0 / (1.0 + dot(counts, high) + dot(counts, low))
    for c in range(CH):
        part = dot(placing, pay_ref[:, c * 128 : (c + 1) * 128])
        mg_ref[:, c * 128 : (c + 1) * 128] = (part * scale).astype(bf16)
    width = CH * 128
    step = 256
    for n in range(0, width, step):
        source = iota((width, step), 0)
        to = iota((width, step), 1) + n
        wanted = (to // 8 % CH) * 128 + (to // 64) * 8 + to % 8
        y_ref[:, n : n + step] = dot(mg_ref[...], onehot(source == wanted))
    low_half = iota((TOK_H, 128), 1) < 64
    order = iota((GRP, GRP), 1)
    want = iota((GRP, GRP), 0)
    reorder = onehot(order == (want % 4) * TOK_H + want // 4)
    for g in range(4):
        for jj in range(4):
            j = 4 * g + jj
            tile = (j // 2) * 128
            for pp in range(4):
                a = y_ref[2 * pp * TOK_H : (2 * pp + 1) * TOK_H, tile : tile + 128]
                b = y_ref[(2 * pp + 1) * TOK_H : (2 * pp + 2) * TOK_H, tile : tile + 128]
                if j % 2 == 0:
                    piece = jnp.where(low_half, a, pltpu.roll(b, 64, 1))
                else:
                    piece = jnp.where(low_half, pltpu.roll(a, 64, 1), b)
                xg_ref[jj * TOK_H : (jj + 1) * TOK_H, pp * 128 : (pp + 1) * 128] = piece.astype(
                    bf16
                )
        tokens = dot(reorder, xg_ref[...]).astype(bf16)
        x_ref[g * GRP : (g + 1) * GRP, :] = tokens
        top_ref[g * HALO : (g + 1) * HALO, :] = tokens[:HALO, :]
        bot_ref[g * HALO : (g + 1) * HALO, :] = tokens[GRP - HALO :, :]
    for copy in copies:
        copy.wait()


def merge(payload, profiles, embed, qkv_weight):
    vmem = pl.BlockSpec(memory_space=pltpu.VMEM)
    hbm = pl.BlockSpec(memory_space=pltpu.HBM)
    return pl.pallas_call(
        merge_kernel,
        out_shape=[
            jax.ShapeDtypeStruct((4 * GRP, PATCH), bf16),
            jax.ShapeDtypeStruct((EDGE, PATCH), bf16),
            jax.ShapeDtypeStruct((EDGE, PATCH), bf16),
            pltpu.VMEM((PATCH, MODEL), bf16),
            pltpu.VMEM((MODEL, MODEL), bf16),
        ],
        in_specs=[vmem, vmem, hbm, hbm],
        scratch_shapes=[
            pltpu.VMEM((TOK_H * 8, CH * 128), bf16),
            pltpu.VMEM((TOK_H * 8, CH * 128), f32),
            pltpu.VMEM((GRP, PATCH), bf16),
            pltpu.SemaphoreType.DMA((2,)),
        ],
        compiler_params=pltpu.CompilerParams(vmem_limit_bytes=VMEM_BYTES),
        name="merge",
    )(payload, profiles, in_hbm(embed), in_hbm(qkv_weight))


def normed(stream, gain):
    centre = jnp.mean(stream, -1, keepdims=True)
    moved = stream - centre
    spread = jnp.mean(jnp.square(moved), -1, keepdims=True)
    return (moved * lax.rsqrt(spread + 1e-05) * gain).astype(bf16)


def own_kernel(
    place_ref, x_ref, top_ref, bot_ref, embed_ref, gain_ref, wq_ref, w_hbm, o_hbm,
    stream_ref, q_ref, kv_ref, mid_ref, later_q_ref, later_kv_ref, wkv_ref, o_ref, next_ref,
    inp_ref, att_ref, sem,
):
    copies = [
        pltpu.make_async_copy(w_hbm.at[0, :, pl.ds(MODEL, 2 * MODEL)], wkv_ref, sem.at[0]),
        pltpu.make_async_copy(o_hbm.at[0], o_ref, sem.at[1]),
        pltpu.make_async_copy(w_hbm.at[1], next_ref, sem.at[2]),
    ]
    for copy in copies:
        copy.start()
    for g in range(4):
        edge = slice(g * HALO, (g + 1) * HALO)
        tokens = jnp.concatenate(
            [top_ref[edge, :], x_ref[g * GRP : (g + 1) * GRP, :], bot_ref[edge, :]], axis=0
        )
        stream = dot(tokens, embed_ref[...])
        rows = slice(g * WIDE, (g + 1) * WIDE)
        stream_ref[rows, :] = stream
        inp_ref[rows, :] = normed(stream, gain_ref[0:1, :])
    project_queries(inp_ref[...], wq_ref, q_ref)
    copies[0].wait()
    project_keys(inp_ref[...], wkv_ref, 0, kv_ref)
    attention(
        [1],
        5,
        lambda g: (q_ref, (g - 1) * WIDE + 16),
        lambda g: (kv_ref, (g - 2) * WIDE),
        lambda g: (att_ref, (g - 2) * MID),
        place_ref[0] - 8,
        place_ref[1] - 8,
        (place_ref[2], place_ref[3]),
    )
    for copy in copies[1:]:
        copy.wait()
    for n in range(2):
        rows = slice(n * MID, (n + 1) * MID)
        before = stream_ref[(n + 1) * WIDE + 16 : (n + 1) * WIDE + 16 + MID, :]
        stream = before + dot(att_ref[rows, :], o_ref[...])
        mid_ref[n * GRP : (n + 1) * GRP, :] = stream[16 : 16 + GRP, :]
        inp_ref[rows, :] = normed(stream, gain_ref[1:2, :])
    inputs = inp_ref[: 2 * MID, :]
    project(inputs, inputs, next_ref, later_q_ref, later_kv_ref)


def project_queries(inputs, w_ref, q_ref):
    step = 256
    for m in range(0, MODEL, step):
        part = dot(inputs, w_ref[:, m : m + step]).astype(bf16)
        q_ref[: part.shape[0], m : m + step] = part * jnp.asarray(0.125, bf16)


def project_keys(inputs, w_ref, start, kv_ref):
    step = 256
    for m in range(0, 2 * MODEL, step):
        part = dot(inputs, w_ref[:, start + m : start + m + step]).astype(bf16)
        kv_ref[: part.shape[0], m : m + step] = part


def project(query_inputs, inputs, w_ref, q_ref, kv_ref):
    project_queries(query_inputs, w_ref, q_ref)
    project_keys(inputs, w_ref, MODEL, kv_ref)


def own_part(place, x, top, bottom, embed, gain, w, qkv_weight, out_weight):
    hbm = pl.BlockSpec(memory_space=pltpu.HBM)
    vmem = pl.BlockSpec(memory_space=pltpu.VMEM)
    smem = pl.BlockSpec(memory_space=pltpu.SMEM)
    return pl.pallas_call(
        own_kernel,
        out_shape=[
            jax.ShapeDtypeStruct((4 * WIDE, MODEL), f32),
            jax.ShapeDtypeStruct((4 * WIDE, MODEL), bf16),
            jax.ShapeDtypeStruct((4 * WIDE, 2 * MODEL), bf16),
            jax.ShapeDtypeStruct((2 * GRP, MODEL), f32),
            jax.ShapeDtypeStruct((2 * MID, MODEL), bf16),
            jax.ShapeDtypeStruct((2 * MID, 2 * MODEL), bf16),
            pltpu.VMEM((MODEL, 2 * MODEL), bf16),
            pltpu.VMEM((MODEL, MODEL), bf16),
            pltpu.VMEM((MODEL, 3 * MODEL), bf16),
        ],
        in_specs=[smem] + [vmem] * 6 + [hbm] * 2,
        scratch_shapes=[
            pltpu.VMEM((4 * WIDE, MODEL), bf16),
            pltpu.VMEM((2 * MID, MODEL), bf16),
            pltpu.SemaphoreType.DMA((3,)),
        ],
        compiler_params=pltpu.CompilerParams(vmem_limit_bytes=VMEM_BYTES),
        cost_estimate=pl.CostEstimate(
            flops=2 * 4 * WIDE * MODEL * 3 * MODEL, bytes_accessed=12 << 20, transcendentals=0
        ),
        name="own",
    )(
        place, x, top, bottom, in_vmem(embed), gain, in_vmem(w),
        in_hbm(qkv_weight), in_hbm(out_weight),
    )


def attention(broad, tall, q_of, kv_of, a_of, row, col, ends):
    query = iota((64, 256), 0)
    key = iota((64, 256), 1)
    row_gap = (key % 64) // 4 - 4 - (query % 32) // 4
    col_gap = (key // 64 - 1) * 4 + key % 4 - (query // 32) * 4 - query % 4
    near = (jnp.abs(row_gap) <= RADIUS) & (jnp.abs(col_gap) <= RADIUS)
    near_bias = jnp.where(near, 0.0, -1e30)
    lane_key = iota((1, 256), 1)
    key_row = (lane_key % 64) // 4 + row
    key_col = (lane_key // 64) * 4 + lane_key % 4 + col
    low_half = iota((64, 128), 1) < 64
    zero = jnp.zeros((64, 128), bf16)
    ones = jnp.ones((256, 128), bf16)

    for bi in range(tall):
        at_row = key_row + bi * 8
        row_inside = (at_row >= 0) & (at_row < ends[0])
        for bj in broad:
            at_col = key_col + bj * 8
            inside = row_inside & (at_col >= 0) & (at_col < ends[1])
            bias = near_bias + jnp.where(inside, 0.0, -1e30)
            bias = jnp.concatenate([bias, bias], axis=0)
            q_from = [q_of(2 * bj + g) for g in range(2)]
            k_from = [kv_of(2 * bj + g) for g in range(4)]
            a_to = [a_of(2 * bj + g) for g in range(2)]
            at = bi * 32
            for h in range(HEADS // 2):
                lanes = slice(h * 128, (h + 1) * 128)
                q = jnp.concatenate([r[b + at : b + at + 32, lanes] for r, b in q_from], axis=0)
                q = jnp.concatenate(
                    [jnp.where(low_half, q, zero), jnp.where(low_half, zero, q)], axis=0
                )
                k = jnp.concatenate([r[b + at : b + at + 64, lanes] for r, b in k_from], axis=0)
                v_lanes = slice(MODEL + h * 128, MODEL + (h + 1) * 128)
                v = jnp.concatenate([r[b + at : b + at + 64, v_lanes] for r, b in k_from], axis=0)
                logits = dot_nt(q, k) + bias
                top = jnp.max(logits, axis=-1, keepdims=True)
                share = jnp.exp(logits - top).astype(bf16)
                both = dot(share, jnp.concatenate([v, ones], axis=1))
                mixed = jnp.where(low_half, both[:64, :128], both[64:, :128])
                total = jnp.where(low_half, both[:64, 128:], both[64:, 128:])
                picked = (mixed / total).astype(bf16)
                for g, (r, b) in enumerate(a_to):
                    r[b + at : b + at + 32, lanes] = picked[g * 32 : (g + 1) * 32, :]


def rest_kernel(
    place_ref, right_ref, left_ref, stream_ref, oq_ref, okv_ref, omid_ref, mq_ref, mkv_ref, wkv_ref,
    o_ref, next_ref, gain_ref, embed_ref, wq_ref, o_hbm, out_ref,
    last_ref, side_ref, sq_ref, skv_ref, q_ref, kv_ref, mid_ref, att_ref, inp_ref, sem,
):
    copy = pltpu.make_async_copy(o_hbm.at[1], last_ref, sem)
    copy.start()

    for n in range(4):
        ref, g = (left_ref, right_ref)[n // 2], n % 2
        below = 2 * HALO + 2 * GRP
        tokens = jnp.concatenate(
            [
                ref[g * HALO : (g + 1) * HALO, :],
                ref[2 * HALO + g * GRP : 2 * HALO + (g + 1) * GRP, :],
                ref[below + g * HALO : below + (g + 1) * HALO, :],
            ],
            axis=0,
        )
        stream = dot(tokens, embed_ref[...])
        inp_ref[n * WIDE : (n + 1) * WIDE, :] = normed(stream, gain_ref[0:1, :])
        if n in (1, 2):
            side_ref[(n - 1) * WIDE : n * WIDE, :] = stream
    project_queries(inp_ref[WIDE : 3 * WIDE, :], wq_ref, sq_ref)
    project_keys(inp_ref[: 4 * WIDE, :], wkv_ref, 0, skv_ref)

    def q_of(g):
        if g in (0, 5):
            return sq_ref, (g // 5) * WIDE + 16
        return oq_ref, (g - 1) * WIDE + 16

    def kv_of(g):
        if g in (0, 1, 6, 7):
            return skv_ref, (g if g < 2 else g - 4) * WIDE
        return okv_ref, (g - 2) * WIDE

    ends = (place_ref[2], place_ref[3])
    attention(
        [0, 2], 5, q_of, kv_of, lambda g: (att_ref, g * MID), place_ref[0] - 8, place_ref[1] - 8, ends
    )
    for n, g in enumerate((0, 1, 4, 5)):
        rows = slice(n * MID, (n + 1) * MID)
        if g in (0, 5):
            before = side_ref[(g // 5) * WIDE + 16 : (g // 5) * WIDE + 16 + MID, :]
        else:
            before = stream_ref[(g - 1) * WIDE + 16 : (g - 1) * WIDE + 16 + MID, :]
        stream = before + dot(att_ref[g * MID : (g + 1) * MID, :], o_ref[...])
        if n in (1, 2):
            mid_ref[(n - 1) * GRP : n * GRP, :] = stream[16 : 16 + GRP, :]
        inp_ref[rows, :] = normed(stream, gain_ref[1:2, :])

    project(inp_ref[MID : 3 * MID, :], inp_ref[: 4 * MID, :], next_ref, q_ref, kv_ref)

    def later_q_of(g):
        if g in (0, 3):
            return q_ref, (g // 3) * MID + 16
        return mq_ref, (g - 1) * MID + 16

    def later_kv_of(g):
        if g in (2, 3):
            return mkv_ref, (g - 2) * MID
        return kv_ref, (g if g < 2 else g - 2) * MID

    attention(
        [0, 1],
        4,
        later_q_of,
        later_kv_of,
        lambda g: (att_ref, g * GRP),
        place_ref[0] - 4,
        place_ref[1] - 4,
        ends,
    )
    copy.wait()
    for g in range(4):
        rows = slice(g * GRP, (g + 1) * GRP)
        before = omid_ref[(g - 1) * GRP : g * GRP, :] if g in (1, 2) else mid_ref[
            (g // 3) * GRP : (g // 3 + 1) * GRP, :
        ]
        inp_ref[rows, :] = (before + dot(att_ref[rows, :], last_ref[...])).astype(bf16)
    for r in range(0, 4 * GRP, GRP):
        to = iota((GRP, 4 * GRP), 0) + r
        source = iota((GRP, 4 * GRP), 1)
        wanted = (to // 4 % 4) * GRP + (to // 16) * 4 + to % 4
        out_ref[r : r + GRP, :] = dot(onehot(source == wanted), inp_ref[: 4 * GRP, :]).astype(bf16)


def rest(place, left, right, own, gain, embed, w, out_weight):
    hbm = pl.BlockSpec(memory_space=pltpu.HBM)
    vmem = pl.BlockSpec(memory_space=pltpu.VMEM)
    smem = pl.BlockSpec(memory_space=pltpu.SMEM)
    *own, wkv, o, later = own
    return pl.pallas_call(
        rest_kernel,
        out_shape=jax.ShapeDtypeStruct((4 * GRP, MODEL), bf16),
        in_specs=[smem] + [vmem] * 14 + [hbm],
        scratch_shapes=[
            pltpu.VMEM((MODEL, MODEL), bf16),
            pltpu.VMEM((2 * WIDE, MODEL), f32),
            pltpu.VMEM((2 * WIDE, MODEL), bf16),
            pltpu.VMEM((4 * WIDE, 2 * MODEL), bf16),
            pltpu.VMEM((2 * MID, MODEL), bf16),
            pltpu.VMEM((4 * MID, 2 * MODEL), bf16),
            pltpu.VMEM((2 * GRP, MODEL), f32),
            pltpu.VMEM((6 * MID, MODEL), bf16),
            pltpu.VMEM((4 * WIDE, MODEL), bf16),
            pltpu.SemaphoreType.DMA,
        ],
        compiler_params=pltpu.CompilerParams(vmem_limit_bytes=LARGE_BYTES),
        name="rest",
    )(
        place, right, left, *own, in_vmem(wkv), in_vmem(o), in_vmem(later), gain, in_vmem(embed),
        in_vmem(w), in_hbm(out_weight),
    )


def shifted(cells, axis, by):
    count = lax.axis_size(axis)
    return lax.ppermute(cells, axis, [(i, (i + by) % count) for i in range(count)])


def around(x, first, last):
    top = shifted(last, ROW, 1)
    bottom = shifted(first, ROW, -1)
    two = 2 * HALO
    right_edge = jnp.concatenate([top[two:], x[2 * GRP :], bottom[two:]], axis=0)
    left_edge = jnp.concatenate([top[:two], x[: 2 * GRP], bottom[:two]], axis=0)
    right = shifted(left_edge, "col", -1)
    left = shifted(right_edge, "col", 1)
    return top, bottom, left, right


def per_device(
    scans, dest, offsets, profile_index, profiles, embed_weight, attn_gain, qkv_weight, out_weight
):
    place = jnp.stack(
        [
            lax.axis_index(ROW) * TOK_H,
            lax.axis_index("col") * TOK_W,
            jnp.asarray(lax.axis_size(ROW) * TOK_H, i32),
            jnp.asarray(lax.axis_size("col") * TOK_W, i32),
        ]
    ).astype(i32)
    embed = embed_weight.reshape(CH, 8, 8, MODEL).transpose(1, 0, 2, 3).reshape(PATCH, MODEL)
    payload = pack(dest, offsets, profile_index, profiles, scans)
    payload = lax.all_to_all(
        payload, ("core", "z", "col"), split_axis=0, concat_axis=0, tiled=True
    )
    payload, place = lax.optimization_barrier((payload, place))
    x, first, last, embed, w = merge(payload, profiles, embed, qkv_weight)
    top, bottom, left, right = around(x, first, last)
    own = own_part(place, x, top, bottom, embed, attn_gain, w, qkv_weight, out_weight)
    tokens = rest(place, left, right, own, attn_gain, embed, w, out_weight)
    return tokens.reshape(TOK_H, TOK_W, MODEL)


def solution(mesh):
    rows, cols = mesh.shape["row"], mesh.shape["col"]
    chips = Mesh(mesh.devices.reshape(rows // 2, 2, cols), (*ROW, "col"))
    every = (*ROW, "col")
    placed = (P(every, None, None, None), P(every, None), P(every), P(every), P(), P(), P(), P(), P())
    return jax.shard_map(
        per_device, mesh=chips, in_specs=placed, out_specs=P(ROW, "col", None), check_vma=False
    )
```

```python
import functools

import jax
import jax.numpy as jnp
from jax import lax
from jax.experimental import pallas as pl
from jax.experimental.pallas import tpu as pltpu
from jax.sharding import PartitionSpec as P

HEADS = 16
RADIUS = 4
TOK_H = 32
TOK_W = 16
BR = 4
CH = 8
MODEL = 1024
PATCH = 512
GRP = 128
MID = 160
WIDE = 192
HALO = 32
EDGE = 4 * HALO
META = 128
CHUNKS = 4
VMEM_BYTES = 16 * 1024 * 1024
LARGE_BYTES = 22 * 1024 * 1024

f32 = jnp.float32
bf16 = jnp.bfloat16
i32 = jnp.int32


def dot(a, b):
    return lax.dot_general(a, b, (((1,), (0,)), ((), ())), preferred_element_type=f32)


def dot_nt(a, b):
    return lax.dot_general(a, b, (((1,), (1,)), ((), ())), preferred_element_type=f32)


def iota(shape, dim):
    return lax.broadcasted_iota(i32, shape, dim)


def onehot(cond):
    return jnp.where(cond, 1.0, 0.0).astype(bf16)


def halves(x):
    high = x.astype(bf16)
    return high, (x - high.astype(f32)).astype(bf16)


def pack_kernel(
    dest_hbm, offs_hbm, pidx_hbm, prof_hbm, scans_hbm, out_hbm,
    dest_ref, offs_ref, pidx_ref, prof_ref, scans_ref, w_ref, packed_ref, sem, out_sem,
):
    count = dest_ref.shape[1]
    chunk = scans_ref.shape[0] // CHUNKS
    small = [
        pltpu.make_async_copy(a, b, sem.at[n])
        for n, (a, b) in enumerate(
            [(dest_hbm, dest_ref), (offs_hbm, offs_ref), (pidx_hbm, pidx_ref), (prof_hbm, prof_ref)]
        )
    ]
    large = [
        pltpu.make_async_copy(
            scans_hbm.at[pl.ds(n * chunk, chunk)], scans_ref.at[pl.ds(n * chunk, chunk)], sem.at[4 + n]
        )
        for n in range(CHUNKS)
    ]
    for copy in small + large:
        copy.start()
    for copy in small:
        copy.wait()
    eye = iota((count, count), 0) == iota((count, count), 1)
    dest_row = dest_ref[...].astype(f32)
    dest_col = jnp.sum(jnp.where(eye, dest_row, 0.0), axis=1, keepdims=True)
    before = iota((count, count), 0) < iota((count, count), 1)
    same = (dest_col == dest_row) & before
    rank = jnp.sum(jnp.where(same, 1.0, 0.0), axis=0, keepdims=True)
    slot = dest_row * (2.0 * BR) + rank * float(BR)
    offs_col = jnp.sum(jnp.where(eye, offs_ref[...].astype(f32), 0.0), axis=1, keepdims=True)
    pidx_col = jnp.sum(jnp.where(eye, pidx_ref[...].astype(f32), 0.0), axis=1, keepdims=True)
    chosen = onehot(pidx_col == iota((count, prof_ref.shape[0]), 1).astype(f32))
    lane = iota((count, META), 1)
    meta = jnp.where(lane == 0, offs_col, jnp.where(lane == 1, pidx_col, 1.0)).astype(bf16)
    weights = []
    for k in range(BR):
        high, low = halves(prof_ref[:, k, :])
        weights.append(dot(chosen, high) + dot(chosen, low))
        w_ref[k * count : (k + 1) * count, CH * 128 :] = meta
    some = count // CHUNKS
    for n in range(CHUNKS):
        large[n].wait()
        for k in range(BR):
            for c in range(CH):
                block = scans_ref[pl.ds(n * chunk + k * CH + c, some, stride=BR * CH), :]
                at = k * count + n * some
                w_ref[at : at + some, c * 128 : (c + 1) * 128] = (
                    block * weights[k][n * some : (n + 1) * some, :]
                ).astype(bf16)
    slots = jnp.concatenate([slot + float(k) for k in range(BR)], axis=1)
    step = packed_ref.shape[0] // CHUNKS
    outs = []
    for n in range(CHUNKS):
        here = (iota((step, BR * count), 0) + n * step).astype(f32)
        rows = pl.ds(n * step, step)
        packed_ref[rows, :] = dot(onehot(here == slots), w_ref[...]).astype(bf16)
        outs.append(
            pltpu.make_async_copy(packed_ref.at[rows, :], out_hbm.at[rows, :], out_sem.at[n])
        )
        outs[-1].start()
    for copy in outs:
        copy.wait()


def pack(dest, offsets, profile_index, profiles, scans):
    count = scans.shape[0]
    rows = count * 2 * BR
    return pl.pallas_call(
        pack_kernel,
        out_shape=jax.ShapeDtypeStruct((rows, CH * 128 + META), bf16),
        in_specs=[pl.BlockSpec(memory_space=pltpu.HBM)] * 5,
        out_specs=pl.BlockSpec(memory_space=pltpu.HBM),
        scratch_shapes=[
            pltpu.VMEM((1, count), i32),
            pltpu.VMEM((1, count), i32),
            pltpu.VMEM((1, count), i32),
            pltpu.VMEM(profiles.shape, f32),
            pltpu.VMEM((count * BR * CH, 128), f32),
            pltpu.VMEM((BR * count, CH * 128 + META), bf16),
            pltpu.VMEM((rows, CH * 128 + META), bf16),
            pltpu.SemaphoreType.DMA((4 + CHUNKS,)),
            pltpu.SemaphoreType.DMA((CHUNKS,)),
        ],
        compiler_params=pltpu.CompilerParams(vmem_limit_bytes=VMEM_BYTES),
        name="pack",
    )(
        in_hbm(dest.reshape(1, count)),
        in_hbm(offsets.reshape(1, count)),
        in_hbm(profile_index.reshape(1, count)),
        in_hbm(profiles),
        in_hbm(scans.reshape(count * BR * CH, 128)),
    )


def in_hbm(x):
    return pltpu.with_memory_space_constraint(x, pltpu.HBM)


def in_vmem(x):
    return pltpu.with_memory_space_constraint(x, pltpu.VMEM)


def merge_kernel(
    pay_ref, prof_ref, embed_hbm, w_hbm, x_ref, top_ref, bot_ref, embed_ref, wq_ref,
    mg_ref, y_ref, xg_ref, sem,
):
    rows = pay_ref.shape[0]
    copies = [
        pltpu.make_async_copy(embed_hbm, embed_ref, sem.at[0]),
        pltpu.make_async_copy(w_hbm.at[0, :, pl.ds(0, MODEL)], wq_ref, sem.at[1]),
    ]
    for copy in copies:
        copy.start()
    pick = onehot(iota((8, META), 0) == iota((8, META), 1))
    fields = dot_nt(pick, pay_ref[:, CH * 128 :])
    offs = fields[0:1, :]
    pidx = fields[1:2, :]
    valid = fields[2:3, :]
    strip = (iota((1, rows), 1) % BR).astype(f32)
    land = jnp.where(valid > 0.5, offs + strip, 4096.0)
    kind = pidx + 16.0 * strip
    r = iota((TOK_H * 8, rows), 0)
    pixel = (r % TOK_H) * 8 + r // TOK_H
    placing = onehot(pixel.astype(f32) == land)
    kinds = onehot(iota((16 * BR, rows), 0).astype(f32) == kind)
    counts = dot_nt(placing, kinds).astype(bf16)
    table = jnp.concatenate([prof_ref[:, k, :] for k in range(BR)], axis=0)
    high, low = halves(table)
    scale = 1.0 / (1.0 + dot(counts, high) + dot(counts, low))
    for c in range(CH):
        part = dot(placing, pay_ref[:, c * 128 : (c + 1) * 128])
        mg_ref[:, c * 128 : (c + 1) * 128] = (part * scale).astype(bf16)
    width = CH * 128
    step = 256
    for n in range(0, width, step):
        source = iota((width, step), 0)
        to = iota((width, step), 1) + n
        wanted = (to // 8 % CH) * 128 + (to // 64) * 8 + to % 8
        y_ref[:, n : n + step] = dot(mg_ref[...], onehot(source == wanted))
    low_half = iota((TOK_H, 128), 1) < 64
    order = iota((GRP, GRP), 1)
    want = iota((GRP, GRP), 0)
    reorder = onehot(order == (want % 4) * TOK_H + want // 4)
    for g in range(4):
        for jj in range(4):
            j = 4 * g + jj
            tile = (j // 2) * 128
            for pp in range(4):
                a = y_ref[2 * pp * TOK_H : (2 * pp + 1) * TOK_H, tile : tile + 128]
                b = y_ref[(2 * pp + 1) * TOK_H : (2 * pp + 2) * TOK_H, tile : tile + 128]
                if j % 2 == 0:
                    piece = jnp.where(low_half, a, pltpu.roll(b, 64, 1))
                else:
                    piece = jnp.where(low_half, pltpu.roll(a, 64, 1), b)
                xg_ref[jj * TOK_H : (jj + 1) * TOK_H, pp * 128 : (pp + 1) * 128] = piece.astype(
                    bf16
                )
        tokens = dot(reorder, xg_ref[...]).astype(bf16)
        x_ref[g * GRP : (g + 1) * GRP, :] = tokens
        top_ref[g * HALO : (g + 1) * HALO, :] = tokens[:HALO, :]
        bot_ref[g * HALO : (g + 1) * HALO, :] = tokens[GRP - HALO :, :]
    for copy in copies:
        copy.wait()


def merge(payload, profiles, embed, qkv_weight):
    vmem = pl.BlockSpec(memory_space=pltpu.VMEM)
    hbm = pl.BlockSpec(memory_space=pltpu.HBM)
    return pl.pallas_call(
        merge_kernel,
        out_shape=[
            jax.ShapeDtypeStruct((4 * GRP, PATCH), bf16),
            jax.ShapeDtypeStruct((EDGE, PATCH), bf16),
            jax.ShapeDtypeStruct((EDGE, PATCH), bf16),
            pltpu.VMEM((PATCH, MODEL), bf16),
            pltpu.VMEM((MODEL, MODEL), bf16),
        ],
        in_specs=[vmem, vmem, hbm, hbm],
        scratch_shapes=[
            pltpu.VMEM((TOK_H * 8, CH * 128), bf16),
            pltpu.VMEM((TOK_H * 8, CH * 128), f32),
            pltpu.VMEM((GRP, PATCH), bf16),
            pltpu.SemaphoreType.DMA((2,)),
        ],
        compiler_params=pltpu.CompilerParams(vmem_limit_bytes=VMEM_BYTES),
        name="merge",
    )(payload, profiles, in_hbm(embed), in_hbm(qkv_weight))


def normed(stream, gain):
    centre = jnp.mean(stream, -1, keepdims=True)
    moved = stream - centre
    spread = jnp.mean(jnp.square(moved), -1, keepdims=True)
    return (moved * lax.rsqrt(spread + 1e-05) * gain).astype(bf16)


def own_kernel(
    place_ref, x_ref, top_ref, bot_ref, embed_ref, gain_ref, wq_ref, w_hbm, o_hbm,
    stream_ref, q_ref, kv_ref, mid_ref, later_q_ref, later_kv_ref, wkv_ref, o_ref, next_ref,
    inp_ref, att_ref, sem,
):
    copies = [
        pltpu.make_async_copy(w_hbm.at[0, :, pl.ds(MODEL, 2 * MODEL)], wkv_ref, sem.at[0]),
        pltpu.make_async_copy(o_hbm.at[0], o_ref, sem.at[1]),
        pltpu.make_async_copy(w_hbm.at[1], next_ref, sem.at[2]),
    ]
    for copy in copies:
        copy.start()
    for g in range(4):
        edge = slice(g * HALO, (g + 1) * HALO)
        tokens = jnp.concatenate(
            [top_ref[edge, :], x_ref[g * GRP : (g + 1) * GRP, :], bot_ref[edge, :]], axis=0
        )
        stream = dot(tokens, embed_ref[...])
        rows = slice(g * WIDE, (g + 1) * WIDE)
        stream_ref[rows, :] = stream
        inp_ref[rows, :] = normed(stream, gain_ref[0:1, :])
    project_queries(inp_ref[...], wq_ref, q_ref)
    copies[0].wait()
    project_keys(inp_ref[...], wkv_ref, 0, kv_ref)
    attention(
        [1],
        5,
        lambda g: (q_ref, (g - 1) * WIDE + 16),
        lambda g: (kv_ref, (g - 2) * WIDE),
        lambda g: (att_ref, (g - 2) * MID),
        place_ref[0] - 8,
        place_ref[1] - 8,
        (place_ref[2], place_ref[3]),
    )
    for copy in copies[1:]:
        copy.wait()
    for n in range(2):
        rows = slice(n * MID, (n + 1) * MID)
        before = stream_ref[(n + 1) * WIDE + 16 : (n + 1) * WIDE + 16 + MID, :]
        stream = before + dot(att_ref[rows, :], o_ref[...])
        mid_ref[n * GRP : (n + 1) * GRP, :] = stream[16 : 16 + GRP, :]
        inp_ref[rows, :] = normed(stream, gain_ref[1:2, :])
    inputs = inp_ref[: 2 * MID, :]
    project(inputs, inputs, next_ref, later_q_ref, later_kv_ref)


def project_queries(inputs, w_ref, q_ref):
    step = 256
    for m in range(0, MODEL, step):
        part = dot(inputs, w_ref[:, m : m + step]).astype(bf16)
        q_ref[: part.shape[0], m : m + step] = part * jnp.asarray(0.125, bf16)


def project_keys(inputs, w_ref, start, kv_ref):
    step = 256
    for m in range(0, 2 * MODEL, step):
        part = dot(inputs, w_ref[:, start + m : start + m + step]).astype(bf16)
        kv_ref[: part.shape[0], m : m + step] = part


def project(query_inputs, inputs, w_ref, q_ref, kv_ref):
    project_queries(query_inputs, w_ref, q_ref)
    project_keys(inputs, w_ref, MODEL, kv_ref)


def own_part(place, x, top, bottom, embed, gain, w, qkv_weight, out_weight):
    hbm = pl.BlockSpec(memory_space=pltpu.HBM)
    vmem = pl.BlockSpec(memory_space=pltpu.VMEM)
    smem = pl.BlockSpec(memory_space=pltpu.SMEM)
    return pl.pallas_call(
        own_kernel,
        out_shape=[
            jax.ShapeDtypeStruct((4 * WIDE, MODEL), f32),
            jax.ShapeDtypeStruct((4 * WIDE, MODEL), bf16),
            jax.ShapeDtypeStruct((4 * WIDE, 2 * MODEL), bf16),
            jax.ShapeDtypeStruct((2 * GRP, MODEL), f32),
            jax.ShapeDtypeStruct((2 * MID, MODEL), bf16),
            jax.ShapeDtypeStruct((2 * MID, 2 * MODEL), bf16),
            pltpu.VMEM((MODEL, 2 * MODEL), bf16),
            pltpu.VMEM((MODEL, MODEL), bf16),
            pltpu.VMEM((MODEL, 3 * MODEL), bf16),
        ],
        in_specs=[smem] + [vmem] * 6 + [hbm] * 2,
        scratch_shapes=[
            pltpu.VMEM((4 * WIDE, MODEL), bf16),
            pltpu.VMEM((2 * MID, MODEL), bf16),
            pltpu.SemaphoreType.DMA((3,)),
        ],
        compiler_params=pltpu.CompilerParams(vmem_limit_bytes=VMEM_BYTES),
        cost_estimate=pl.CostEstimate(
            flops=2 * 4 * WIDE * MODEL * 3 * MODEL, bytes_accessed=12 << 20, transcendentals=0
        ),
        name="own",
    )(
        place, x, top, bottom, in_vmem(embed), gain, in_vmem(w),
        in_hbm(qkv_weight), in_hbm(out_weight),
    )


def attention(broad, tall, q_of, kv_of, a_of, row, col, ends):
    query = iota((64, 256), 0)
    key = iota((64, 256), 1)
    row_gap = (key % 64) // 4 - 4 - (query % 32) // 4
    col_gap = (key // 64 - 1) * 4 + key % 4 - (query // 32) * 4 - query % 4
    near = (jnp.abs(row_gap) <= RADIUS) & (jnp.abs(col_gap) <= RADIUS)
    near_bias = jnp.where(near, 0.0, -1e30)
    lane_key = iota((1, 256), 1)
    key_row = (lane_key % 64) // 4 + row
    key_col = (lane_key // 64) * 4 + lane_key % 4 + col
    low_half = iota((64, 128), 1) < 64
    zero = jnp.zeros((64, 128), bf16)
    ones = jnp.ones((256, 128), bf16)

    for bi in range(tall):
        at_row = key_row + bi * 8
        row_inside = (at_row >= 0) & (at_row < ends[0])
        for bj in broad:
            at_col = key_col + bj * 8
            inside = row_inside & (at_col >= 0) & (at_col < ends[1])
            bias = near_bias + jnp.where(inside, 0.0, -1e30)
            bias = jnp.concatenate([bias, bias], axis=0)
            q_from = [q_of(2 * bj + g) for g in range(2)]
            k_from = [kv_of(2 * bj + g) for g in range(4)]
            a_to = [a_of(2 * bj + g) for g in range(2)]
            at = bi * 32
            for h in range(HEADS // 2):
                lanes = slice(h * 128, (h + 1) * 128)
                q = jnp.concatenate([r[b + at : b + at + 32, lanes] for r, b in q_from], axis=0)
                q = jnp.concatenate(
                    [jnp.where(low_half, q, zero), jnp.where(low_half, zero, q)], axis=0
                )
                k = jnp.concatenate([r[b + at : b + at + 64, lanes] for r, b in k_from], axis=0)
                v_lanes = slice(MODEL + h * 128, MODEL + (h + 1) * 128)
                v = jnp.concatenate([r[b + at : b + at + 64, v_lanes] for r, b in k_from], axis=0)
                logits = dot_nt(q, k) + bias
                top = jnp.max(logits, axis=-1, keepdims=True)
                share = jnp.exp(logits - top).astype(bf16)
                both = dot(share, jnp.concatenate([v, ones], axis=1))
                mixed = jnp.where(low_half, both[:64, :128], both[64:, :128])
                total = jnp.where(low_half, both[:64, 128:], both[64:, 128:])
                picked = (mixed / total).astype(bf16)
                for g, (r, b) in enumerate(a_to):
                    r[b + at : b + at + 32, lanes] = picked[g * 32 : (g + 1) * 32, :]


def rest_kernel(
    place_ref, right_ref, left_ref, stream_ref, oq_ref, okv_ref, omid_ref, mq_ref, mkv_ref, wkv_ref,
    o_ref, next_ref, gain_ref, embed_ref, wq_ref, o_hbm, out_hbm,
    last_ref, side_ref, sq_ref, skv_ref, q_ref, kv_ref, mid_ref, att_ref, inp_ref, sem, out_sem,
):
    copy = pltpu.make_async_copy(o_hbm.at[1], last_ref, sem)
    copy.start()

    for n in range(4):
        ref, g = (left_ref, right_ref)[n // 2], n % 2
        below = 2 * HALO + 2 * GRP
        tokens = jnp.concatenate(
            [
                ref[g * HALO : (g + 1) * HALO, :],
                ref[2 * HALO + g * GRP : 2 * HALO + (g + 1) * GRP, :],
                ref[below + g * HALO : below + (g + 1) * HALO, :],
            ],
            axis=0,
        )
        stream = dot(tokens, embed_ref[...])
        inp_ref[n * WIDE : (n + 1) * WIDE, :] = normed(stream, gain_ref[0:1, :])
        if n in (1, 2):
            side_ref[(n - 1) * WIDE : n * WIDE, :] = stream
    project_queries(inp_ref[WIDE : 3 * WIDE, :], wq_ref, sq_ref)
    project_keys(inp_ref[: 4 * WIDE, :], wkv_ref, 0, skv_ref)

    def q_of(g):
        if g in (0, 5):
            return sq_ref, (g // 5) * WIDE + 16
        return oq_ref, (g - 1) * WIDE + 16

    def kv_of(g):
        if g in (0, 1, 6, 7):
            return skv_ref, (g if g < 2 else g - 4) * WIDE
        return okv_ref, (g - 2) * WIDE

    ends = (place_ref[2], place_ref[3])
    attention(
        [0, 2], 5, q_of, kv_of, lambda g: (att_ref, g * MID), place_ref[0] - 8, place_ref[1] - 8, ends
    )
    for n, g in enumerate((0, 1, 4, 5)):
        rows = slice(n * MID, (n + 1) * MID)
        if g in (0, 5):
            before = side_ref[(g // 5) * WIDE + 16 : (g // 5) * WIDE + 16 + MID, :]
        else:
            before = stream_ref[(g - 1) * WIDE + 16 : (g - 1) * WIDE + 16 + MID, :]
        stream = before + dot(att_ref[g * MID : (g + 1) * MID, :], o_ref[...])
        if n in (1, 2):
            mid_ref[(n - 1) * GRP : n * GRP, :] = stream[16 : 16 + GRP, :]
        inp_ref[rows, :] = normed(stream, gain_ref[1:2, :])

    project(inp_ref[MID : 3 * MID, :], inp_ref[: 4 * MID, :], next_ref, q_ref, kv_ref)

    def later_q_of(g):
        if g in (0, 3):
            return q_ref, (g // 3) * MID + 16
        return mq_ref, (g - 1) * MID + 16

    def later_kv_of(g):
        if g in (2, 3):
            return mkv_ref, (g - 2) * MID
        return kv_ref, (g if g < 2 else g - 2) * MID

    attention(
        [0, 1],
        4,
        later_q_of,
        later_kv_of,
        lambda g: (att_ref, g * GRP),
        place_ref[0] - 4,
        place_ref[1] - 4,
        ends,
    )
    copy.wait()
    for g in range(4):
        rows = slice(g * GRP, (g + 1) * GRP)
        before = omid_ref[(g - 1) * GRP : g * GRP, :] if g in (1, 2) else mid_ref[
            (g // 3) * GRP : (g // 3 + 1) * GRP, :
        ]
        inp_ref[rows, :] = (before + dot(att_ref[rows, :], last_ref[...])).astype(bf16)
    to = iota((GRP, GRP), 0)
    wanted = (to // 4 % 4) * 32 + (to // 16) * 4 + to % 4
    reorder = onehot(iota((GRP, GRP), 1) == wanted)
    outs = []
    for n in range(4):
        rows = slice(n * GRP, (n + 1) * GRP)
        tokens = jnp.concatenate(
            [inp_ref[g * GRP + n * 32 : g * GRP + (n + 1) * 32, :] for g in range(4)], axis=0
        )
        att_ref[rows, :] = dot(reorder, tokens).astype(bf16)
        span = pl.ds(n * GRP, GRP)
        outs.append(
            pltpu.make_async_copy(att_ref.at[span, :], out_hbm.at[span, :], out_sem.at[n])
        )
        outs[-1].start()
    for out in outs:
        out.wait()


def rest(place, left, right, own, gain, embed, w, out_weight):
    hbm = pl.BlockSpec(memory_space=pltpu.HBM)
    vmem = pl.BlockSpec(memory_space=pltpu.VMEM)
    smem = pl.BlockSpec(memory_space=pltpu.SMEM)
    *own, wkv, o, later = own
    return pl.pallas_call(
        rest_kernel,
        out_shape=jax.ShapeDtypeStruct((4 * GRP, MODEL), bf16),
        in_specs=[smem] + [vmem] * 14 + [hbm],
        out_specs=hbm,
        scratch_shapes=[
            pltpu.VMEM((MODEL, MODEL), bf16),
            pltpu.VMEM((2 * WIDE, MODEL), f32),
            pltpu.VMEM((2 * WIDE, MODEL), bf16),
            pltpu.VMEM((4 * WIDE, 2 * MODEL), bf16),
            pltpu.VMEM((2 * MID, MODEL), bf16),
            pltpu.VMEM((4 * MID, 2 * MODEL), bf16),
            pltpu.VMEM((2 * GRP, MODEL), f32),
            pltpu.VMEM((6 * MID, MODEL), bf16),
            pltpu.VMEM((4 * WIDE, MODEL), bf16),
            pltpu.SemaphoreType.DMA,
            pltpu.SemaphoreType.DMA((4,)),
        ],
        compiler_params=pltpu.CompilerParams(vmem_limit_bytes=LARGE_BYTES),
        name="rest",
    )(
        place, right, left, *own, in_vmem(wkv), in_vmem(o), in_vmem(later), gain, in_vmem(embed),
        in_vmem(w), in_hbm(out_weight),
    )


def shifted(cells, axis, by):
    count = lax.axis_size(axis)
    return lax.ppermute(cells, axis, [(i, (i + by) % count) for i in range(count)])


def around(x, first, last):
    top = shifted(last, "row", 1)
    bottom = shifted(first, "row", -1)
    two = 2 * HALO
    right_edge = jnp.concatenate([top[two:], x[2 * GRP :], bottom[two:]], axis=0)
    left_edge = jnp.concatenate([top[:two], x[: 2 * GRP], bottom[:two]], axis=0)
    right = shifted(left_edge, "col", -1)
    left = shifted(right_edge, "col", 1)
    return top, bottom, left, right


def per_device(
    scans, dest, offsets, profile_index, profiles, embed_weight, attn_gain, qkv_weight, out_weight
):
    place = jnp.stack(
        [
            lax.axis_index("row") * TOK_H,
            lax.axis_index("col") * TOK_W,
            jnp.asarray(lax.axis_size("row") * TOK_H, i32),
            jnp.asarray(lax.axis_size("col") * TOK_W, i32),
        ]
    ).astype(i32)
    embed = embed_weight.reshape(CH, 8, 8, MODEL).transpose(1, 0, 2, 3).reshape(PATCH, MODEL)
    payload = pack(dest, offsets, profile_index, profiles, scans)
    payload = lax.all_to_all(payload, ("row", "col"), split_axis=0, concat_axis=0, tiled=True)
    payload, place = lax.optimization_barrier((payload, place))
    x, first, last, embed, w = merge(payload, profiles, embed, qkv_weight)
    top, bottom, left, right = around(x, first, last)
    own = own_part(place, x, top, bottom, embed, attn_gain, w, qkv_weight, out_weight)
    tokens = rest(place, left, right, own, attn_gain, embed, w, out_weight)
    return tokens.reshape(TOK_H, TOK_W, MODEL)


def solution(mesh):
    placed = (
        P(("row", "col"), None, None, None),
        P(("row", "col"), None),
        P(("row", "col")),
        P(("row", "col")),
        P(),
        P(),
        P(),
        P(),
        P(),
    )
    return jax.shard_map(
        per_device, mesh=mesh, in_specs=placed, out_specs=P("row", "col", None), check_vma=False
    )
```

```python
import functools

import jax
import jax.numpy as jnp
from jax import lax
from jax.experimental import pallas as pl
from jax.experimental.pallas import tpu as pltpu
from jax.sharding import PartitionSpec as P

HEADS = 16
RADIUS = 4
TOK_H = 32
TOK_W = 16
BR = 4
CH = 8
MODEL = 1024
PATCH = 512
GRP = 128
MID = 160
WIDE = 192
HALO = 32
EDGE = 4 * HALO
META = 128
CHUNKS = 4
VMEM_BYTES = 16 * 1024 * 1024
LARGE_BYTES = 22 * 1024 * 1024

f32 = jnp.float32
bf16 = jnp.bfloat16
i32 = jnp.int32


def dot(a, b):
    return lax.dot_general(a, b, (((1,), (0,)), ((), ())), preferred_element_type=f32)


def dot_nt(a, b):
    return lax.dot_general(a, b, (((1,), (1,)), ((), ())), preferred_element_type=f32)


def iota(shape, dim):
    return lax.broadcasted_iota(i32, shape, dim)


def onehot(cond):
    return jnp.where(cond, 1.0, 0.0).astype(bf16)


def halves(x):
    high = x.astype(bf16)
    return high, (x - high.astype(f32)).astype(bf16)


def pack_kernel(
    dest_hbm, offs_hbm, pidx_hbm, prof_hbm, scans_hbm, out_hbm,
    dest_ref, offs_ref, pidx_ref, prof_ref, scans_ref, w_ref, packed_ref, sem, out_sem,
):
    count = dest_ref.shape[1]
    chunk = scans_ref.shape[0] // CHUNKS
    small = [
        pltpu.make_async_copy(a, b, sem.at[n])
        for n, (a, b) in enumerate(
            [(dest_hbm, dest_ref), (offs_hbm, offs_ref), (pidx_hbm, pidx_ref), (prof_hbm, prof_ref)]
        )
    ]
    large = [
        pltpu.make_async_copy(
            scans_hbm.at[pl.ds(n * chunk, chunk)], scans_ref.at[pl.ds(n * chunk, chunk)], sem.at[4 + n]
        )
        for n in range(CHUNKS)
    ]
    for copy in small + large:
        copy.start()
    for copy in small:
        copy.wait()
    eye = iota((count, count), 0) == iota((count, count), 1)
    dest_row = dest_ref[...].astype(f32)
    dest_col = jnp.sum(jnp.where(eye, dest_row, 0.0), axis=1, keepdims=True)
    before = iota((count, count), 0) < iota((count, count), 1)
    same = (dest_col == dest_row) & before
    rank = jnp.sum(jnp.where(same, 1.0, 0.0), axis=0, keepdims=True)
    slot = dest_row * (2.0 * BR) + rank * float(BR)
    offs_col = jnp.sum(jnp.where(eye, offs_ref[...].astype(f32), 0.0), axis=1, keepdims=True)
    pidx_col = jnp.sum(jnp.where(eye, pidx_ref[...].astype(f32), 0.0), axis=1, keepdims=True)
    chosen = onehot(pidx_col == iota((count, prof_ref.shape[0]), 1).astype(f32))
    lane = iota((count, META), 1)
    meta = jnp.where(lane == 0, offs_col, jnp.where(lane == 1, pidx_col, 1.0)).astype(bf16)
    weights = []
    for k in range(BR):
        high, low = halves(prof_ref[:, k, :])
        weights.append(dot(chosen, high) + dot(chosen, low))
        w_ref[k * count : (k + 1) * count, CH * 128 :] = meta
    some = count // CHUNKS
    for n in range(CHUNKS):
        large[n].wait()
        for k in range(BR):
            for c in range(CH):
                block = scans_ref[pl.ds(n * chunk + k * CH + c, some, stride=BR * CH), :]
                at = k * count + n * some
                w_ref[at : at + some, c * 128 : (c + 1) * 128] = (
                    block * weights[k][n * some : (n + 1) * some, :]
                ).astype(bf16)
    slots = jnp.concatenate([slot + float(k) for k in range(BR)], axis=1)
    step = packed_ref.shape[0] // CHUNKS
    outs = []
    for n in range(CHUNKS):
        here = (iota((step, BR * count), 0) + n * step).astype(f32)
        rows = pl.ds(n * step, step)
        packed_ref[rows, :] = dot(onehot(here == slots), w_ref[...]).astype(bf16)
        outs.append(
            pltpu.make_async_copy(packed_ref.at[rows, :], out_hbm.at[rows, :], out_sem.at[n])
        )
        outs[-1].start()
    for copy in outs:
        copy.wait()


def pack(dest, offsets, profile_index, profiles, scans):
    count = scans.shape[0]
    rows = count * 2 * BR
    return pl.pallas_call(
        pack_kernel,
        out_shape=jax.ShapeDtypeStruct((rows, CH * 128 + META), bf16),
        in_specs=[pl.BlockSpec(memory_space=pltpu.HBM)] * 5,
        out_specs=pl.BlockSpec(memory_space=pltpu.HBM),
        scratch_shapes=[
            pltpu.VMEM((1, count), i32),
            pltpu.VMEM((1, count), i32),
            pltpu.VMEM((1, count), i32),
            pltpu.VMEM(profiles.shape, f32),
            pltpu.VMEM((count * BR * CH, 128), f32),
            pltpu.VMEM((BR * count, CH * 128 + META), bf16),
            pltpu.VMEM((rows, CH * 128 + META), bf16),
            pltpu.SemaphoreType.DMA((4 + CHUNKS,)),
            pltpu.SemaphoreType.DMA((CHUNKS,)),
        ],
        compiler_params=pltpu.CompilerParams(vmem_limit_bytes=VMEM_BYTES),
        name="pack",
    )(
        in_hbm(dest.reshape(1, count)),
        in_hbm(offsets.reshape(1, count)),
        in_hbm(profile_index.reshape(1, count)),
        in_hbm(profiles),
        in_hbm(scans.reshape(count * BR * CH, 128)),
    )


def in_hbm(x):
    return pltpu.with_memory_space_constraint(x, pltpu.HBM)


def in_vmem(x):
    return pltpu.with_memory_space_constraint(x, pltpu.VMEM)


def merge_kernel(
    pay_ref, prof_ref, embed_hbm, w_hbm, x_ref, top_ref, bot_ref, embed_ref, wq_ref,
    mg_ref, y_ref, xg_ref, sem,
):
    rows = pay_ref.shape[0]
    copies = [
        pltpu.make_async_copy(embed_hbm, embed_ref, sem.at[0]),
        pltpu.make_async_copy(w_hbm.at[0, :, pl.ds(0, MODEL)], wq_ref, sem.at[1]),
    ]
    for copy in copies:
        copy.start()
    pick = onehot(iota((8, META), 0) == iota((8, META), 1))
    fields = dot_nt(pick, pay_ref[:, CH * 128 :])
    offs = fields[0:1, :]
    pidx = fields[1:2, :]
    valid = fields[2:3, :]
    strip = (iota((1, rows), 1) % BR).astype(f32)
    land = jnp.where(valid > 0.5, offs + strip, 4096.0)
    kind = pidx + 16.0 * strip
    r = iota((TOK_H * 8, rows), 0)
    pixel = (r % TOK_H) * 8 + r // TOK_H
    placing = onehot(pixel.astype(f32) == land)
    kinds = onehot(iota((16 * BR, rows), 0).astype(f32) == kind)
    counts = dot_nt(placing, kinds).astype(bf16)
    table = jnp.concatenate([prof_ref[:, k, :] for k in range(BR)], axis=0)
    high, low = halves(table)
    scale = 1.0 / (1.0 + dot(counts, high) + dot(counts, low))
    for c in range(CH):
        part = dot(placing, pay_ref[:, c * 128 : (c + 1) * 128])
        mg_ref[:, c * 128 : (c + 1) * 128] = (part * scale).astype(bf16)
    width = CH * 128
    step = 256
    for n in range(0, width, step):
        source = iota((width, step), 0)
        to = iota((width, step), 1) + n
        wanted = (to // 8 % CH) * 128 + (to // 64) * 8 + to % 8
        y_ref[:, n : n + step] = dot(mg_ref[...], onehot(source == wanted))
    low_half = iota((TOK_H, 128), 1) < 64
    order = iota((GRP, GRP), 1)
    want = iota((GRP, GRP), 0)
    reorder = onehot(order == (want % 4) * TOK_H + want // 4)
    for g in range(4):
        for jj in range(4):
            j = 4 * g + jj
            tile = (j // 2) * 128
            for pp in range(4):
                a = y_ref[2 * pp * TOK_H : (2 * pp + 1) * TOK_H, tile : tile + 128]
                b = y_ref[(2 * pp + 1) * TOK_H : (2 * pp + 2) * TOK_H, tile : tile + 128]
                if j % 2 == 0:
                    piece = jnp.where(low_half, a, pltpu.roll(b, 64, 1))
                else:
                    piece = jnp.where(low_half, pltpu.roll(a, 64, 1), b)
                xg_ref[jj * TOK_H : (jj + 1) * TOK_H, pp * 128 : (pp + 1) * 128] = piece.astype(
                    bf16
                )
        tokens = dot(reorder, xg_ref[...]).astype(bf16)
        x_ref[g * GRP : (g + 1) * GRP, :] = tokens
        top_ref[g * HALO : (g + 1) * HALO, :] = tokens[:HALO, :]
        bot_ref[g * HALO : (g + 1) * HALO, :] = tokens[GRP - HALO :, :]
    for copy in copies:
        copy.wait()


def merge(payload, profiles, embed, qkv_weight):
    vmem = pl.BlockSpec(memory_space=pltpu.VMEM)
    hbm = pl.BlockSpec(memory_space=pltpu.HBM)
    return pl.pallas_call(
        merge_kernel,
        out_shape=[
            jax.ShapeDtypeStruct((4 * GRP, PATCH), bf16),
            jax.ShapeDtypeStruct((EDGE, PATCH), bf16),
            jax.ShapeDtypeStruct((EDGE, PATCH), bf16),
            pltpu.VMEM((PATCH, MODEL), bf16),
            pltpu.VMEM((MODEL, MODEL), bf16),
        ],
        in_specs=[vmem, vmem, hbm, hbm],
        scratch_shapes=[
            pltpu.VMEM((TOK_H * 8, CH * 128), bf16),
            pltpu.VMEM((TOK_H * 8, CH * 128), f32),
            pltpu.VMEM((GRP, PATCH), bf16),
            pltpu.SemaphoreType.DMA((2,)),
        ],
        compiler_params=pltpu.CompilerParams(vmem_limit_bytes=VMEM_BYTES),
        name="merge",
    )(payload, profiles, in_hbm(embed), in_hbm(qkv_weight))


def normed(stream, gain):
    centre = jnp.mean(stream, -1, keepdims=True)
    moved = stream - centre
    spread = jnp.mean(jnp.square(moved), -1, keepdims=True)
    return (moved * lax.rsqrt(spread + 1e-05) * gain).astype(bf16)


def own_kernel(
    place_ref, x_ref, top_ref, bot_ref, embed_ref, gain_ref, wq_ref, w_hbm, o_hbm,
    stream_ref, q_ref, kv_ref, mid_ref, later_q_ref, later_kv_ref, wkv_ref, o_ref, next_ref,
    inp_ref, att_ref, sem,
):
    copies = [
        pltpu.make_async_copy(w_hbm.at[0, :, pl.ds(MODEL, 2 * MODEL)], wkv_ref, sem.at[0]),
        pltpu.make_async_copy(o_hbm.at[0], o_ref, sem.at[1]),
        pltpu.make_async_copy(w_hbm.at[1], next_ref, sem.at[2]),
    ]
    for copy in copies:
        copy.start()
    for g in range(4):
        edge = slice(g * HALO, (g + 1) * HALO)
        tokens = jnp.concatenate(
            [top_ref[edge, :], x_ref[g * GRP : (g + 1) * GRP, :], bot_ref[edge, :]], axis=0
        )
        stream = dot(tokens, embed_ref[...])
        rows = slice(g * WIDE, (g + 1) * WIDE)
        stream_ref[rows, :] = stream
        inp_ref[rows, :] = normed(stream, gain_ref[0:1, :])
    queries = [inp_ref[g * WIDE + 16 : g * WIDE + 16 + MID, :] for g in range(4)]
    project_queries(jnp.concatenate(queries, axis=0), wq_ref, q_ref)
    copies[0].wait()
    project_keys(inp_ref[...], wkv_ref, 0, kv_ref)
    attention(
        [1],
        5,
        lambda g: (q_ref, (g - 1) * MID),
        lambda g: (kv_ref, (g - 2) * WIDE),
        lambda g: (att_ref, (g - 2) * MID),
        place_ref[0] - 8,
        place_ref[1] - 8,
        (place_ref[2], place_ref[3]),
    )
    for copy in copies[1:]:
        copy.wait()
    for n in range(2):
        rows = slice(n * MID, (n + 1) * MID)
        before = stream_ref[(n + 1) * WIDE + 16 : (n + 1) * WIDE + 16 + MID, :]
        stream = before + dot(att_ref[rows, :], o_ref[...])
        mid_ref[n * GRP : (n + 1) * GRP, :] = stream[16 : 16 + GRP, :]
        inp_ref[rows, :] = normed(stream, gain_ref[1:2, :])
    queries = [inp_ref[n * MID + 16 : n * MID + 16 + GRP, :] for n in range(2)]
    queries = jnp.concatenate(queries, axis=0)
    project(queries, inp_ref[: 2 * MID, :], next_ref, later_q_ref, later_kv_ref)


def project_queries(inputs, w_ref, q_ref):
    step = 256
    for m in range(0, MODEL, step):
        part = dot(inputs, w_ref[:, m : m + step]).astype(bf16)
        q_ref[: part.shape[0], m : m + step] = part * jnp.asarray(0.125, bf16)


def project_keys(inputs, w_ref, start, kv_ref):
    step = 256
    for m in range(0, 2 * MODEL, step):
        part = dot(inputs, w_ref[:, start + m : start + m + step]).astype(bf16)
        kv_ref[: part.shape[0], m : m + step] = part


def project(query_inputs, inputs, w_ref, q_ref, kv_ref):
    project_queries(query_inputs, w_ref, q_ref)
    project_keys(inputs, w_ref, MODEL, kv_ref)


def own_part(place, x, top, bottom, embed, gain, w, qkv_weight, out_weight):
    hbm = pl.BlockSpec(memory_space=pltpu.HBM)
    vmem = pl.BlockSpec(memory_space=pltpu.VMEM)
    smem = pl.BlockSpec(memory_space=pltpu.SMEM)
    return pl.pallas_call(
        own_kernel,
        out_shape=[
            jax.ShapeDtypeStruct((4 * WIDE, MODEL), f32),
            jax.ShapeDtypeStruct((4 * MID, MODEL), bf16),
            jax.ShapeDtypeStruct((4 * WIDE, 2 * MODEL), bf16),
            jax.ShapeDtypeStruct((2 * GRP, MODEL), f32),
            jax.ShapeDtypeStruct((2 * GRP, MODEL), bf16),
            jax.ShapeDtypeStruct((2 * MID, 2 * MODEL), bf16),
            pltpu.VMEM((MODEL, 2 * MODEL), bf16),
            pltpu.VMEM((MODEL, MODEL), bf16),
            pltpu.VMEM((MODEL, 3 * MODEL), bf16),
        ],
        in_specs=[smem] + [vmem] * 6 + [hbm] * 2,
        scratch_shapes=[
            pltpu.VMEM((4 * WIDE, MODEL), bf16),
            pltpu.VMEM((2 * MID, MODEL), bf16),
            pltpu.SemaphoreType.DMA((3,)),
        ],
        compiler_params=pltpu.CompilerParams(vmem_limit_bytes=VMEM_BYTES),
        cost_estimate=pl.CostEstimate(
            flops=2 * 4 * WIDE * MODEL * 3 * MODEL, bytes_accessed=12 << 20, transcendentals=0
        ),
        name="own",
    )(
        place, x, top, bottom, in_vmem(embed), gain, in_vmem(w),
        in_hbm(qkv_weight), in_hbm(out_weight),
    )


def attention(broad, tall, q_of, kv_of, a_of, row, col, ends):
    query = iota((64, 256), 0)
    key = iota((64, 256), 1)
    row_gap = (key % 64) // 4 - 4 - (query % 32) // 4
    col_gap = (key // 64 - 1) * 4 + key % 4 - (query // 32) * 4 - query % 4
    near = (jnp.abs(row_gap) <= RADIUS) & (jnp.abs(col_gap) <= RADIUS)
    near_bias = jnp.where(near, 0.0, -1e30)
    lane_key = iota((1, 256), 1)
    key_row = (lane_key % 64) // 4 + row
    key_col = (lane_key // 64) * 4 + lane_key % 4 + col
    low_half = iota((64, 128), 1) < 64
    zero = jnp.zeros((64, 128), bf16)
    ones = jnp.ones((256, 128), bf16)

    for bi in range(tall):
        at_row = key_row + bi * 8
        row_inside = (at_row >= 0) & (at_row < ends[0])
        for bj in broad:
            at_col = key_col + bj * 8
            inside = row_inside & (at_col >= 0) & (at_col < ends[1])
            bias = near_bias + jnp.where(inside, 0.0, -1e30)
            bias = jnp.concatenate([bias, bias], axis=0)
            q_from = [q_of(2 * bj + g) for g in range(2)]
            k_from = [kv_of(2 * bj + g) for g in range(4)]
            a_to = [a_of(2 * bj + g) for g in range(2)]
            at = bi * 32
            for h in range(HEADS // 2):
                lanes = slice(h * 128, (h + 1) * 128)
                q = jnp.concatenate([r[b + at : b + at + 32, lanes] for r, b in q_from], axis=0)
                q = jnp.concatenate(
                    [jnp.where(low_half, q, zero), jnp.where(low_half, zero, q)], axis=0
                )
                k = jnp.concatenate([r[b + at : b + at + 64, lanes] for r, b in k_from], axis=0)
                v_lanes = slice(MODEL + h * 128, MODEL + (h + 1) * 128)
                v = jnp.concatenate([r[b + at : b + at + 64, v_lanes] for r, b in k_from], axis=0)
                logits = dot_nt(q, k) + bias
                top = jnp.max(logits, axis=-1, keepdims=True)
                share = jnp.exp(logits - top).astype(bf16)
                both = dot(share, jnp.concatenate([v, ones], axis=1))
                mixed = jnp.where(low_half, both[:64, :128], both[64:, :128])
                total = jnp.where(low_half, both[:64, 128:], both[64:, 128:])
                picked = (mixed / total).astype(bf16)
                for g, (r, b) in enumerate(a_to):
                    r[b + at : b + at + 32, lanes] = picked[g * 32 : (g + 1) * 32, :]


def rest_kernel(
    place_ref, right_ref, left_ref, stream_ref, oq_ref, okv_ref, omid_ref, mq_ref, mkv_ref, wkv_ref,
    o_ref, next_ref, gain_ref, embed_ref, wq_ref, o_hbm, out_hbm,
    last_ref, side_ref, sq_ref, skv_ref, q_ref, kv_ref, mid_ref, att_ref, inp_ref, sem, out_sem,
):
    copy = pltpu.make_async_copy(o_hbm.at[1], last_ref, sem)
    copy.start()

    for n in range(4):
        ref, g = (left_ref, right_ref)[n // 2], n % 2
        below = 2 * HALO + 2 * GRP
        tokens = jnp.concatenate(
            [
                ref[g * HALO : (g + 1) * HALO, :],
                ref[2 * HALO + g * GRP : 2 * HALO + (g + 1) * GRP, :],
                ref[below + g * HALO : below + (g + 1) * HALO, :],
            ],
            axis=0,
        )
        stream = dot(tokens, embed_ref[...])
        inp_ref[n * WIDE : (n + 1) * WIDE, :] = normed(stream, gain_ref[0:1, :])
        if n in (1, 2):
            side_ref[(n - 1) * WIDE : n * WIDE, :] = stream
    queries = [inp_ref[g * WIDE + 16 : g * WIDE + 16 + MID, :] for g in (1, 2)]
    project_queries(jnp.concatenate(queries, axis=0), wq_ref, sq_ref)
    project_keys(inp_ref[: 4 * WIDE, :], wkv_ref, 0, skv_ref)

    def q_of(g):
        if g in (0, 5):
            return sq_ref, (g // 5) * MID
        return oq_ref, (g - 1) * MID

    def kv_of(g):
        if g in (0, 1, 6, 7):
            return skv_ref, (g if g < 2 else g - 4) * WIDE
        return okv_ref, (g - 2) * WIDE

    ends = (place_ref[2], place_ref[3])
    attention(
        [0, 2], 5, q_of, kv_of, lambda g: (att_ref, g * MID), place_ref[0] - 8, place_ref[1] - 8, ends
    )
    for n, g in enumerate((0, 1, 4, 5)):
        rows = slice(n * MID, (n + 1) * MID)
        if g in (0, 5):
            before = side_ref[(g // 5) * WIDE + 16 : (g // 5) * WIDE + 16 + MID, :]
        else:
            before = stream_ref[(g - 1) * WIDE + 16 : (g - 1) * WIDE + 16 + MID, :]
        stream = before + dot(att_ref[g * MID : (g + 1) * MID, :], o_ref[...])
        if n in (1, 2):
            mid_ref[(n - 1) * GRP : n * GRP, :] = stream[16 : 16 + GRP, :]
        inp_ref[rows, :] = normed(stream, gain_ref[1:2, :])

    queries = [inp_ref[n * MID + 16 : n * MID + 16 + GRP, :] for n in (1, 2)]
    queries = jnp.concatenate(queries, axis=0)
    project(queries, inp_ref[: 4 * MID, :], next_ref, q_ref, kv_ref)

    def later_q_of(g):
        if g in (0, 3):
            return q_ref, (g // 3) * GRP
        return mq_ref, (g - 1) * GRP

    def later_kv_of(g):
        if g in (2, 3):
            return mkv_ref, (g - 2) * MID
        return kv_ref, (g if g < 2 else g - 2) * MID

    attention(
        [0, 1],
        4,
        later_q_of,
        later_kv_of,
        lambda g: (att_ref, g * GRP),
        place_ref[0] - 4,
        place_ref[1] - 4,
        ends,
    )
    copy.wait()
    for g in range(4):
        rows = slice(g * GRP, (g + 1) * GRP)
        before = omid_ref[(g - 1) * GRP : g * GRP, :] if g in (1, 2) else mid_ref[
            (g // 3) * GRP : (g // 3 + 1) * GRP, :
        ]
        inp_ref[rows, :] = (before + dot(att_ref[rows, :], last_ref[...])).astype(bf16)
    to = iota((GRP, GRP), 0)
    wanted = (to // 4 % 4) * 32 + (to // 16) * 4 + to % 4
    reorder = onehot(iota((GRP, GRP), 1) == wanted)
    outs = []
    for n in range(4):
        rows = slice(n * GRP, (n + 1) * GRP)
        tokens = jnp.concatenate(
            [inp_ref[g * GRP + n * 32 : g * GRP + (n + 1) * 32, :] for g in range(4)], axis=0
        )
        att_ref[rows, :] = dot(reorder, tokens).astype(bf16)
        span = pl.ds(n * GRP, GRP)
        outs.append(
            pltpu.make_async_copy(att_ref.at[span, :], out_hbm.at[span, :], out_sem.at[n])
        )
        outs[-1].start()
    for out in outs:
        out.wait()


def rest(place, left, right, own, gain, embed, w, out_weight):
    hbm = pl.BlockSpec(memory_space=pltpu.HBM)
    vmem = pl.BlockSpec(memory_space=pltpu.VMEM)
    smem = pl.BlockSpec(memory_space=pltpu.SMEM)
    *own, wkv, o, later = own
    return pl.pallas_call(
        rest_kernel,
        out_shape=jax.ShapeDtypeStruct((4 * GRP, MODEL), bf16),
        in_specs=[smem] + [vmem] * 14 + [hbm],
        out_specs=hbm,
        scratch_shapes=[
            pltpu.VMEM((MODEL, MODEL), bf16),
            pltpu.VMEM((2 * WIDE, MODEL), f32),
            pltpu.VMEM((2 * MID, MODEL), bf16),
            pltpu.VMEM((4 * WIDE, 2 * MODEL), bf16),
            pltpu.VMEM((2 * MID, MODEL), bf16),
            pltpu.VMEM((4 * MID, 2 * MODEL), bf16),
            pltpu.VMEM((2 * GRP, MODEL), f32),
            pltpu.VMEM((6 * MID, MODEL), bf16),
            pltpu.VMEM((4 * WIDE, MODEL), bf16),
            pltpu.SemaphoreType.DMA,
            pltpu.SemaphoreType.DMA((4,)),
        ],
        compiler_params=pltpu.CompilerParams(vmem_limit_bytes=LARGE_BYTES),
        name="rest",
    )(
        place, right, left, *own, in_vmem(wkv), in_vmem(o), in_vmem(later), gain, in_vmem(embed),
        in_vmem(w), in_hbm(out_weight),
    )


def shifted(cells, axis, by):
    count = lax.axis_size(axis)
    return lax.ppermute(cells, axis, [(i, (i + by) % count) for i in range(count)])


def around(x, first, last):
    top = shifted(last, "row", 1)
    bottom = shifted(first, "row", -1)
    two = 2 * HALO
    right_edge = jnp.concatenate([top[two:], x[2 * GRP :], bottom[two:]], axis=0)
    left_edge = jnp.concatenate([top[:two], x[: 2 * GRP], bottom[:two]], axis=0)
    right = shifted(left_edge, "col", -1)
    left = shifted(right_edge, "col", 1)
    return top, bottom, left, right


def per_device(
    scans, dest, offsets, profile_index, profiles, embed_weight, attn_gain, qkv_weight, out_weight
):
    place = jnp.stack(
        [
            lax.axis_index("row") * TOK_H,
            lax.axis_index("col") * TOK_W,
            jnp.asarray(lax.axis_size("row") * TOK_H, i32),
            jnp.asarray(lax.axis_size("col") * TOK_W, i32),
        ]
    ).astype(i32)
    embed = embed_weight.reshape(CH, 8, 8, MODEL).transpose(1, 0, 2, 3).reshape(PATCH, MODEL)
    payload = pack(dest, offsets, profile_index, profiles, scans)
    payload = lax.all_to_all(payload, ("row", "col"), split_axis=0, concat_axis=0, tiled=True)
    payload, place = lax.optimization_barrier((payload, place))
    x, first, last, embed, w = merge(payload, profiles, embed, qkv_weight)
    top, bottom, left, right = around(x, first, last)
    own = own_part(place, x, top, bottom, embed, attn_gain, w, qkv_weight, out_weight)
    tokens = rest(place, left, right, own, attn_gain, embed, w, out_weight)
    return tokens.reshape(TOK_H, TOK_W, MODEL)


def solution(mesh):
    placed = (
        P(("row", "col"), None, None, None),
        P(("row", "col"), None),
        P(("row", "col")),
        P(("row", "col")),
        P(),
        P(),
        P(),
        P(),
        P(),
    )
    return jax.shard_map(
        per_device, mesh=mesh, in_specs=placed, out_specs=P("row", "col", None), check_vma=False
    )
```
